32 devices in a mesh: group: 4 (over y, core), mp: 8 (over z, x).
Axes of the slice: x: 2, y: 2, z: 4, core: 2. Of those that a mesh axis runs over, the one named last changes fastest.
Arguments:
- tokens: bfloat16 [5120, 2048], P(('group', 'mp')), may hold values from -6 to 6
- lengths: int32 [4, 8], P('group'), may hold values from 1 to 512, 1280 in all within a row
- query_gain: float32 [2048], replicated, may hold values from 0.5 to 8
- key_gain: float32 [2048], replicated, may hold values from 0.5 to 8
- attn_post_gain: float32 [2048], replicated, may hold values from 0.5 to 1.5
- mlp_post_gain: float32 [2048], replicated, may hold values from 0.5 to 1.5
- query_weight: float32 [2048, 2048], P(('mp', 'group')), may hold values from -4 to 4
- key_weight: float32 [2048, 2048], P(('mp', 'group')), may hold values from -4 to 4
- value_weight: float32 [2048, 2048], P(('mp', 'group')), may hold values from -0.125 to 0.125
- output_weight: float32 [2048, 2048], P(('mp', 'group')), may hold values from -0.125 to 0.125
- gate_weight: float32 [2048, 8192], P(('mp', 'group')), may hold values from -0.125 to 0.125
- up_weight: float32 [2048, 8192], P(('mp', 'group')), may hold values from -0.125 to 0.125
- down_weight: float32 [8192, 2048], P(('mp', 'group')), may hold values from -0.0625 to 0.0625
Outputs:
- layer_out: bfloat16 [5120, 2048], P(('group', 'mp'))
The draws below stay inside these ranges and needn't reach their ends.
Inputs may be any that keep to these rules, and one draw needn't show every extreme that they name: In each group the 8 prompt lengths sum to 1280; the longest is exactly 512.
All inputs are finite; a program needn't handle non-finite values.
Results may differ from the reference program's by a relative error of at most 0.034.
Values may be sent and summed in bfloat16 or wider, within the bound.
No kernel may reach another device: no remote copies, remote signals or barrier semaphores. Data moves between devices by JAX's collectives and lax.ppermute only.
A program may use at most 128 MiB of HBM per device.

```python
import math
import jax
import jax.numpy as jnp
import numpy as np
from jax import lax

D = 2048
HEADS = 16
HEAD_DIM = 128
FF = 8192
TOK_GRP = 1280
MOST = 512
REQS = 8
GROUPS = 4
TOKENS = 5120
N_GROUP = 4


def gain_draw(key, salt):
    base = jnp.exp(jax.random.uniform(jax.random.fold_in(key, salt), (D,), jnp.float32, math.log(0.5), math.log(2.0)))
    return base


def column_ramped(key, salt):
    base = jax.random.truncated_normal(jax.random.fold_in(key, salt), -6.0, 6.0, (D, D), jnp.float32) / math.sqrt(D)
    ramp = jnp.exp(jnp.arange(D, dtype=jnp.float32) * (math.log(3.0) / (D - 1)))
    return base * ramp[None, :]


def draw_query_gain(key, part):
    return gain_draw(key, 11)


def draw_key_gain(key, part):
    return gain_draw(key, 31)


def draw_query_weight(key, part):
    return column_ramped(key, 51)


def draw_key_weight(key, part):
    return column_ramped(key, 71)


def steps_of(own_key, shape, shards, smallest, high):
    def one(dim, parts):
        steps = jax.random.uniform(jax.random.fold_in(jax.random.fold_in(own_key, 6), dim), (parts,), jnp.float32, smallest / len(shards), high / len(shards))
        return jnp.repeat(jnp.exp(steps), shape[dim] // parts).reshape((-1,) + (1,) * (len(shape) - dim - 1))

    factor_of = one(*shards[0])
    for cut in shards[1:]:
        factor_of = factor_of * one(*cut)
    return factor_of


def length_profile(number_of, total, bound, lean):
    weights = [(1 << 20) // math.isqrt(grade ** lean) + 1 for grade in range(2, number_of + 1)]
    rest, given = total - bound - (number_of - 1), [1] * (number_of - 1)
    while rest > 0:
        free = [i for i in range(number_of - 1) if given[i] < bound]
        mass, budget = sum([weights[i] for i in free]), rest
        for i in free:
            addition = min(bound - given[i], max(1, budget * weights[i] // mass), rest)
            given[i] = given[i] + addition
            rest = rest - addition
    return np.array([bound] + given)


def ragged_sizes(rng, amount, total, limit, slope):
    if amount == 2:
        one = jax.random.randint(rng, (), max(1, total - limit), min(limit, total - 1) + 1)
        return jnp.stack([one, total - one])
    tallies = jnp.asarray(length_profile(amount, total, limit, slope), jnp.int32)
    twos = (amount - 1) // 2
    source_of, sink = tallies[1:1 + 2 * twos:2], tallies[2:2 + 2 * twos:2]
    room = jnp.minimum(source_of - 1, limit - sink)
    shifted = jax.random.randint(jax.random.fold_in(rng, 1), (twos,), 0, 1 << 20) % (room + 1)
    tallies = tallies.at[1:1 + 2 * twos:2].set(source_of - shifted).at[2:2 + 2 * twos:2].set(sink + shifted)
    return tallies[jax.random.permutation(jax.random.fold_in(rng, 2), amount)]


def gaussian(stream_key, shape, width, bound, cuts=(), kind=jnp.bfloat16):
    values = jax.random.normal(stream_key, shape, jnp.float32) * width
    if len(cuts) > 0:
        values = steps_of(stream_key, shape, cuts, -0.22, 0.18) * values
    return jnp.clip(values, min=-bound, max=bound).astype(kind)


def setup_inputs(seed: int = 0) -> dict:
    arg_keys = jax.random.split(jax.random.key(seed), 14)
    return {
        "tokens": gaussian(arg_keys[0], (TOKENS, D), 1.0, 6.0, ((0, 32),)),
        "lengths": jax.vmap(lambda own: ragged_sizes(own, REQS, TOK_GRP, MOST, 2))(jax.random.split(arg_keys[1], GROUPS)).reshape((GROUPS, REQS)).astype(jnp.int32),
        "query_gain": draw_query_gain(jax.random.fold_in(arg_keys[13], 71), 0),
        "key_gain": draw_key_gain(jax.random.fold_in(arg_keys[13], 71), 0),
        "attn_post_gain": jnp.clip(1.0 + 0.1 * jax.random.normal(arg_keys[4], (D,), jnp.float32), 0.5, 1.5),
        "mlp_post_gain": jnp.clip(1.0 + 0.1 * jax.random.normal(arg_keys[5], (D,), jnp.float32), 0.5, 1.5),
        "query_weight": draw_query_weight(jax.random.fold_in(arg_keys[13], 71), 0),
        "key_weight": draw_key_weight(jax.random.fold_in(arg_keys[13], 71), 0),
        "value_weight": gaussian(arg_keys[8], (D, D), D ** -0.5, 0.125, ((0, 32),), jnp.float32),
        "output_weight": gaussian(arg_keys[9], (D, D), D ** -0.5, 0.125, ((0, 32),), jnp.float32),
        "gate_weight": gaussian(arg_keys[10], (D, FF), D ** -0.5, 0.125, ((0, 32),), jnp.float32),
        "up_weight": gaussian(arg_keys[11], (D, FF), D ** -0.5, 0.125, ((0, 32),), jnp.float32),
        "down_weight": gaussian(arg_keys[12], (FF, D), FF ** -0.5, 0.0625, ((0, 32),), jnp.float32),
    }


NORM_EPSILON = 1e-06
ROPE_BASE = 500000.0

def token_layout(prompt_lens, row_count):
    seg_ends = jnp.cumsum(prompt_lens).astype(jnp.int32)
    starts = (seg_ends - prompt_lens).astype(jnp.int32)
    indices = jnp.arange(row_count, dtype=jnp.int32)
    segment = lax.optimization_barrier(jnp.sum((indices[:, None] >= seg_ends[None, :]).astype(jnp.int32), axis=1)).astype(jnp.int32)
    member = segment[:, None] == jnp.arange(prompt_lens.shape[0], dtype=jnp.int32)[None, :]
    opening = lax.optimization_barrier(jnp.sum(jnp.where(member, starts[None, :], 0), axis=1)).astype(jnp.int32)
    return (segment, (indices - opening).astype(jnp.int32))

def rotary(head_values, position, head_size):
    half_size = head_size // 2
    frequency = jnp.exp(jnp.arange(half_size, dtype=jnp.float32) * (-2.0 * math.log(ROPE_BASE) / head_size))
    angles = position.astype(jnp.float32)[:, None] * frequency[None, :]
    cosines = jnp.cos(angles)
    sines = jnp.sin(angles)
    front_half = head_values[..., :half_size]
    back_half = head_values[..., half_size:]
    return jnp.concatenate([front_half * cosines - back_half * sines, back_half * cosines + front_half * sines], axis=-1)

def head_attention(queries, keys_rot, values_h, segment, head_size):
    scores = lax.dot_general(queries, keys_rot, (((1,), (1,)), ((), ())), preferred_element_type=jnp.float32)
    scores = scores * (1.0 / math.sqrt(head_size))
    indices = jnp.arange(queries.shape[0], dtype=jnp.int32)
    allowed = (segment[:, None] == segment[None, :]) & (indices[None, :] <= indices[:, None])
    scores = jnp.where(allowed, scores, -1e+30)
    row_max = lax.optimization_barrier(jnp.max(scores, axis=1, keepdims=True))
    weights = jnp.exp(scores - row_max)
    weights = weights / lax.optimization_barrier(jnp.sum(weights, axis=1, keepdims=True))
    probabilities = weights.astype(jnp.bfloat16)
    return jnp.dot(probabilities, values_h, preferred_element_type=jnp.float32).astype(jnp.bfloat16)

def rms_scale(values_in, gain):
    return values_in * lax.rsqrt(lax.optimization_barrier(jnp.mean(values_in * values_in, axis=-1, keepdims=True)) + NORM_EPSILON) * gain

def reference(tokens, lengths, query_gain, key_gain, attn_post_gain, mlp_post_gain, query_weight, key_weight, value_weight, output_weight, gate_weight, up_weight, down_weight):
    query_server = query_weight.astype(jnp.bfloat16)
    key_server = key_weight.astype(jnp.bfloat16)
    value_server = value_weight.astype(jnp.bfloat16)
    output_server = output_weight.astype(jnp.bfloat16)
    gate_server = gate_weight.astype(jnp.bfloat16)
    up_server = up_weight.astype(jnp.bfloat16)
    down_server = down_weight.astype(jnp.bfloat16)

    def heads_first(flat):
        return flat.reshape(TOK_GRP, HEADS, HEAD_DIM).transpose(1, 0, 2)

    def one_group(inputs):
        group_x, prompt_lens = inputs
        segment, position = token_layout(prompt_lens, TOK_GRP)
        q_raw = jnp.dot(group_x, query_server, preferred_element_type=jnp.float32)
        k_raw = jnp.dot(group_x, key_server, preferred_element_type=jnp.float32)
        v_raw = jnp.dot(group_x, value_server, preferred_element_type=jnp.float32)
        q_normed = rms_scale(q_raw, query_gain)
        k_normed = rms_scale(k_raw, key_gain)
        queries = rotary(heads_first(q_normed), position, HEAD_DIM).astype(jnp.bfloat16)
        keys_rot = rotary(heads_first(k_normed), position, HEAD_DIM).astype(jnp.bfloat16)
        values_h = heads_first(v_raw.astype(jnp.bfloat16))

        def per_head(triple):
            return head_attention(triple[0], triple[1], triple[2], segment, HEAD_DIM)
        attended = lax.map(per_head, (queries, keys_rot, values_h))
        attended = attended.transpose(1, 0, 2).reshape(TOK_GRP, D)
        attn_out = jnp.dot(attended, output_server, preferred_element_type=jnp.float32)
        hidden = (group_x.astype(jnp.float32) + rms_scale(attn_out, attn_post_gain)).astype(jnp.bfloat16)
        gate_proj = jnp.dot(hidden, gate_server, preferred_element_type=jnp.float32)
        up_proj = jnp.dot(hidden, up_server, preferred_element_type=jnp.float32)
        activated = (jax.nn.silu(gate_proj) * up_proj).astype(jnp.bfloat16)
        mlp_out = jnp.dot(activated, down_server, preferred_element_type=jnp.float32)
        return (hidden.astype(jnp.float32) + rms_scale(mlp_out, mlp_post_gain)).astype(jnp.bfloat16)
    result = lax.map(one_group, (tokens.reshape(N_GROUP, TOK_GRP, D), lengths))
    return result.reshape(TOKENS, D)
```

```python
import math

import jax
import jax.numpy as jnp
from jax import lax
from jax.sharding import PartitionSpec as P

HEAD_DIM = 128


NORM_EPSILON = 1e-06
ROPE_BASE = 500000.0


def partner_2(block, axis, apart):
    count = lax.axis_size(axis)
    route = []
    for low in range(count):
        high = low | 1 << apart
        if high != low and high < count:
            route += [(low, high), (high, low)]
    return lax.ppermute(block, axis, route)


def token_layout(prompt_lens, row_count):
    seg_ends = jnp.cumsum(prompt_lens)
    starts = seg_ends - prompt_lens
    indices = jnp.arange(row_count, dtype=jnp.int32)
    segment = jnp.sum((indices[:, None] >= seg_ends[None, :]).astype(jnp.int32), axis=1)
    member = segment[:, None] == jnp.arange(prompt_lens.shape[0], dtype=jnp.int32)[None, :]
    opening = jnp.sum(jnp.where(member, starts[None, :], 0), axis=1)
    return (segment, indices - opening)


def rotary(head_values, position, head_size):
    half_size = head_size // 2
    frequency = jnp.exp(
        jnp.arange(half_size, dtype=jnp.float32) * (-2.0 * math.log(ROPE_BASE) / head_size)
    )
    angles = position.astype(jnp.float32)[:, None] * frequency[None, :]
    cosines = jnp.cos(angles)
    sines = jnp.sin(angles)
    front_half = head_values[..., :half_size]
    back_half = head_values[..., half_size:]
    return jnp.concatenate(
        [front_half * cosines - back_half * sines, back_half * cosines + front_half * sines],
        axis=-1,
    )


def head_attention(queries, query_rows, keys_rot, values_h, segment, head_size):
    scores = lax.dot_general(
        queries, keys_rot, (((1,), (1,)), ((), ())), preferred_element_type=jnp.float32
    )
    scores = scores * (1.0 / math.sqrt(head_size))
    key_rows = jnp.arange(keys_rot.shape[0], dtype=jnp.int32)
    query_segment = jnp.take(segment, query_rows)
    allowed = (query_segment[:, None] == segment[None, :]) & (
        key_rows[None, :] <= query_rows[:, None]
    )
    scores = jnp.where(allowed, scores, -1e30)
    row_max = jnp.max(scores, axis=1, keepdims=True)
    weights = jnp.exp(scores - row_max)
    weights = weights / jnp.sum(weights, axis=1, keepdims=True)
    probabilities = weights.astype(jnp.bfloat16)
    return jnp.dot(probabilities, values_h, preferred_element_type=jnp.float32).astype(jnp.bfloat16)


def rms_scale(values_in, gain):
    return (
        values_in
        * lax.rsqrt(jnp.mean(values_in * values_in, axis=-1, keepdims=True) + NORM_EPSILON)
        * gain
    )


def per_device_general(
    tokens,
    lengths,
    query_gain,
    key_gain,
    attn_post_gain,
    mlp_post_gain,
    query_weight,
    key_weight,
    value_weight,
    output_weight,
    gate_weight,
    up_weight,
    down_weight,
):
    features = tokens.shape[1]
    shards = lax.axis_size("mp")
    my_index = lax.axis_index("mp")
    col_width = features // shards
    tok_rows = tokens.shape[0]
    group_rows = tok_rows * shards
    halves = col_width < HEAD_DIM
    stack_attn = jnp.stack([query_weight, key_weight, value_weight]).astype(jnp.bfloat16)
    stack_mlp = jnp.stack([gate_weight, up_weight]).astype(jnp.bfloat16)
    down_piece = down_weight.astype(jnp.bfloat16)[None]
    output_piece = output_weight.astype(jnp.bfloat16)[None]
    attn_rows, mlp_rows, down_rows, output_rows = (
        lax.all_gather(stack_attn, "group", axis=1, tiled=True),
        lax.all_gather(stack_mlp, "group", axis=1, tiled=True),
        lax.all_gather(down_piece, "group", axis=1, tiled=True),
        lax.all_gather(output_piece, "group", axis=1, tiled=True),
    )
    attn_block, mlp_block = (
        lax.all_to_all(attn_rows, "mp", split_axis=2, concat_axis=1, tiled=True),
        lax.all_to_all(mlp_rows, "mp", split_axis=2, concat_axis=1, tiled=True),
    )
    down_block = down_rows[0]
    output_block = output_rows[0]
    parity = my_index % 2
    if halves:
        partner = partner_2(attn_block, "mp", 0)
        attn_block = jnp.where(
            parity == 0,
            jnp.concatenate([attn_block, partner], axis=2),
            jnp.concatenate([partner, attn_block], axis=2),
        )
    head_cols = attn_block.shape[2]
    col_start = my_index * col_width // HEAD_DIM * HEAD_DIM
    share_part = col_width / head_cols
    projected = jnp.einsum(
        "td,kdc->ktc",
        lax.all_gather(tokens, "mp", axis=0, tiled=True),
        attn_block,
        preferred_element_type=jnp.float32,
    )
    query_sq = jnp.sum(projected[0] * projected[0], axis=1) * share_part
    key_sq = jnp.sum(projected[1] * projected[1], axis=1) * share_part
    query_total, key_total = lax.psum((query_sq, key_sq), "mp")
    query_part = lax.dynamic_slice_in_dim(query_gain, col_start, head_cols)
    key_part = lax.dynamic_slice_in_dim(key_gain, col_start, head_cols)
    q_normed = projected[0] * lax.rsqrt(query_total / features + NORM_EPSILON)[:, None] * query_part
    k_normed = projected[1] * lax.rsqrt(key_total / features + NORM_EPSILON)[:, None] * key_part
    segment, position = token_layout(lengths[0], group_rows)
    local_heads = head_cols // HEAD_DIM

    def heads_first(flat):
        return flat.reshape(group_rows, local_heads, HEAD_DIM).transpose(1, 0, 2)

    queries = rotary(heads_first(q_normed), position, HEAD_DIM).astype(jnp.bfloat16)
    keys_rot = rotary(heads_first(k_normed), position, HEAD_DIM).astype(jnp.bfloat16)
    values_h = heads_first(projected[2].astype(jnp.bfloat16))
    all_rows = jnp.arange(group_rows, dtype=jnp.int32)

    def per_head(triple):
        return head_attention(triple[0], all_rows, triple[1], triple[2], segment, HEAD_DIM)

    attended = lax.map(per_head, (queries, keys_rot, values_h))
    attended = attended.transpose(1, 0, 2).reshape(group_rows, head_cols)
    if halves:
        attended = lax.dynamic_slice_in_dim(attended, parity * col_width, col_width, 1)
    rows_part = attended
    attn_out = lax.psum_scatter(
        jnp.dot(rows_part, output_block, preferred_element_type=jnp.float32).astype(jnp.bfloat16),
        "mp",
        scatter_dimension=0,
        tiled=True,
    ).astype(jnp.float32)
    hidden = (tokens.astype(jnp.float32) + rms_scale(attn_out, attn_post_gain)).astype(jnp.bfloat16)
    hidden_width = mlp_block.shape[2]
    mlp_weights = jnp.concatenate([mlp_block[0], mlp_block[1]], axis=1)
    both_proj = jnp.dot(
        lax.all_gather(hidden, "mp", axis=0, tiled=True),
        mlp_weights,
        preferred_element_type=jnp.float32,
    )
    activated = (jax.nn.silu(both_proj[:, :hidden_width]) * both_proj[:, hidden_width:]).astype(
        jnp.bfloat16
    )
    rows_part = activated
    mlp_out = lax.psum_scatter(
        jnp.dot(rows_part, down_block, preferred_element_type=jnp.float32).astype(jnp.bfloat16),
        "mp",
        scatter_dimension=0,
        tiled=True,
    ).astype(jnp.float32)
    return (hidden.astype(jnp.float32) + rms_scale(mlp_out, mlp_post_gain)).astype(jnp.bfloat16)


def over_mp(block, lines, step):
    count = 2 * lines
    return lax.ppermute(block, "mp", [(i, (i + 2 * step) % count) for i in range(count)])


def swap_x(block):
    return lax.ppermute(block, "mp", [(i, i ^ 1) for i in range(lax.axis_size("mp"))])


def swap_y(block):
    return lax.ppermute(block, "group", [(i, i ^ 2) for i in range(lax.axis_size("group"))])


def swap_core(block):
    return lax.ppermute(block, "group", [(i, i ^ 1) for i in range(lax.axis_size("group"))])


def swap_home(block):
    shards = lax.axis_size("mp")
    route = []
    for group in range(lax.axis_size("group")):
        for index in range(shards):
            if index % 2 != group % 2:
                route.append((group * shards + index, (group ^ 1) * shards + (index ^ 1)))
    return lax.ppermute(block, ("group", "mp"), route)


def pair(core, mine, other, axis):
    return jnp.concatenate(
        [jnp.where(core == 0, mine, other), jnp.where(core == 0, other, mine)], axis=axis
    )


def put(buffer, block, index, axis):
    return lax.dynamic_update_slice_in_dim(buffer, block, index, axis)


def spread_xy(piece, x, y, axis, length):
    at_x = swap_x(piece)
    at_y = swap_y(piece)
    split = piece.shape[-2] // 2
    low = (Ellipsis, slice(0, split), slice(None))
    high = (Ellipsis, slice(split, None), slice(None))
    far_low = swap_y(at_x[low])
    far_high = swap_x(at_y[high])
    far = jnp.concatenate([far_low, far_high], axis=-2)
    shape = list(piece.shape)
    shape[axis] = 4 * length
    whole = jnp.zeros(shape, piece.dtype)
    whole = put(whole, piece, (2 * x + y) * length, axis)
    whole = put(whole, at_x, (2 * (1 - x) + y) * length, axis)
    whole = put(whole, at_y, (2 * x + 1 - y) * length, axis)
    return put(whole, far, (2 * (1 - x) + 1 - y) * length, axis)


def columns_to_owners(cut, lines, z, core):
    held = None
    for step in range(lines):
        piece = cut((z + step) % lines)
        if step:
            piece = over_mp(piece, lines, step)
        if held is None:
            held = jnp.zeros((lines,) + piece.shape, piece.dtype)
        held = put(held, piece[None], (z - step) % lines, 0)
    mine = lax.dynamic_index_in_dim(held, core, 1, keepdims=True)
    other = swap_core(lax.dynamic_index_in_dim(held, 1 - core, 1, keepdims=True))
    rows = pair(core, mine, other, 1)
    return rows.reshape(-1, rows.shape[-1])


def per_device_lines(
    tokens,
    lengths,
    query_gain,
    key_gain,
    attn_post_gain,
    mlp_post_gain,
    query_weight,
    key_weight,
    value_weight,
    output_weight,
    gate_weight,
    up_weight,
    down_weight,
):
    bf16, f32 = jnp.bfloat16, jnp.float32
    features = tokens.shape[1]
    shards = lax.axis_size("mp")
    lines = shards // 2
    index = lax.axis_index("mp")
    z, x = index // 2, index % 2
    group = lax.axis_index("group")
    y, core = group // 2, group % 2
    tok_rows = tokens.shape[0]
    chip_rows = 2 * tok_rows
    group_rows = shards * tok_rows
    home = x == core

    block = jnp.where(home, tokens, swap_home(tokens))
    prompt_lens = jnp.where(home, lengths, swap_core(lengths))[0]

    def server_order(rows):
        parts = rows.reshape(rows.shape[0], lines, 4, features // shards // 2)
        return parts.transpose(0, 2, 1, 3).reshape(rows.shape)

    def chips(own):
        blocks = []
        for step in range(lines):
            if step:
                own = over_mp(own, lines, 1)
            blocks.append(pair(core, own, swap_core(own), 0))
        return blocks

    token_blocks = chips(server_order(block))

    z_cols = features // lines
    head_cols = z_cols // 2

    def cut_attn(dest):
        parts = [
            lax.dynamic_slice_in_dim(w, dest * z_cols, z_cols, 1).astype(bf16)
            for w in (query_weight, key_weight, value_weight)
        ]
        return jnp.stack(
            [
                jnp.concatenate([p[:, h * head_cols : (h + 1) * head_cols] for p in parts], axis=1)
                for h in range(2)
            ]
        )

    attn_piece = columns_to_owners(cut_attn, lines, z, core)
    attn_weights = spread_xy(attn_piece, x, y, 0, attn_piece.shape[0])

    out_own = output_weight.astype(bf16)
    out_rows = [out_own]
    for step in range(lines - 1):
        out_rows.append(over_mp(out_rows[-1], lines, 1))
    out_piece = jnp.stack(out_rows)[:, None]
    out_weights = spread_xy(out_piece, x, y, 1, 1).reshape(-1, features)

    z_units = gate_weight.shape[1] // lines
    run = z_units // 8

    def cut_mlp(dest):
        parts = [
            lax.dynamic_slice_in_dim(w, dest * z_units, z_units, 1).astype(bf16)
            for w in (gate_weight, up_weight)
        ]
        return jnp.stack(
            [
                jnp.concatenate(
                    [p[:, (2 * q + h) * run : (2 * q + h + 1) * run] for p in parts for q in range(4)],
                    axis=1,
                )
                for h in range(2)
            ]
        )

    mlp_piece = columns_to_owners(cut_mlp, lines, z, core)
    mlp_weights = spread_xy(mlp_piece, x, y, 0, mlp_piece.shape[0])
    down_piece = down_weight.astype(bf16)
    down_block = spread_xy(down_piece, x, y, 0, down_piece.shape[0])
    units = down_block.shape[0]

    projected = jnp.zeros((group_rows, 3 * head_cols), f32)
    for step, rows in enumerate(token_blocks):
        part = jnp.dot(rows, attn_weights, preferred_element_type=f32)
        projected = put(projected, part, (z - step) % lines * chip_rows, 0)
    q_raw = projected[:, :head_cols]
    k_raw = projected[:, head_cols : 2 * head_cols]
    squares = jnp.stack([jnp.sum(q_raw * q_raw, axis=1), jnp.sum(k_raw * k_raw, axis=1)])
    squares = squares + swap_core(squares)
    total = squares
    for step in range(1, lines):
        total = total + over_mp(squares, lines, step)
    col_start = z * z_cols + core * head_cols
    query_part = lax.dynamic_slice_in_dim(query_gain, col_start, head_cols)
    key_part = lax.dynamic_slice_in_dim(key_gain, col_start, head_cols)
    q_normed = q_raw * lax.rsqrt(total[0] / features + NORM_EPSILON)[:, None] * query_part
    k_normed = k_raw * lax.rsqrt(total[1] / features + NORM_EPSILON)[:, None] * key_part
    segment, position = token_layout(prompt_lens, group_rows)
    local_heads = head_cols // HEAD_DIM

    def heads_first(flat):
        return flat.reshape(group_rows, local_heads, HEAD_DIM).transpose(1, 0, 2)

    queries = rotary(heads_first(q_normed), position, HEAD_DIM).astype(bf16)
    keys_rot = rotary(heads_first(k_normed), position, HEAD_DIM).astype(bf16)
    values_h = heads_first(projected[:, 2 * head_cols :].astype(bf16))
    all_rows = jnp.arange(group_rows, dtype=jnp.int32)

    def per_head(triple):
        return head_attention(triple[0], all_rows, triple[1], triple[2], segment, HEAD_DIM)

    attended = lax.map(per_head, (queries, keys_rot, values_h))

    out_run = out_own.shape[0]
    runs = head_cols // out_run // 2
    attended = attended.transpose(1, 0, 2).reshape(group_rows, runs, 2, out_run)
    attended = attended.transpose(2, 0, 1, 3).reshape(2, group_rows, runs * out_run)
    arrived = []
    for step in range(lines):
        dest = (z + step) % lines
        part = lax.dynamic_slice_in_dim(attended, dest * chip_rows, chip_rows, 1)
        arrived.append(over_mp(part, lines, step) if step else part)
    arrived = jnp.stack(arrived, axis=1)
    keep = lax.dynamic_index_in_dim(arrived, core, 0, keepdims=False)
    got = swap_core(lax.dynamic_index_in_dim(arrived, 1 - core, 0, keepdims=False))
    both = pair(core, keep, got, 2)
    both = both.transpose(1, 0, 2).reshape(chip_rows, -1)
    partial = jnp.dot(both, out_weights, preferred_element_type=f32)

    def share(partial):
        mine = lax.dynamic_slice_in_dim(partial, core * tok_rows, tok_rows, 0)
        theirs = lax.dynamic_slice_in_dim(partial, (1 - core) * tok_rows, tok_rows, 0)
        return mine.astype(f32) + swap_core(theirs.astype(bf16)).astype(f32)

    attn_out = share(partial)
    hidden = (block.astype(f32) + rms_scale(attn_out, attn_post_gain)).astype(bf16)

    def feed_forward(rows):
        both_proj = jnp.dot(rows, mlp_weights, preferred_element_type=f32)
        activated = (jax.nn.silu(both_proj[:, :units]) * both_proj[:, units:]).astype(bf16)
        return share(jnp.dot(activated, down_block, preferred_element_type=f32))

    hidden_blocks = chips(server_order(hidden))
    total_out = None
    for step in range(1, lines + 1):
        part = feed_forward(hidden_blocks[step % lines])
        if total_out is not None:
            part = part + total_out.astype(f32)
        if step < lines:
            total_out = over_mp(part.astype(bf16), lines, 1)
    layer_out = (hidden.astype(f32) + rms_scale(part, mlp_post_gain)).astype(bf16)
    return jnp.where(home, layer_out, swap_home(layer_out))


def per_device(*arrays):
    heads = arrays[0].shape[1] // HEAD_DIM
    shards = lax.axis_size("mp")
    if lax.axis_size("group") == 4 and shards % 2 == 0 and heads % shards == 0:
        return per_device_lines(*arrays)
    return per_device_general(*arrays)


def solution(mesh):
    return jax.shard_map(
        per_device,
        mesh=mesh,
        in_specs=(
            P(("group", "mp"), None),
            P("group", None),
            P(),
            P(),
            P(),
            P(),
            P(("mp", "group"), None),
            P(("mp", "group"), None),
            P(("mp", "group"), None),
            P(("mp", "group"), None),
            P(("mp", "group"), None),
            P(("mp", "group"), None),
            P(("mp", "group"), None),
        ),
        out_specs=P(("group", "mp"), None),
        check_vma=False,
    )
```

```python
import math

import jax
import jax.numpy as jnp
from jax import lax
from jax.sharding import PartitionSpec as P

HEAD_DIM = 128


NORM_EPSILON = 1e-06
ROPE_BASE = 500000.0


def partner_2(block, axis, apart):
    count = lax.axis_size(axis)
    route = []
    for low in range(count):
        high = low | 1 << apart
        if high != low and high < count:
            route += [(low, high), (high, low)]
    return lax.ppermute(block, axis, route)


def token_layout(prompt_lens, row_count):
    seg_ends = jnp.cumsum(prompt_lens)
    starts = seg_ends - prompt_lens
    indices = jnp.arange(row_count, dtype=jnp.int32)
    segment = jnp.sum((indices[:, None] >= seg_ends[None, :]).astype(jnp.int32), axis=1)
    member = segment[:, None] == jnp.arange(prompt_lens.shape[0], dtype=jnp.int32)[None, :]
    opening = jnp.sum(jnp.where(member, starts[None, :], 0), axis=1)
    return (segment, indices - opening)


def rotary(head_values, position, head_size):
    half_size = head_size // 2
    frequency = jnp.exp(
        jnp.arange(half_size, dtype=jnp.float32) * (-2.0 * math.log(ROPE_BASE) / head_size)
    )
    angles = position.astype(jnp.float32)[:, None] * frequency[None, :]
    cosines = jnp.cos(angles)
    sines = jnp.sin(angles)
    front_half = head_values[..., :half_size]
    back_half = head_values[..., half_size:]
    return jnp.concatenate(
        [front_half * cosines - back_half * sines, back_half * cosines + front_half * sines],
        axis=-1,
    )


def head_attention(queries, keys_rot, values_h, segment, head_size):
    scores = lax.dot_general(
        queries, keys_rot, (((1,), (1,)), ((), ())), preferred_element_type=jnp.float32
    )
    scores = scores * (1.0 / math.sqrt(head_size))
    key_rows = jnp.arange(keys_rot.shape[0], dtype=jnp.int32)
    query_segment = segment
    allowed = (query_segment[:, None] == segment[None, :]) & (
        key_rows[None, :] <= key_rows[:, None]
    )
    scores = jnp.where(allowed, scores, -1e30)
    row_max = jnp.max(scores, axis=1, keepdims=True)
    weights = jnp.exp(scores - row_max)
    weights = weights / jnp.sum(weights, axis=1, keepdims=True)
    probabilities = weights.astype(jnp.bfloat16)
    return jnp.dot(probabilities, values_h, preferred_element_type=jnp.float32).astype(jnp.bfloat16)


def rms_scale(values_in, gain):
    return (
        values_in
        * lax.rsqrt(jnp.mean(values_in * values_in, axis=-1, keepdims=True) + NORM_EPSILON)
        * gain
    )


def per_device_general(
    tokens,
    lengths,
    query_gain,
    key_gain,
    attn_post_gain,
    mlp_post_gain,
    query_weight,
    key_weight,
    value_weight,
    output_weight,
    gate_weight,
    up_weight,
    down_weight,
):
    features = tokens.shape[1]
    shards = lax.axis_size("mp")
    my_index = lax.axis_index("mp")
    col_width = features // shards
    tok_rows = tokens.shape[0]
    group_rows = tok_rows * shards
    halves = col_width < HEAD_DIM
    stack_attn = jnp.stack([query_weight, key_weight, value_weight]).astype(jnp.bfloat16)
    stack_mlp = jnp.stack([gate_weight, up_weight]).astype(jnp.bfloat16)
    down_piece = down_weight.astype(jnp.bfloat16)[None]
    output_piece = output_weight.astype(jnp.bfloat16)[None]
    attn_rows, mlp_rows, down_rows, output_rows = (
        lax.all_gather(stack_attn, "group", axis=1, tiled=True),
        lax.all_gather(stack_mlp, "group", axis=1, tiled=True),
        lax.all_gather(down_piece, "group", axis=1, tiled=True),
        lax.all_gather(output_piece, "group", axis=1, tiled=True),
    )
    attn_block, mlp_block = (
        lax.all_to_all(attn_rows, "mp", split_axis=2, concat_axis=1, tiled=True),
        lax.all_to_all(mlp_rows, "mp", split_axis=2, concat_axis=1, tiled=True),
    )
    down_block = down_rows[0]
    output_block = output_rows[0]
    parity = my_index % 2
    if halves:
        partner = partner_2(attn_block, "mp", 0)
        attn_block = jnp.where(
            parity == 0,
            jnp.concatenate([attn_block, partner], axis=2),
            jnp.concatenate([partner, attn_block], axis=2),
        )
    head_cols = attn_block.shape[2]
    col_start = my_index * col_width // HEAD_DIM * HEAD_DIM
    share_part = col_width / head_cols
    projected = jnp.einsum(
        "td,kdc->ktc",
        lax.all_gather(tokens, "mp", axis=0, tiled=True),
        attn_block,
        preferred_element_type=jnp.float32,
    )
    query_sq = jnp.sum(projected[0] * projected[0], axis=1) * share_part
    key_sq = jnp.sum(projected[1] * projected[1], axis=1) * share_part
    query_total, key_total = lax.psum((query_sq, key_sq), "mp")
    query_part = lax.dynamic_slice_in_dim(query_gain, col_start, head_cols)
    key_part = lax.dynamic_slice_in_dim(key_gain, col_start, head_cols)
    q_normed = projected[0] * lax.rsqrt(query_total / features + NORM_EPSILON)[:, None] * query_part
    k_normed = projected[1] * lax.rsqrt(key_total / features + NORM_EPSILON)[:, None] * key_part
    segment, position = token_layout(lengths[0], group_rows)
    local_heads = head_cols // HEAD_DIM

    def heads_first(flat):
        return flat.reshape(group_rows, local_heads, HEAD_DIM).transpose(1, 0, 2)

    queries = rotary(heads_first(q_normed), position, HEAD_DIM).astype(jnp.bfloat16)
    keys_rot = rotary(heads_first(k_normed), position, HEAD_DIM).astype(jnp.bfloat16)
    values_h = heads_first(projected[2].astype(jnp.bfloat16))

    def per_head(triple):
        return head_attention(triple[0], triple[1], triple[2], segment, HEAD_DIM)

    attended = lax.map(per_head, (queries, keys_rot, values_h))
    attended = attended.transpose(1, 0, 2).reshape(group_rows, head_cols)
    if halves:
        attended = lax.dynamic_slice_in_dim(attended, parity * col_width, col_width, 1)
    rows_part = attended
    attn_out = lax.psum_scatter(
        jnp.dot(rows_part, output_block, preferred_element_type=jnp.float32).astype(jnp.bfloat16),
        "mp",
        scatter_dimension=0,
        tiled=True,
    ).astype(jnp.float32)
    hidden = (tokens.astype(jnp.float32) + rms_scale(attn_out, attn_post_gain)).astype(jnp.bfloat16)
    hidden_width = mlp_block.shape[2]
    mlp_weights = jnp.concatenate([mlp_block[0], mlp_block[1]], axis=1)
    both_proj = jnp.dot(
        lax.all_gather(hidden, "mp", axis=0, tiled=True),
        mlp_weights,
        preferred_element_type=jnp.float32,
    )
    activated = (jax.nn.silu(both_proj[:, :hidden_width]) * both_proj[:, hidden_width:]).astype(
        jnp.bfloat16
    )
    rows_part = activated
    mlp_out = lax.psum_scatter(
        jnp.dot(rows_part, down_block, preferred_element_type=jnp.float32).astype(jnp.bfloat16),
        "mp",
        scatter_dimension=0,
        tiled=True,
    ).astype(jnp.float32)
    return (hidden.astype(jnp.float32) + rms_scale(mlp_out, mlp_post_gain)).astype(jnp.bfloat16)


def over_mp(block, lines, step):
    count = 2 * lines
    return lax.ppermute(block, "mp", [(i, (i + 2 * step) % count) for i in range(count)])


def swap_x(block):
    return lax.ppermute(block, "mp", [(i, i ^ 1) for i in range(lax.axis_size("mp"))])


def swap_y(block):
    return lax.ppermute(block, "group", [(i, i ^ 2) for i in range(lax.axis_size("group"))])


def swap_core(block):
    return lax.ppermute(block, "group", [(i, i ^ 1) for i in range(lax.axis_size("group"))])


def swap_home(block, lines, step):
    shards = 2 * lines
    route = []
    for group in range(lax.axis_size("group")):
        for index in range(shards):
            apart = index % 2 ^ group % 2
            to = ((index + 2 * step) % shards) ^ apart
            if step or apart:
                route.append((group * shards + index, (group ^ apart) * shards + to))
    return lax.ppermute(block, ("group", "mp"), route)


def after(value, *earlier):
    return lax.optimization_barrier((value, *earlier))[0]


def put(buffer, block, *place):
    shape = (1,) * len(place) + block.shape
    rest = (0,) * (buffer.ndim - len(place))
    return lax.dynamic_update_slice(buffer, block.reshape(shape), tuple(place) + rest)


def pick(buffer, index):
    return lax.dynamic_index_in_dim(buffer, index, 0, keepdims=False)


def spread_xy(piece, x, y):
    at_x = swap_x(piece)
    at_y = swap_y(piece)
    split = piece.shape[0] // 2
    far_low = swap_y(at_x[:split])
    far_high = swap_x(at_y[split:])
    whole = jnp.zeros((4, 2, split) + piece.shape[1:], piece.dtype)
    halves = (2, split) + piece.shape[1:]
    whole = put(whole, piece.reshape(halves), 2 * x + y)
    whole = put(whole, at_x.reshape(halves), 2 * (1 - x) + y)
    whole = put(whole, at_y.reshape(halves), 2 * x + 1 - y)
    whole = put(whole, far_low, 2 * (1 - x) + 1 - y, 0)
    whole = put(whole, far_high, 2 * (1 - x) + 1 - y, 1)
    return whole.reshape((4,) + piece.shape)


def rows_to_owners(parts, lines, z, core):
    _, _, rows, width = parts.shape
    held = jnp.zeros(parts.shape, parts.dtype)
    held = put(held, pick(parts, z), z)
    for step in range(1, lines):
        arrived = over_mp(pick(parts, (z + step) % lines), lines, step)
        held = put(held, arrived, (z - step) % lines)
    by_core = held.transpose(1, 0, 2, 3)
    other = swap_core(pick(by_core, 1 - core))
    mine = pick(by_core, core)
    both = jnp.stack([jnp.where(core == 0, mine, other), jnp.where(core == 0, other, mine)], axis=1)
    return both.reshape(lines * 2 * rows, width)


def per_device_lines(
    tokens,
    lengths,
    query_gain,
    key_gain,
    attn_post_gain,
    mlp_post_gain,
    query_weight,
    key_weight,
    value_weight,
    output_weight,
    gate_weight,
    up_weight,
    down_weight,
):
    bf16, f32 = jnp.bfloat16, jnp.float32
    features = tokens.shape[1]
    shards = lax.axis_size("mp")
    lines = shards // 2
    index = lax.axis_index("mp")
    z, x = index // 2, index % 2
    group = lax.axis_index("group")
    y, core = group // 2, group % 2
    tok_rows = tokens.shape[0]
    chip_rows = 2 * tok_rows
    group_rows = shards * tok_rows
    home = x == core

    prompt_lens = jnp.where(home, lengths, swap_core(lengths))[0]

    def server_order(rows):
        parts = rows.reshape(rows.shape[0], lines, 4, features // shards // 2)
        return parts.transpose(0, 2, 1, 3).reshape(rows.shape)

    own_order = server_order(tokens)
    ring = [None, swap_home(own_order, lines, 1)]
    moved = swap_home(tokens, lines, 0)
    block = jnp.where(home, tokens, moved)
    ring[0] = server_order(block)
    for step in range(2, lines):
        ring.append(over_mp(ring[-1], lines, 1))
    rows = jnp.zeros((lines, 2) + tokens.shape, bf16)
    for step, own in enumerate(ring):
        rows = put(rows, own, (z - step) % lines, core)
        rows = put(rows, swap_core(own), (z - step) % lines, 1 - core)
    rows = rows.reshape(group_rows, features)

    z_cols = features // lines
    head_cols = z_cols // 2

    def by_owner(weights, runs):
        parts = [w.astype(bf16).reshape(w.shape[0], lines, runs, 2, -1) for w in weights]
        parts = jnp.stack(parts, axis=2).transpose(1, 4, 0, 2, 3, 5)
        return parts.reshape(lines, 2, weights[0].shape[0], -1)

    attn_parts = by_owner((query_weight, key_weight, value_weight), 1)
    attn_piece = rows_to_owners(attn_parts, lines, z, core)
    attn_weights = spread_xy(attn_piece, x, y).reshape(features, -1)

    out_own = after(output_weight.astype(bf16), ring[-2])
    out_rows = [out_own]
    for step in range(1, lines):
        out_rows.append(over_mp(out_own, lines, step))
    out_weights = spread_xy(jnp.stack(out_rows, axis=0), x, y)
    out_weights = out_weights.reshape(-1, features)

    gate_parts = after(by_owner((gate_weight,), 4), ring[-1])
    up_parts = after(by_owner((up_weight,), 4), ring[-1])
    gate_piece = rows_to_owners(gate_parts, lines, z, core)
    up_piece = rows_to_owners(up_parts, lines, z, core)
    gate_block = spread_xy(gate_piece, x, y).reshape(features, -1)
    up_block = spread_xy(up_piece, x, y).reshape(features, -1)
    down_block = spread_xy(down_weight.astype(bf16), x, y).reshape(-1, features)

    projected = jnp.dot(rows, attn_weights, preferred_element_type=f32)
    q_raw = projected[:, :head_cols]
    k_raw = projected[:, head_cols : 2 * head_cols]
    squares = jnp.stack([jnp.sum(q_raw * q_raw, axis=1), jnp.sum(k_raw * k_raw, axis=1)])
    squares = squares + swap_core(squares)
    total = squares
    for step in range(1, lines):
        total = total + over_mp(squares, lines, step)
    col_start = z * z_cols + core * head_cols
    query_part = lax.dynamic_slice_in_dim(query_gain, col_start, head_cols)
    key_part = lax.dynamic_slice_in_dim(key_gain, col_start, head_cols)
    q_normed = q_raw * lax.rsqrt(total[0] / features + NORM_EPSILON)[:, None] * query_part
    k_normed = k_raw * lax.rsqrt(total[1] / features + NORM_EPSILON)[:, None] * key_part
    segment, position = token_layout(prompt_lens, group_rows)
    local_heads = head_cols // HEAD_DIM

    def heads_first(flat):
        return flat.reshape(group_rows, local_heads, HEAD_DIM).transpose(1, 0, 2)

    queries = rotary(heads_first(q_normed), position, HEAD_DIM).astype(bf16)
    keys_rot = rotary(heads_first(k_normed), position, HEAD_DIM).astype(bf16)
    values_h = heads_first(projected[:, 2 * head_cols :].astype(bf16))

    attended = jnp.stack(
        [
            head_attention(queries[h], keys_rot[h], values_h[h], segment, HEAD_DIM)
            for h in range(local_heads)
        ]
    )

    out_run = out_own.shape[0]
    runs = head_cols // out_run // 2
    attended = attended.transpose(1, 0, 2).reshape(lines, chip_rows, runs, 2, out_run)
    attended = attended.transpose(0, 3, 1, 2, 4).reshape(lines, 2, chip_rows, runs * out_run)
    arrived = [pick(attended, z)]
    for step in range(1, lines):
        arrived.append(over_mp(pick(attended, (z + step) % lines), lines, step))
    arrived = jnp.stack(arrived, axis=1)
    keep = pick(arrived, core)
    got = swap_core(pick(arrived, 1 - core))
    both = jnp.stack([jnp.where(core == 0, keep, got), jnp.where(core == 0, got, keep)], axis=0)
    both = both.reshape(2, lines, chip_rows, runs, out_run).transpose(2, 0, 3, 1, 4)
    both = both.reshape(chip_rows, -1)
    partial = jnp.dot(both, out_weights, preferred_element_type=f32)

    partial = partial.reshape(2, tok_rows, features)
    attn_out = pick(partial, core) + swap_core(pick(partial, 1 - core).astype(bf16)).astype(f32)
    hidden = (block.astype(f32) + rms_scale(attn_out, attn_post_gain)).astype(bf16)

    def feed_forward(own):
        rows = jnp.concatenate([own, swap_core(own)], axis=0)
        gate = jnp.dot(rows, gate_block, preferred_element_type=f32)
        up = jnp.dot(rows, up_block, preferred_element_type=f32)
        activated = (jax.nn.silu(gate) * up).astype(bf16)
        out = jnp.dot(activated, down_block, preferred_element_type=f32)
        return out[:tok_rows] + swap_core(out[tok_rows:].astype(bf16)).astype(f32)

    ring = [server_order(hidden)]
    for step in range(1, lines):
        ring.append(over_mp(ring[-1], lines, 1))
    total_out = None
    for step in range(1, lines):
        part = feed_forward(ring[step])
        if total_out is not None:
            part = part + total_out.astype(f32)
        part = part.astype(bf16)
        total_out = over_mp(part, lines, 1) if step + 1 < lines else swap_home(part, lines, 1)
    own_out = feed_forward(ring[0]).astype(bf16)
    own_out = jnp.where(home, own_out, swap_home(own_out, lines, 0)).astype(f32)
    hidden = jnp.where(home, hidden, swap_home(hidden, lines, 0)).astype(f32)
    mlp_out = own_out + total_out.astype(f32)
    return (hidden + rms_scale(mlp_out, mlp_post_gain)).astype(bf16)


def per_device(*arrays):
    heads = arrays[0].shape[1] // HEAD_DIM
    shards = lax.axis_size("mp")
    if lax.axis_size("group") == 4 and shards % 2 == 0 and heads % shards == 0:
        return per_device_lines(*arrays)
    return per_device_general(*arrays)


def solution(mesh):
    return jax.shard_map(
        per_device,
        mesh=mesh,
        in_specs=(
            P(("group", "mp"), None),
            P("group", None),
            P(),
            P(),
            P(),
            P(),
            P(("mp", "group"), None),
            P(("mp", "group"), None),
            P(("mp", "group"), None),
            P(("mp", "group"), None),
            P(("mp", "group"), None),
            P(("mp", "group"), None),
            P(("mp", "group"), None),
        ),
        out_specs=P(("group", "mp"), None),
        check_vma=False,
    )
```

```python
import math

import jax
import jax.numpy as jnp
from jax import lax
from jax.sharding import PartitionSpec as P

HEAD_DIM = 128


NORM_EPSILON = 1e-06
ROPE_BASE = 500000.0


def partner_2(block, axis, apart):
    count = lax.axis_size(axis)
    route = []
    for low in range(count):
        high = low | 1 << apart
        if high != low and high < count:
            route += [(low, high), (high, low)]
    return lax.ppermute(block, axis, route)


def token_layout(prompt_lens, row_count):
    seg_ends = jnp.cumsum(prompt_lens)
    starts = seg_ends - prompt_lens
    indices = jnp.arange(row_count, dtype=jnp.int32)
    segment = jnp.sum((indices[:, None] >= seg_ends[None, :]).astype(jnp.int32), axis=1)
    member = segment[:, None] == jnp.arange(prompt_lens.shape[0], dtype=jnp.int32)[None, :]
    opening = jnp.sum(jnp.where(member, starts[None, :], 0), axis=1)
    return (segment, indices - opening)


def rotary(head_values, position, head_size):
    half_size = head_size // 2
    frequency = jnp.exp(
        jnp.arange(half_size, dtype=jnp.float32) * (-2.0 * math.log(ROPE_BASE) / head_size)
    )
    angles = position.astype(jnp.float32)[:, None] * frequency[None, :]
    cosines = jnp.cos(angles)
    sines = jnp.sin(angles)
    front_half = head_values[..., :half_size]
    back_half = head_values[..., half_size:]
    return jnp.concatenate(
        [front_half * cosines - back_half * sines, back_half * cosines + front_half * sines],
        axis=-1,
    )


def head_attention(queries, keys_rot, values_h, segment, head_size):
    scores = lax.dot_general(
        queries, keys_rot, (((1,), (1,)), ((), ())), preferred_element_type=jnp.float32
    )
    scores = scores * (1.0 / math.sqrt(head_size))
    key_rows = jnp.arange(keys_rot.shape[0], dtype=jnp.int32)
    query_segment = segment
    allowed = (query_segment[:, None] == segment[None, :]) & (
        key_rows[None, :] <= key_rows[:, None]
    )
    scores = jnp.where(allowed, scores, -1e30)
    row_max = jnp.max(scores, axis=1, keepdims=True)
    weights = jnp.exp(scores - row_max)
    weights = weights / jnp.sum(weights, axis=1, keepdims=True)
    probabilities = weights.astype(jnp.bfloat16)
    return jnp.dot(probabilities, values_h, preferred_element_type=jnp.float32).astype(jnp.bfloat16)


def rms_scale(values_in, gain):
    return (
        values_in
        * lax.rsqrt(jnp.mean(values_in * values_in, axis=-1, keepdims=True) + NORM_EPSILON)
        * gain
    )


def per_device_general(
    tokens,
    lengths,
    query_gain,
    key_gain,
    attn_post_gain,
    mlp_post_gain,
    query_weight,
    key_weight,
    value_weight,
    output_weight,
    gate_weight,
    up_weight,
    down_weight,
):
    features = tokens.shape[1]
    shards = lax.axis_size("mp")
    my_index = lax.axis_index("mp")
    col_width = features // shards
    tok_rows = tokens.shape[0]
    group_rows = tok_rows * shards
    halves = col_width < HEAD_DIM
    stack_attn = jnp.stack([query_weight, key_weight, value_weight]).astype(jnp.bfloat16)
    stack_mlp = jnp.stack([gate_weight, up_weight]).astype(jnp.bfloat16)
    down_piece = down_weight.astype(jnp.bfloat16)[None]
    output_piece = output_weight.astype(jnp.bfloat16)[None]
    attn_rows, mlp_rows, down_rows, output_rows = (
        lax.all_gather(stack_attn, "group", axis=1, tiled=True),
        lax.all_gather(stack_mlp, "group", axis=1, tiled=True),
        lax.all_gather(down_piece, "group", axis=1, tiled=True),
        lax.all_gather(output_piece, "group", axis=1, tiled=True),
    )
    attn_block, mlp_block = (
        lax.all_to_all(attn_rows, "mp", split_axis=2, concat_axis=1, tiled=True),
        lax.all_to_all(mlp_rows, "mp", split_axis=2, concat_axis=1, tiled=True),
    )
    down_block = down_rows[0]
    output_block = output_rows[0]
    parity = my_index % 2
    if halves:
        partner = partner_2(attn_block, "mp", 0)
        attn_block = jnp.where(
            parity == 0,
            jnp.concatenate([attn_block, partner], axis=2),
            jnp.concatenate([partner, attn_block], axis=2),
        )
    head_cols = attn_block.shape[2]
    col_start = my_index * col_width // HEAD_DIM * HEAD_DIM
    share_part = col_width / head_cols
    projected = jnp.einsum(
        "td,kdc->ktc",
        lax.all_gather(tokens, "mp", axis=0, tiled=True),
        attn_block,
        preferred_element_type=jnp.float32,
    )
    query_sq = jnp.sum(projected[0] * projected[0], axis=1) * share_part
    key_sq = jnp.sum(projected[1] * projected[1], axis=1) * share_part
    query_total, key_total = lax.psum((query_sq, key_sq), "mp")
    query_part = lax.dynamic_slice_in_dim(query_gain, col_start, head_cols)
    key_part = lax.dynamic_slice_in_dim(key_gain, col_start, head_cols)
    q_normed = projected[0] * lax.rsqrt(query_total / features + NORM_EPSILON)[:, None] * query_part
    k_normed = projected[1] * lax.rsqrt(key_total / features + NORM_EPSILON)[:, None] * key_part
    segment, position = token_layout(lengths[0], group_rows)
    local_heads = head_cols // HEAD_DIM

    def heads_first(flat):
        return flat.reshape(group_rows, local_heads, HEAD_DIM).transpose(1, 0, 2)

    queries = rotary(heads_first(q_normed), position, HEAD_DIM).astype(jnp.bfloat16)
    keys_rot = rotary(heads_first(k_normed), position, HEAD_DIM).astype(jnp.bfloat16)
    values_h = heads_first(projected[2].astype(jnp.bfloat16))

    def per_head(triple):
        return head_attention(triple[0], triple[1], triple[2], segment, HEAD_DIM)

    attended = lax.map(per_head, (queries, keys_rot, values_h))
    attended = attended.transpose(1, 0, 2).reshape(group_rows, head_cols)
    if halves:
        attended = lax.dynamic_slice_in_dim(attended, parity * col_width, col_width, 1)
    rows_part = attended
    attn_out = lax.psum_scatter(
        jnp.dot(rows_part, output_block, preferred_element_type=jnp.float32).astype(jnp.bfloat16),
        "mp",
        scatter_dimension=0,
        tiled=True,
    ).astype(jnp.float32)
    hidden = (tokens.astype(jnp.float32) + rms_scale(attn_out, attn_post_gain)).astype(jnp.bfloat16)
    hidden_width = mlp_block.shape[2]
    mlp_weights = jnp.concatenate([mlp_block[0], mlp_block[1]], axis=1)
    both_proj = jnp.dot(
        lax.all_gather(hidden, "mp", axis=0, tiled=True),
        mlp_weights,
        preferred_element_type=jnp.float32,
    )
    activated = (jax.nn.silu(both_proj[:, :hidden_width]) * both_proj[:, hidden_width:]).astype(
        jnp.bfloat16
    )
    rows_part = activated
    mlp_out = lax.psum_scatter(
        jnp.dot(rows_part, down_block, preferred_element_type=jnp.float32).astype(jnp.bfloat16),
        "mp",
        scatter_dimension=0,
        tiled=True,
    ).astype(jnp.float32)
    return (hidden.astype(jnp.float32) + rms_scale(mlp_out, mlp_post_gain)).astype(jnp.bfloat16)


def over_mp(block, lines, step):
    count = 2 * lines
    return lax.ppermute(block, "mp", [(i, (i + 2 * step) % count) for i in range(count)])


def swap_x(block):
    return lax.ppermute(block, "mp", [(i, i ^ 1) for i in range(lax.axis_size("mp"))])


def swap_y(block):
    return lax.ppermute(block, "group", [(i, i ^ 2) for i in range(lax.axis_size("group"))])


def swap_core(block):
    return lax.ppermute(block, "group", [(i, i ^ 1) for i in range(lax.axis_size("group"))])


def swap_home(block, lines, step):
    shards = 2 * lines
    route = []
    for group in range(lax.axis_size("group")):
        for index in range(shards):
            apart = index % 2 ^ group % 2
            to = ((index + 2 * step) % shards) ^ apart
            if step or apart:
                route.append((group * shards + index, (group ^ apart) * shards + to))
    return lax.ppermute(block, ("group", "mp"), route)


def together(*arrays):
    return lax.optimization_barrier(arrays)


def put(buffer, block, *place):
    shape = (1,) * len(place) + block.shape
    rest = (0,) * (buffer.ndim - len(place))
    return lax.dynamic_update_slice(buffer, block.reshape(shape), tuple(place) + rest)


def pick(buffer, index):
    return lax.dynamic_index_in_dim(buffer, index, 0, keepdims=False)


def first_hop(piece):
    return swap_x(piece), swap_y(piece)


def second_hop(at_x, at_y):
    split = at_x.shape[0] // 2
    return swap_y(at_x[:split]), swap_x(at_y[split:])


def four_pieces(piece, at_x, at_y, far_low, far_high, x, y):
    halves = (2, piece.shape[0] // 2) + piece.shape[1:]
    whole = jnp.zeros((4,) + halves, piece.dtype)
    whole = put(whole, piece.reshape(halves), 2 * x + y)
    whole = put(whole, at_x.reshape(halves), 2 * (1 - x) + y)
    whole = put(whole, at_y.reshape(halves), 2 * x + 1 - y)
    whole = put(whole, far_low, 2 * (1 - x) + 1 - y, 0)
    whole = put(whole, far_high, 2 * (1 - x) + 1 - y, 1)
    return whole.reshape((4,) + piece.shape)


def to_lines(parts, lines, z):
    return [over_mp(pick(parts, (z + step) % lines), lines, step) for step in range(1, lines)]


def both_cores(parts, arrived, lines, z, core):
    held = jnp.zeros(parts.shape, parts.dtype)
    held = put(held, pick(parts, z), z)
    for step, block in enumerate(arrived, 1):
        held = put(held, block, (z - step) % lines)
    held = held.transpose(1, 0, 2, 3)
    other = swap_core(pick(held, 1 - core))
    mine = pick(held, core)
    both = jnp.stack([jnp.where(core == 0, mine, other), jnp.where(core == 0, other, mine)], axis=1)
    return both.reshape((2 * lines,) + both.shape[2:])


def per_device_lines(
    tokens,
    lengths,
    query_gain,
    key_gain,
    attn_post_gain,
    mlp_post_gain,
    query_weight,
    key_weight,
    value_weight,
    output_weight,
    gate_weight,
    up_weight,
    down_weight,
):
    bf16, f32 = jnp.bfloat16, jnp.float32
    features = tokens.shape[1]
    shards = lax.axis_size("mp")
    lines = shards // 2
    index = lax.axis_index("mp")
    z, x = index // 2, index % 2
    group = lax.axis_index("group")
    y, core = group // 2, group % 2
    tok_rows = tokens.shape[0]
    chip_rows = 2 * tok_rows
    group_rows = shards * tok_rows
    home = x == core

    prompt_lens = jnp.where(home, lengths, swap_core(lengths))[0]
    z_cols = features // lines
    head_cols = z_cols // 2
    run = features // shards // 2

    def server_order(rows):
        parts = rows.reshape(rows.shape[:-1] + (lines, 4, run))
        return jnp.swapaxes(parts, -3, -2).reshape(rows.shape)

    def given_order(rows):
        parts = rows.reshape(rows.shape[:-1] + (4, lines, run))
        return jnp.swapaxes(parts, -3, -2).reshape(rows.shape)

    def by_owner(weights, runs):
        parts = [w.astype(bf16).reshape(w.shape[0], lines, runs, 2, -1) for w in weights]
        parts = jnp.stack(parts, axis=2).transpose(1, 4, 0, 2, 3, 5)
        return parts.reshape(lines, 2, weights[0].shape[0], -1)

    own_order = server_order(tokens)
    attn_parts = by_owner((query_weight, key_weight, value_weight), 1)
    attn_arrived = to_lines(attn_parts, lines, z)
    ring_1 = swap_home(own_order, lines, 1)
    moved = swap_home(own_order, lines, 0)
    own_order, ring_1, moved, *attn_arrived = together(own_order, ring_1, moved, *attn_arrived)
    block = jnp.where(home, own_order, moved)
    ring = [block, ring_1]
    down_own = down_weight.astype(bf16)
    down_near = first_hop(down_own)

    attn_piece = both_cores(attn_parts, attn_arrived, lines, z, core)
    attn_near = first_hop(attn_piece)
    if lines > 2:
        ring.append(over_mp(ring[-1], lines, 1))
    swapped = [swap_core(own) for own in ring[:2]]
    out_own = server_order(output_weight.astype(bf16))
    out_arrived = [over_mp(out_own, lines, step) for step in range(1, lines)]
    ring[-1], down_own, attn_piece, *rest = together(
        ring[-1], down_own, attn_piece, *down_near, *attn_near, *swapped
    )
    down_near, attn_near, swapped = rest[:2], rest[2:4], rest[4:]

    attn_far = second_hop(*attn_near)
    down_far = second_hop(*down_near)
    for step in range(3, lines):
        ring.append(over_mp(ring[-1], lines, 1))
    gate_up = by_owner((gate_weight, up_weight), 4)
    rows_half = gate_up.shape[2] // 2
    gate_up, attn_piece, ring[-1], *rest = together(
        gate_up, attn_piece, ring[-1], *attn_near, *attn_far, *out_arrived
    )
    attn_near, attn_far, out_arrived = rest[:2], rest[2:4], rest[4:]
    halves = [gate_up[:, :, :rows_half], gate_up[:, :, rows_half:]]
    arrived_1 = to_lines(halves[0], lines, z)
    arrived_2 = to_lines(halves[1], lines, z)
    out_piece = jnp.stack([out_own, *out_arrived])
    out_near = first_hop(out_piece)

    swapped += [swap_core(own) for own in ring[2:]]
    rows = jnp.zeros((lines, 2) + tokens.shape, bf16)
    for step, (own, other) in enumerate(zip(ring, swapped)):
        rows = put(rows, own, (z - step) % lines, core)
        rows = put(rows, other, (z - step) % lines, 1 - core)
    rows = rows.reshape(group_rows, features)
    attn_weights = four_pieces(attn_piece, *attn_near, *attn_far, x, y).reshape(features, -1)
    projected = jnp.dot(rows, attn_weights, preferred_element_type=f32)
    q_raw = projected[:, :head_cols]
    k_raw = projected[:, head_cols : 2 * head_cols]
    squares = jnp.stack([jnp.sum(q_raw * q_raw, axis=1), jnp.sum(k_raw * k_raw, axis=1)])
    squares = squares + swap_core(squares)
    total = squares
    for step in range(1, lines):
        total = total + over_mp(squares, lines, step)
    col_start = z * z_cols + core * head_cols
    query_part = lax.dynamic_slice_in_dim(query_gain, col_start, head_cols)
    key_part = lax.dynamic_slice_in_dim(key_gain, col_start, head_cols)
    total, out_piece, *rest = together(total, out_piece, *out_near, *arrived_1)
    out_near, arrived_1 = rest[:2], rest[2:]
    out_far = second_hop(*out_near)
    piece_1 = both_cores(halves[0], arrived_1, lines, z, core)
    near_1 = first_hop(piece_1)

    q_normed = q_raw * lax.rsqrt(total[0] / features + NORM_EPSILON)[:, None] * query_part
    k_normed = k_raw * lax.rsqrt(total[1] / features + NORM_EPSILON)[:, None] * key_part
    segment, position = token_layout(prompt_lens, group_rows)
    local_heads = head_cols // HEAD_DIM

    def heads_first(flat):
        return flat.reshape(group_rows, local_heads, HEAD_DIM).transpose(1, 0, 2)

    queries = rotary(heads_first(q_normed), position, HEAD_DIM).astype(bf16)
    keys_rot = rotary(heads_first(k_normed), position, HEAD_DIM).astype(bf16)
    values_h = heads_first(projected[:, 2 * head_cols :].astype(bf16))
    attended = jnp.stack(
        [
            head_attention(queries[h], keys_rot[h], values_h[h], segment, HEAD_DIM)
            for h in range(local_heads)
        ]
    )

    out_run = out_own.shape[0]
    runs = head_cols // out_run // 2
    attended = attended.transpose(1, 0, 2).reshape(lines, chip_rows, runs, 2, out_run)
    attended = attended.transpose(0, 3, 1, 2, 4).reshape(lines, 2, chip_rows, runs * out_run)
    arrived = jnp.stack([pick(attended, z)] + to_lines(attended, lines, z), axis=1)
    arrived, piece_1, out_piece, *rest = together(
        arrived, piece_1, out_piece, *out_near, *out_far, *near_1, *arrived_2
    )
    out_near, out_far, near_1, arrived_2 = rest[:2], rest[2:4], rest[4:6], rest[6:]
    far_1 = second_hop(*near_1)
    piece_2 = both_cores(halves[1], arrived_2, lines, z, core)
    near_2 = first_hop(piece_2)

    keep = pick(arrived, core)
    got = swap_core(pick(arrived, 1 - core))
    both = jnp.stack([jnp.where(core == 0, keep, got), jnp.where(core == 0, got, keep)], axis=0)
    both = both.reshape(2, lines, chip_rows, runs, out_run).transpose(2, 0, 3, 1, 4)
    both = both.reshape(chip_rows, -1)
    out_weights = four_pieces(out_piece, *out_near, *out_far, x, y).reshape(-1, features)
    partial = jnp.dot(both, out_weights, preferred_element_type=f32)
    partial = partial.reshape(2, tok_rows, features)
    attn_out = pick(partial, core) + swap_core(pick(partial, 1 - core).astype(bf16)).astype(f32)
    hidden = block.astype(f32) + rms_scale(attn_out, server_order(attn_post_gain))
    hidden = hidden.astype(bf16)

    ring = [hidden]
    for step in range(1, lines):
        ring.append(over_mp(ring[-1], lines, 1))
    ring[1], piece_2, *rest = together(ring[1], piece_2, *near_2, *far_1)
    near_2, far_1 = rest[:2], rest[2:]
    far_2 = second_hop(*near_2)
    first = four_pieces(piece_1, *near_1, *far_1, x, y)
    second = four_pieces(piece_2, *near_2, *far_2, x, y)
    mlp_weights = jnp.concatenate([first, second], axis=2).reshape(features, -1)
    down_block = four_pieces(down_own, *down_near, *down_far, x, y).reshape(-1, features)
    units = down_block.shape[0]

    def feed_forward(own):
        rows = jnp.concatenate([own, swap_core(own)], axis=0)
        both_proj = jnp.dot(rows, mlp_weights, preferred_element_type=f32)
        activated = (jax.nn.silu(both_proj[:, :units]) * both_proj[:, units:]).astype(bf16)
        out = jnp.dot(activated, down_block, preferred_element_type=f32)
        return out[:tok_rows] + swap_core(out[tok_rows:].astype(bf16)).astype(f32)

    total_out = None
    for step in range(1, lines):
        part = feed_forward(ring[step])
        if total_out is not None:
            part = part + total_out.astype(f32)
        part = part.astype(bf16)
        total_out = over_mp(part, lines, 1) if step + 1 < lines else swap_home(part, lines, 1)
    own_out = feed_forward(hidden).astype(bf16)
    own_out = jnp.where(home, own_out, swap_home(own_out, lines, 0)).astype(f32)
    hidden = given_order(hidden)
    hidden = jnp.where(home, hidden, swap_home(hidden, lines, 0)).astype(f32)
    mlp_out = own_out + total_out.astype(f32)
    return (hidden + rms_scale(mlp_out, mlp_post_gain)).astype(bf16)


def per_device(*arrays):
    heads = arrays[0].shape[1] // HEAD_DIM
    shards = lax.axis_size("mp")
    if lax.axis_size("group") == 4 and shards % 4 == 0 and heads % shards == 0:
        return per_device_lines(*arrays)
    return per_device_general(*arrays)


def solution(mesh):
    return jax.shard_map(
        per_device,
        mesh=mesh,
        in_specs=(
            P(("group", "mp"), None),
            P("group", None),
            P(),
            P(),
            P(),
            P(),
            P(("mp", "group"), None),
            P(("mp", "group"), None),
            P(("mp", "group"), None),
            P(("mp", "group"), None),
            P(("mp", "group"), None),
            P(("mp", "group"), None),
            P(("mp", "group"), None),
        ),
        out_specs=P(("group", "mp"), None),
        check_vma=False,
    )
```

```python
import math

import jax
import jax.numpy as jnp
from jax import lax
from jax.sharding import PartitionSpec as P

HEAD_DIM = 128


NORM_EPSILON = 1e-06
ROPE_BASE = 500000.0


def partner_2(block, axis, apart):
    count = lax.axis_size(axis)
    route = []
    for low in range(count):
        high = low | 1 << apart
        if high != low and high < count:
            route += [(low, high), (high, low)]
    return lax.ppermute(block, axis, route)


def token_layout(prompt_lens, row_count):
    seg_ends = jnp.cumsum(prompt_lens)
    starts = seg_ends - prompt_lens
    indices = jnp.arange(row_count, dtype=jnp.int32)
    segment = jnp.sum((indices[:, None] >= seg_ends[None, :]).astype(jnp.int32), axis=1)
    member = segment[:, None] == jnp.arange(prompt_lens.shape[0], dtype=jnp.int32)[None, :]
    opening = jnp.sum(jnp.where(member, starts[None, :], 0), axis=1)
    return (segment, indices - opening)


def rotary(head_values, position, head_size):
    half_size = head_size // 2
    frequency = jnp.exp(
        jnp.arange(half_size, dtype=jnp.float32) * (-2.0 * math.log(ROPE_BASE) / head_size)
    )
    angles = position.astype(jnp.float32)[:, None] * frequency[None, :]
    cosines = jnp.cos(angles)
    sines = jnp.sin(angles)
    front_half = head_values[..., :half_size]
    back_half = head_values[..., half_size:]
    return jnp.concatenate(
        [front_half * cosines - back_half * sines, back_half * cosines + front_half * sines],
        axis=-1,
    )


def head_attention(queries, keys_rot, values_h, segment, head_size):
    scores = lax.dot_general(
        queries, keys_rot, (((1,), (1,)), ((), ())), preferred_element_type=jnp.float32
    )
    scores = scores * (1.0 / math.sqrt(head_size))
    key_rows = jnp.arange(keys_rot.shape[0], dtype=jnp.int32)
    query_segment = segment
    allowed = (query_segment[:, None] == segment[None, :]) & (
        key_rows[None, :] <= key_rows[:, None]
    )
    scores = jnp.where(allowed, scores, -1e30)
    row_max = jnp.max(scores, axis=1, keepdims=True)
    weights = jnp.exp(scores - row_max)
    weights = weights / jnp.sum(weights, axis=1, keepdims=True)
    probabilities = weights.astype(jnp.bfloat16)
    return jnp.dot(probabilities, values_h, preferred_element_type=jnp.float32).astype(jnp.bfloat16)


def rms_scale(values_in, gain):
    return (
        values_in
        * lax.rsqrt(jnp.mean(values_in * values_in, axis=-1, keepdims=True) + NORM_EPSILON)
        * gain
    )


def per_device_general(
    tokens,
    lengths,
    query_gain,
    key_gain,
    attn_post_gain,
    mlp_post_gain,
    query_weight,
    key_weight,
    value_weight,
    output_weight,
    gate_weight,
    up_weight,
    down_weight,
):
    features = tokens.shape[1]
    shards = lax.axis_size("mp")
    my_index = lax.axis_index("mp")
    col_width = features // shards
    tok_rows = tokens.shape[0]
    group_rows = tok_rows * shards
    halves = col_width < HEAD_DIM
    stack_attn = jnp.stack([query_weight, key_weight, value_weight]).astype(jnp.bfloat16)
    stack_mlp = jnp.stack([gate_weight, up_weight]).astype(jnp.bfloat16)
    down_piece = down_weight.astype(jnp.bfloat16)[None]
    output_piece = output_weight.astype(jnp.bfloat16)[None]
    attn_rows, mlp_rows, down_rows, output_rows = (
        lax.all_gather(stack_attn, "group", axis=1, tiled=True),
        lax.all_gather(stack_mlp, "group", axis=1, tiled=True),
        lax.all_gather(down_piece, "group", axis=1, tiled=True),
        lax.all_gather(output_piece, "group", axis=1, tiled=True),
    )
    attn_block, mlp_block = (
        lax.all_to_all(attn_rows, "mp", split_axis=2, concat_axis=1, tiled=True),
        lax.all_to_all(mlp_rows, "mp", split_axis=2, concat_axis=1, tiled=True),
    )
    down_block = down_rows[0]
    output_block = output_rows[0]
    parity = my_index % 2
    if halves:
        partner = partner_2(attn_block, "mp", 0)
        attn_block = jnp.where(
            parity == 0,
            jnp.concatenate([attn_block, partner], axis=2),
            jnp.concatenate([partner, attn_block], axis=2),
        )
    head_cols = attn_block.shape[2]
    col_start = my_index * col_width // HEAD_DIM * HEAD_DIM
    share_part = col_width / head_cols
    projected = jnp.einsum(
        "td,kdc->ktc",
        lax.all_gather(tokens, "mp", axis=0, tiled=True),
        attn_block,
        preferred_element_type=jnp.float32,
    )
    query_sq = jnp.sum(projected[0] * projected[0], axis=1) * share_part
    key_sq = jnp.sum(projected[1] * projected[1], axis=1) * share_part
    query_total, key_total = lax.psum((query_sq, key_sq), "mp")
    query_part = lax.dynamic_slice_in_dim(query_gain, col_start, head_cols)
    key_part = lax.dynamic_slice_in_dim(key_gain, col_start, head_cols)
    q_normed = projected[0] * lax.rsqrt(query_total / features + NORM_EPSILON)[:, None] * query_part
    k_normed = projected[1] * lax.rsqrt(key_total / features + NORM_EPSILON)[:, None] * key_part
    segment, position = token_layout(lengths[0], group_rows)
    local_heads = head_cols // HEAD_DIM

    def heads_first(flat):
        return flat.reshape(group_rows, local_heads, HEAD_DIM).transpose(1, 0, 2)

    queries = rotary(heads_first(q_normed), position, HEAD_DIM).astype(jnp.bfloat16)
    keys_rot = rotary(heads_first(k_normed), position, HEAD_DIM).astype(jnp.bfloat16)
    values_h = heads_first(projected[2].astype(jnp.bfloat16))

    def per_head(triple):
        return head_attention(triple[0], triple[1], triple[2], segment, HEAD_DIM)

    attended = lax.map(per_head, (queries, keys_rot, values_h))
    attended = attended.transpose(1, 0, 2).reshape(group_rows, head_cols)
    if halves:
        attended = lax.dynamic_slice_in_dim(attended, parity * col_width, col_width, 1)
    rows_part = attended
    attn_out = lax.psum_scatter(
        jnp.dot(rows_part, output_block, preferred_element_type=jnp.float32).astype(jnp.bfloat16),
        "mp",
        scatter_dimension=0,
        tiled=True,
    ).astype(jnp.float32)
    hidden = (tokens.astype(jnp.float32) + rms_scale(attn_out, attn_post_gain)).astype(jnp.bfloat16)
    hidden_width = mlp_block.shape[2]
    mlp_weights = jnp.concatenate([mlp_block[0], mlp_block[1]], axis=1)
    both_proj = jnp.dot(
        lax.all_gather(hidden, "mp", axis=0, tiled=True),
        mlp_weights,
        preferred_element_type=jnp.float32,
    )
    activated = (jax.nn.silu(both_proj[:, :hidden_width]) * both_proj[:, hidden_width:]).astype(
        jnp.bfloat16
    )
    rows_part = activated
    mlp_out = lax.psum_scatter(
        jnp.dot(rows_part, down_block, preferred_element_type=jnp.float32).astype(jnp.bfloat16),
        "mp",
        scatter_dimension=0,
        tiled=True,
    ).astype(jnp.float32)
    return (hidden.astype(jnp.float32) + rms_scale(mlp_out, mlp_post_gain)).astype(jnp.bfloat16)


def over_mp(block, lines, step):
    count = 2 * lines
    return lax.ppermute(block, "mp", [(i, (i + 2 * step) % count) for i in range(count)])


def swap_x(block):
    return lax.ppermute(block, "mp", [(i, i ^ 1) for i in range(lax.axis_size("mp"))])


def swap_y(block):
    return lax.ppermute(block, "group", [(i, i ^ 2) for i in range(lax.axis_size("group"))])


def swap_core(block):
    return lax.ppermute(block, "group", [(i, i ^ 1) for i in range(lax.axis_size("group"))])


def swap_home(block, lines, step):
    shards = 2 * lines
    route = []
    for group in range(lax.axis_size("group")):
        for index in range(shards):
            apart = index % 2 ^ group % 2
            to = ((index + 2 * step) % shards) ^ apart
            if step or apart:
                route.append((group * shards + index, (group ^ apart) * shards + to))
    return lax.ppermute(block, ("group", "mp"), route)


def together(*arrays):
    return lax.optimization_barrier(arrays)


def put(buffer, block, *place):
    shape = (1,) * len(place) + block.shape
    rest = (0,) * (buffer.ndim - len(place))
    return lax.dynamic_update_slice(buffer, block.reshape(shape), tuple(place) + rest)


def pick(buffer, index):
    return lax.dynamic_index_in_dim(buffer, index, 0, keepdims=False)


def first_hop(piece):
    return swap_x(piece), swap_y(piece)


def second_hop(at_x, at_y):
    split = at_x.shape[0] // 2
    return swap_y(at_x[:split]), swap_x(at_y[split:])


def four_pieces(whole, piece, at_x, at_y, far_low, far_high, x, y, part):
    def write(block, column, row, half=None):
        at = 0 if half is None else half
        block = block.reshape((1, -1) + whole.shape[2:3] + (1,) + whole.shape[4:])
        place = (2 * column + row, at, 0, part) + (0,) * (whole.ndim - 4)
        return lax.dynamic_update_slice(whole, block, place)

    whole = write(piece, x, y)
    whole = write(at_x, 1 - x, y)
    whole = write(at_y, x, 1 - y)
    whole = write(far_low, 1 - x, 1 - y, 0)
    return write(far_high, 1 - x, 1 - y, 1)


def gather_chips(block, with_z):
    groups, lines = lax.axis_size("group"), lax.axis_size("mp") // 2
    at = [[[(2 * y + c) * 2 * lines + 2 * z + x for x in range(2) for y in range(2)] for z in range(lines)]
          for c in range(groups // 2)]
    if with_z:
        sets = [sum(at[c], []) for c in range(groups // 2)]
    else:
        sets = [at[c][z] for c in range(groups // 2) for z in range(lines)]
    return lax.all_gather(block, ("group", "mp"), axis=0, axis_index_groups=sets, tiled=True)


def to_lines(parts, lines, z):
    return [over_mp(pick(parts, (z + step) % lines), lines, step) for step in range(1, lines)]


def both_cores(parts, arrived, lines, z, core):
    held = jnp.zeros(parts.shape, parts.dtype)
    held = put(held, pick(parts, z), z)
    for step, block in enumerate(arrived, 1):
        held = put(held, block, (z - step) % lines)
    return to_both_cores(held, core)


def to_both_cores(held, core):
    held = held.transpose(1, 0, 2, 3)
    other = swap_core(pick(held, 1 - core))
    mine = pick(held, core)
    both = jnp.stack([jnp.where(core == 0, mine, other), jnp.where(core == 0, other, mine)], axis=1)
    return both.reshape((-1,) + both.shape[2:])


def per_device_lines(
    tokens,
    lengths,
    query_gain,
    key_gain,
    attn_post_gain,
    mlp_post_gain,
    query_weight,
    key_weight,
    value_weight,
    output_weight,
    gate_weight,
    up_weight,
    down_weight,
):
    bf16, f32 = jnp.bfloat16, jnp.float32
    features = tokens.shape[1]
    shards = lax.axis_size("mp")
    lines = shards // 2
    index = lax.axis_index("mp")
    z, x = index // 2, index % 2
    group = lax.axis_index("group")
    y, core = group // 2, group % 2
    tok_rows = tokens.shape[0]
    chip_rows = 2 * tok_rows
    group_rows = shards * tok_rows
    home = x == core

    z_cols = features // lines
    head_cols = z_cols // 2
    run = features // shards // 2

    def server_order(rows):
        parts = rows.reshape(rows.shape[:-1] + (lines, 4, run))
        return jnp.swapaxes(parts, -3, -2).reshape(rows.shape)

    def given_order(rows):
        parts = rows.reshape(rows.shape[:-1] + (4, lines, run))
        return jnp.swapaxes(parts, -3, -2).reshape(rows.shape)

    def by_owner(weights, runs):
        parts = [w.astype(bf16).reshape(w.shape[0], lines, runs, 2, -1) for w in weights]
        parts = jnp.stack(parts, axis=2).transpose(1, 4, 0, 2, 3, 5)
        return parts.reshape(lines, 2, weights[0].shape[0], -1)

    own_order = server_order(tokens)
    attn_parts = by_owner((query_weight, key_weight, value_weight), 1)
    attn_arrived = to_lines(attn_parts, lines, z)
    ring_1 = swap_home(own_order, lines, 1)
    moved = swap_home(own_order, lines, 0)
    out_own = server_order(output_weight.astype(bf16))
    out_weights = gather_chips(out_own, True)
    own_order, ring_1, moved, *attn_arrived = together(own_order, ring_1, moved, *attn_arrived)
    block = jnp.where(home, own_order, moved)
    ring = [block, ring_1]

    attn_piece = both_cores(attn_parts, attn_arrived, lines, z, core)
    attn_near = first_hop(attn_piece)
    if lines > 2:
        ring.append(over_mp(ring[-1], lines, 1))
    swapped = [swap_core(own) for own in ring[:2]]
    ring[-1], attn_piece, *rest = together(ring[-1], attn_piece, *attn_near, *swapped)
    attn_near, swapped = rest[:2], rest[2:]

    attn_far = second_hop(*attn_near)
    for step in range(3, lines):
        ring.append(over_mp(ring[-1], lines, 1))
    swapped += [swap_core(own) for own in ring[2:-1]]
    gate_up = by_owner((gate_weight, up_weight), 4)
    prompt_lens = jnp.where(home, lengths, swap_core(lengths))[0]
    gate_up, attn_piece, ring[-1], down_own, prompt_lens, *rest = together(
        gate_up, attn_piece, ring[-1], down_weight, prompt_lens, *attn_near, *attn_far, *swapped
    )
    attn_near, attn_far, swapped = rest[:2], rest[2:4], rest[4:]
    rows_half = gate_up.shape[2] // 2
    halves = [gate_up[:, :, :rows_half], gate_up[:, :, rows_half:]]
    arrived_1 = to_lines(halves[0], lines, z)
    down_block = gather_chips(down_own.astype(bf16), False)
    swapped += [swap_core(own) for own in ring[len(swapped) :]]

    rows = jnp.zeros((lines, 2) + tokens.shape, bf16)
    for step, (own, other) in enumerate(zip(ring, swapped)):
        rows = put(rows, own, (z - step) % lines, core)
        rows = put(rows, other, (z - step) % lines, 1 - core)
    rows = rows.reshape(group_rows, features)
    attn_weights = jnp.zeros((4, 2, lines, 1) + attn_piece.shape[1:], bf16)
    attn_weights = four_pieces(attn_weights, attn_piece, *attn_near, *attn_far, x, y, 0)
    attn_weights = attn_weights.reshape(features, -1)
    projected = jnp.dot(rows, attn_weights, preferred_element_type=f32)
    q_raw = projected[:, :head_cols]
    k_raw = projected[:, head_cols : 2 * head_cols]
    squares = jnp.stack([jnp.sum(q_raw * q_raw, axis=1), jnp.sum(k_raw * k_raw, axis=1)])
    squares = squares + swap_core(squares)
    total = squares
    for step in range(1, lines):
        total = total + over_mp(squares, lines, step)
    col_start = z * z_cols + core * head_cols
    query_part = lax.dynamic_slice_in_dim(query_gain, col_start, head_cols)
    key_part = lax.dynamic_slice_in_dim(key_gain, col_start, head_cols)
    total, *halves = together(total, *halves)
    sets = [[2 * a + b for a in range(lines)] for b in range(2)]
    arrived_2 = lax.all_to_all(
        halves[1], "mp", split_axis=0, concat_axis=0, axis_index_groups=sets, tiled=True
    )

    q_normed = q_raw * lax.rsqrt(total[0] / features + NORM_EPSILON)[:, None] * query_part
    k_normed = k_raw * lax.rsqrt(total[1] / features + NORM_EPSILON)[:, None] * key_part
    segment, position = token_layout(prompt_lens, group_rows)
    local_heads = head_cols // HEAD_DIM

    def heads_first(flat):
        return flat.reshape(group_rows, local_heads, HEAD_DIM).transpose(1, 0, 2)

    queries = rotary(heads_first(q_normed), position, HEAD_DIM).astype(bf16)
    keys_rot = rotary(heads_first(k_normed), position, HEAD_DIM).astype(bf16)
    values_h = heads_first(projected[:, 2 * head_cols :].astype(bf16))
    attended = jnp.stack(
        [
            head_attention(queries[h], keys_rot[h], values_h[h], segment, HEAD_DIM)
            for h in range(local_heads)
        ]
    )

    out_run = out_own.shape[0]
    runs = head_cols // out_run // 2
    attended = attended.transpose(1, 0, 2).reshape(lines, chip_rows, runs, 2, out_run)
    attended = attended.transpose(0, 3, 1, 2, 4).reshape(lines, 2, chip_rows, runs * out_run)
    attended, out_weights, *arrived_1 = together(attended, out_weights, *arrived_1)
    arrived = jnp.zeros(attended.shape, bf16)
    arrived = put(arrived, pick(attended, z), z)
    for step, part in enumerate(to_lines(attended, lines, z), 1):
        arrived = put(arrived, part, (z - step) % lines)
    arrived = arrived.transpose(1, 0, 2, 3)
    piece_1 = both_cores(halves[0], arrived_1, lines, z, core)
    near_1 = first_hop(piece_1)

    keep = pick(arrived, core)
    got = swap_core(pick(arrived, 1 - core))
    both = jnp.stack([jnp.where(core == 0, keep, got), jnp.where(core == 0, got, keep)], axis=0)
    both = both.reshape(2, lines, chip_rows, runs, out_run).transpose(2, 1, 0, 3, 4)
    both = both.reshape(chip_rows, -1)
    partial = jnp.dot(both, out_weights, preferred_element_type=f32)
    partial = partial.reshape(2, tok_rows, features)
    attn_out = pick(partial, core) + swap_core(pick(partial, 1 - core).astype(bf16)).astype(f32)
    hidden = block.astype(f32) + rms_scale(attn_out, server_order(attn_post_gain))
    hidden = hidden.astype(bf16)

    hidden, piece_1, arrived_2, *near_1 = together(hidden, piece_1, arrived_2, *near_1)
    far_1 = second_hop(*near_1)
    piece_2 = to_both_cores(arrived_2, core)
    near_2 = first_hop(piece_2)
    ring = [hidden]
    for step in range(1, lines):
        ring.append(over_mp(ring[-1], lines, 1))
    late = min(2, lines - 1)
    ring[late], piece_2, down_block, *rest = together(
        ring[late], piece_2, down_block, *far_1, *near_2
    )
    far_1, near_2 = rest[:2], rest[2:]
    for step in range(late + 1, lines):
        ring[step] = over_mp(ring[step - 1], lines, 1)
    far_2 = second_hop(*near_2)
    mlp_weights = jnp.zeros((4, 2, lines, 2) + piece_1.shape[1:], bf16)
    mlp_weights = four_pieces(mlp_weights, piece_1, *near_1, *far_1, x, y, 0)
    mlp_weights = four_pieces(mlp_weights, piece_2, *near_2, *far_2, x, y, 1)
    mlp_weights = mlp_weights.reshape(features, -1)
    units = down_block.shape[0]

    def feed_forward(own):
        rows = jnp.concatenate([own, swap_core(own)], axis=0)
        both_proj = jnp.dot(rows, mlp_weights, preferred_element_type=f32)
        activated = (jax.nn.silu(both_proj[:, :units]) * both_proj[:, units:]).astype(bf16)
        out = jnp.dot(activated, down_block, preferred_element_type=f32)
        return out[:tok_rows] + swap_core(out[tok_rows:].astype(bf16)).astype(f32)

    total_out = None
    for step in range(1, lines):
        part = feed_forward(ring[step])
        if total_out is not None:
            part = part + total_out.astype(f32)
        part = part.astype(bf16)
        total_out = over_mp(part, lines, 1) if step + 1 < lines else swap_home(part, lines, 1)
    own_out = feed_forward(hidden).astype(bf16)
    own_out = jnp.where(home, own_out, swap_home(own_out, lines, 0)).astype(f32)
    hidden = given_order(hidden)
    hidden = jnp.where(home, hidden, swap_home(hidden, lines, 0)).astype(f32)
    mlp_out = own_out + total_out.astype(f32)
    return (hidden + rms_scale(mlp_out, mlp_post_gain)).astype(bf16)


def per_device(*arrays):
    heads = arrays[0].shape[1] // HEAD_DIM
    shards = lax.axis_size("mp")
    if lax.axis_size("group") == 4 and shards % 4 == 0 and heads % shards == 0:
        return per_device_lines(*arrays)
    return per_device_general(*arrays)


def solution(mesh):
    return jax.shard_map(
        per_device,
        mesh=mesh,
        in_specs=(
            P(("group", "mp"), None),
            P("group", None),
            P(),
            P(),
            P(),
            P(),
            P(("mp", "group"), None),
            P(("mp", "group"), None),
            P(("mp", "group"), None),
            P(("mp", "group"), None),
            P(("mp", "group"), None),
            P(("mp", "group"), None),
            P(("mp", "group"), None),
        ),
        out_specs=P(("group", "mp"), None),
        check_vma=False,
    )
```

```python
import math

import jax
import jax.numpy as jnp
from jax import lax
from jax.sharding import PartitionSpec as P

HEAD_DIM = 128


NORM_EPSILON = 1e-06
ROPE_BASE = 500000.0


def partner_2(block, axis, apart):
    count = lax.axis_size(axis)
    route = []
    for low in range(count):
        high = low | 1 << apart
        if high != low and high < count:
            route += [(low, high), (high, low)]
    return lax.ppermute(block, axis, route)


def token_layout(prompt_lens, row_count):
    seg_ends = jnp.cumsum(prompt_lens)
    starts = seg_ends - prompt_lens
    indices = jnp.arange(row_count, dtype=jnp.int32)
    segment = jnp.sum((indices[:, None] >= seg_ends[None, :]).astype(jnp.int32), axis=1)
    member = segment[:, None] == jnp.arange(prompt_lens.shape[0], dtype=jnp.int32)[None, :]
    opening = jnp.sum(jnp.where(member, starts[None, :], 0), axis=1)
    return (segment, indices - opening)


def rotary(head_values, position, head_size):
    half_size = head_size // 2
    frequency = jnp.exp(
        jnp.arange(half_size, dtype=jnp.float32) * (-2.0 * math.log(ROPE_BASE) / head_size)
    )
    angles = position.astype(jnp.float32)[:, None] * frequency[None, :]
    cosines = jnp.cos(angles)
    sines = jnp.sin(angles)
    front_half = head_values[..., :half_size]
    back_half = head_values[..., half_size:]
    return jnp.concatenate(
        [front_half * cosines - back_half * sines, back_half * cosines + front_half * sines],
        axis=-1,
    )


def head_attention(queries, keys_rot, values_h, segment, head_size):
    scores = lax.dot_general(
        queries, keys_rot, (((1,), (1,)), ((), ())), preferred_element_type=jnp.float32
    )
    scores = scores * (1.0 / math.sqrt(head_size))
    key_rows = jnp.arange(keys_rot.shape[0], dtype=jnp.int32)
    query_segment = segment
    allowed = (query_segment[:, None] == segment[None, :]) & (
        key_rows[None, :] <= key_rows[:, None]
    )
    scores = jnp.where(allowed, scores, -1e30)
    row_max = jnp.max(scores, axis=1, keepdims=True)
    weights = jnp.exp(scores - row_max)
    weights = weights / jnp.sum(weights, axis=1, keepdims=True)
    probabilities = weights.astype(jnp.bfloat16)
    return jnp.dot(probabilities, values_h, preferred_element_type=jnp.float32).astype(jnp.bfloat16)


def rms_scale(values_in, gain):
    return (
        values_in
        * lax.rsqrt(jnp.mean(values_in * values_in, axis=-1, keepdims=True) + NORM_EPSILON)
        * gain
    )


def per_device_general(
    tokens,
    lengths,
    query_gain,
    key_gain,
    attn_post_gain,
    mlp_post_gain,
    query_weight,
    key_weight,
    value_weight,
    output_weight,
    gate_weight,
    up_weight,
    down_weight,
):
    features = tokens.shape[1]
    shards = lax.axis_size("mp")
    my_index = lax.axis_index("mp")
    col_width = features // shards
    tok_rows = tokens.shape[0]
    group_rows = tok_rows * shards
    halves = col_width < HEAD_DIM
    stack_attn = jnp.stack([query_weight, key_weight, value_weight]).astype(jnp.bfloat16)
    stack_mlp = jnp.stack([gate_weight, up_weight]).astype(jnp.bfloat16)
    down_piece = down_weight.astype(jnp.bfloat16)[None]
    output_piece = output_weight.astype(jnp.bfloat16)[None]
    attn_rows, mlp_rows, down_rows, output_rows = (
        lax.all_gather(stack_attn, "group", axis=1, tiled=True),
        lax.all_gather(stack_mlp, "group", axis=1, tiled=True),
        lax.all_gather(down_piece, "group", axis=1, tiled=True),
        lax.all_gather(output_piece, "group", axis=1, tiled=True),
    )
    attn_block, mlp_block = (
        lax.all_to_all(attn_rows, "mp", split_axis=2, concat_axis=1, tiled=True),
        lax.all_to_all(mlp_rows, "mp", split_axis=2, concat_axis=1, tiled=True),
    )
    down_block = down_rows[0]
    output_block = output_rows[0]
    parity = my_index % 2
    if halves:
        partner = partner_2(attn_block, "mp", 0)
        attn_block = jnp.where(
            parity == 0,
            jnp.concatenate([attn_block, partner], axis=2),
            jnp.concatenate([partner, attn_block], axis=2),
        )
    head_cols = attn_block.shape[2]
    col_start = my_index * col_width // HEAD_DIM * HEAD_DIM
    share_part = col_width / head_cols
    projected = jnp.einsum(
        "td,kdc->ktc",
        lax.all_gather(tokens, "mp", axis=0, tiled=True),
        attn_block,
        preferred_element_type=jnp.float32,
    )
    query_sq = jnp.sum(projected[0] * projected[0], axis=1) * share_part
    key_sq = jnp.sum(projected[1] * projected[1], axis=1) * share_part
    query_total, key_total = lax.psum((query_sq, key_sq), "mp")
    query_part = lax.dynamic_slice_in_dim(query_gain, col_start, head_cols)
    key_part = lax.dynamic_slice_in_dim(key_gain, col_start, head_cols)
    q_normed = projected[0] * lax.rsqrt(query_total / features + NORM_EPSILON)[:, None] * query_part
    k_normed = projected[1] * lax.rsqrt(key_total / features + NORM_EPSILON)[:, None] * key_part
    segment, position = token_layout(lengths[0], group_rows)
    local_heads = head_cols // HEAD_DIM

    def heads_first(flat):
        return flat.reshape(group_rows, local_heads, HEAD_DIM).transpose(1, 0, 2)

    queries = rotary(heads_first(q_normed), position, HEAD_DIM).astype(jnp.bfloat16)
    keys_rot = rotary(heads_first(k_normed), position, HEAD_DIM).astype(jnp.bfloat16)
    values_h = heads_first(projected[2].astype(jnp.bfloat16))

    def per_head(triple):
        return head_attention(triple[0], triple[1], triple[2], segment, HEAD_DIM)

    attended = lax.map(per_head, (queries, keys_rot, values_h))
    attended = attended.transpose(1, 0, 2).reshape(group_rows, head_cols)
    if halves:
        attended = lax.dynamic_slice_in_dim(attended, parity * col_width, col_width, 1)
    rows_part = attended
    attn_out = lax.psum_scatter(
        jnp.dot(rows_part, output_block, preferred_element_type=jnp.float32).astype(jnp.bfloat16),
        "mp",
        scatter_dimension=0,
        tiled=True,
    ).astype(jnp.float32)
    hidden = (tokens.astype(jnp.float32) + rms_scale(attn_out, attn_post_gain)).astype(jnp.bfloat16)
    hidden_width = mlp_block.shape[2]
    mlp_weights = jnp.concatenate([mlp_block[0], mlp_block[1]], axis=1)
    both_proj = jnp.dot(
        lax.all_gather(hidden, "mp", axis=0, tiled=True),
        mlp_weights,
        preferred_element_type=jnp.float32,
    )
    activated = (jax.nn.silu(both_proj[:, :hidden_width]) * both_proj[:, hidden_width:]).astype(
        jnp.bfloat16
    )
    rows_part = activated
    mlp_out = lax.psum_scatter(
        jnp.dot(rows_part, down_block, preferred_element_type=jnp.float32).astype(jnp.bfloat16),
        "mp",
        scatter_dimension=0,
        tiled=True,
    ).astype(jnp.float32)
    return (hidden.astype(jnp.float32) + rms_scale(mlp_out, mlp_post_gain)).astype(jnp.bfloat16)


def over_mp(block, lines, step):
    count = 2 * lines
    return lax.ppermute(block, "mp", [(i, (i + 2 * step) % count) for i in range(count)])


def swap_x(block):
    return lax.ppermute(block, "mp", [(i, i ^ 1) for i in range(lax.axis_size("mp"))])


def swap_y(block):
    return lax.ppermute(block, "group", [(i, i ^ 2) for i in range(lax.axis_size("group"))])


def swap_core(block):
    return lax.ppermute(block, "group", [(i, i ^ 1) for i in range(lax.axis_size("group"))])


def swap_home(block, lines, step):
    shards = 2 * lines
    route = []
    for group in range(lax.axis_size("group")):
        for index in range(shards):
            apart = index % 2 ^ group % 2
            to = ((index + 2 * step) % shards) ^ apart
            if step or apart:
                route.append((group * shards + index, (group ^ apart) * shards + to))
    return lax.ppermute(block, ("group", "mp"), route)


def together(*arrays):
    return lax.optimization_barrier(arrays)


def put(buffer, block, *place):
    shape = (1,) * len(place) + block.shape
    rest = (0,) * (buffer.ndim - len(place))
    return lax.dynamic_update_slice(buffer, block.reshape(shape), tuple(place) + rest)


def pick(buffer, index):
    return lax.dynamic_index_in_dim(buffer, index, 0, keepdims=False)


def first_hop(piece):
    return swap_x(piece), swap_y(piece)


def second_hop(at_x, at_y):
    split = at_x.shape[0] // 2
    return swap_y(at_x[:split]), swap_x(at_y[split:])


def four_pieces(whole, piece, at_x, at_y, far_low, far_high, x, y, part):
    def write(block, column, row, half=None):
        at = 0 if half is None else half
        block = block.reshape((1, -1) + whole.shape[2:3] + (1,) + whole.shape[4:])
        place = (2 * column + row, at, 0, part) + (0,) * (whole.ndim - 4)
        return lax.dynamic_update_slice(whole, block, place)

    whole = write(piece, x, y)
    whole = write(at_x, 1 - x, y)
    whole = write(at_y, x, 1 - y)
    whole = write(far_low, 1 - x, 1 - y, 0)
    return write(far_high, 1 - x, 1 - y, 1)


def to_lines(parts, lines, z):
    return [over_mp(pick(parts, (z + step) % lines), lines, step) for step in range(1, lines)]


def both_cores(parts, arrived, lines, z, core):
    held = jnp.zeros(parts.shape, parts.dtype)
    held = put(held, pick(parts, z), z)
    for step, block in enumerate(arrived, 1):
        held = put(held, block, (z - step) % lines)
    return to_both_cores(held, core)


def to_both_cores(held, core):
    held = held.transpose(1, 0, 2, 3)
    other = swap_core(pick(held, 1 - core))
    mine = pick(held, core)
    both = jnp.stack([jnp.where(core == 0, mine, other), jnp.where(core == 0, other, mine)], axis=1)
    return both.reshape((-1,) + both.shape[2:])


def per_device_lines(
    tokens,
    lengths,
    query_gain,
    key_gain,
    attn_post_gain,
    mlp_post_gain,
    query_weight,
    key_weight,
    value_weight,
    output_weight,
    gate_weight,
    up_weight,
    down_weight,
):
    bf16, f32 = jnp.bfloat16, jnp.float32
    features = tokens.shape[1]
    shards = lax.axis_size("mp")
    lines = shards // 2
    index = lax.axis_index("mp")
    z, x = index // 2, index % 2
    group = lax.axis_index("group")
    y, core = group // 2, group % 2
    tok_rows = tokens.shape[0]
    chip_rows = 2 * tok_rows
    group_rows = shards * tok_rows
    home = x == core

    z_cols = features // lines
    head_cols = z_cols // 2
    run = features // shards // 2

    def server_order(rows):
        parts = rows.reshape(rows.shape[:-1] + (lines, 4, run))
        return jnp.swapaxes(parts, -3, -2).reshape(rows.shape)

    def given_order(rows):
        parts = rows.reshape(rows.shape[:-1] + (4, lines, run))
        return jnp.swapaxes(parts, -3, -2).reshape(rows.shape)

    def by_owner(weights, runs):
        parts = [w.astype(bf16).reshape(w.shape[0], lines, runs, 2, -1) for w in weights]
        parts = jnp.stack(parts, axis=2).transpose(1, 4, 0, 2, 3, 5)
        return parts.reshape(lines, 2, weights[0].shape[0], -1)

    own = jnp.concatenate([server_order(tokens), server_order(output_weight.astype(bf16))], axis=0)
    attn_parts = by_owner((query_weight, key_weight, value_weight), 1)
    attn_arrived = to_lines(attn_parts, lines, z)
    ring_1 = swap_home(own, lines, 1)
    down_own = down_weight.astype(bf16)
    down_near = first_hop(down_own)
    own, ring_1, down_own, *rest = together(own, ring_1, down_own, *down_near, *attn_arrived)
    down_near, attn_arrived = rest[:2], rest[2:]

    ring = [None, ring_1]
    if lines > 2:
        ring.append(over_mp(ring[-1], lines, 1))
    ring[0] = jnp.where(home, own, swap_home(own, lines, 0))
    attn_piece = both_cores(attn_parts, attn_arrived, lines, z, core)
    attn_near = first_hop(attn_piece)
    swapped = [swap_core(block) for block in ring[:2]]
    ring[-1], attn_piece, *rest = together(ring[-1], attn_piece, *attn_near, *swapped)
    attn_near, swapped = rest[:2], rest[2:]

    attn_far = second_hop(*attn_near)
    down_far = second_hop(*down_near)
    for step in range(3, lines):
        ring.append(over_mp(ring[-1], lines, 1))
    swapped += [swap_core(block) for block in ring[2:-1]]
    gate_up = by_owner((gate_weight, up_weight), 4)
    prompt_lens = jnp.where(home, lengths, swap_core(lengths))[0]
    gate_up, attn_piece, ring[-1], prompt_lens, *rest = together(
        gate_up, attn_piece, ring[-1], prompt_lens, *attn_near, *attn_far, *down_far, *swapped
    )
    attn_near, attn_far, down_far, swapped = rest[:2], rest[2:4], rest[4:6], rest[6:]
    rows_half = gate_up.shape[2] // 2
    halves = [gate_up[:, :, :rows_half], gate_up[:, :, rows_half:]]
    arrived_1 = to_lines(halves[0], lines, z)
    swapped += [swap_core(block) for block in ring[len(swapped) :]]
    block = ring[0][:tok_rows]
    out_piece = jnp.stack([held[tok_rows:] for held in ring])
    out_near = first_hop(out_piece)

    rows = jnp.zeros((lines, 2) + tokens.shape, bf16)
    for step, (own, other) in enumerate(zip(ring, swapped)):
        rows = put(rows, own[:tok_rows], (z - step) % lines, core)
        rows = put(rows, other[:tok_rows], (z - step) % lines, 1 - core)
    rows = rows.reshape(group_rows, features)
    attn_weights = jnp.zeros((4, 2, lines, 1) + attn_piece.shape[1:], bf16)
    attn_weights = four_pieces(attn_weights, attn_piece, *attn_near, *attn_far, x, y, 0)
    attn_weights = attn_weights.reshape(features, -1)
    projected = jnp.dot(rows, attn_weights, preferred_element_type=f32)
    q_raw = projected[:, :head_cols]
    k_raw = projected[:, head_cols : 2 * head_cols]
    squares = jnp.stack([jnp.sum(q_raw * q_raw, axis=1), jnp.sum(k_raw * k_raw, axis=1)])
    squares = squares + swap_core(squares)
    total = squares
    for step in range(1, lines):
        total = total + over_mp(squares, lines, step)
    col_start = z * z_cols + core * head_cols
    query_part = lax.dynamic_slice_in_dim(query_gain, col_start, head_cols)
    key_part = lax.dynamic_slice_in_dim(key_gain, col_start, head_cols)
    total, late_half, out_piece, *out_near = together(total, halves[1], out_piece, *out_near)
    arrived_2 = to_lines(late_half, lines, z)
    out_far = second_hop(*out_near)

    q_normed = q_raw * lax.rsqrt(total[0] / features + NORM_EPSILON)[:, None] * query_part
    k_normed = k_raw * lax.rsqrt(total[1] / features + NORM_EPSILON)[:, None] * key_part
    segment, position = token_layout(prompt_lens, group_rows)
    local_heads = head_cols // HEAD_DIM

    def heads_first(flat):
        return flat.reshape(group_rows, local_heads, HEAD_DIM).transpose(1, 0, 2)

    queries = rotary(heads_first(q_normed), position, HEAD_DIM).astype(bf16)
    keys_rot = rotary(heads_first(k_normed), position, HEAD_DIM).astype(bf16)
    values_h = heads_first(projected[:, 2 * head_cols :].astype(bf16))
    attended = jnp.stack(
        [
            head_attention(queries[h], keys_rot[h], values_h[h], segment, HEAD_DIM)
            for h in range(local_heads)
        ]
    )

    attended = attended.transpose(1, 0, 2).reshape(lines, chip_rows, head_cols)
    attended, out_piece, *rest = together(
        attended, out_piece, *out_near, *out_far, *arrived_1, *arrived_2
    )
    out_near, out_far, rest = rest[:2], rest[2:4], rest[4:]
    arrived_1, arrived_2 = rest[: lines - 1], rest[lines - 1 :]
    both = jnp.concatenate([pick(attended, z)] + to_lines(attended, lines, z), axis=1)
    piece_1 = both_cores(halves[0], arrived_1, lines, z, core)
    near_1 = first_hop(piece_1)
    out_weights = jnp.zeros((lines, 2, 2) + out_piece.shape[1:], bf16)
    split = lines // 2
    for held, row, column, at in (
        (out_piece, y, x, 0),
        (out_near[0], y, 1 - x, 0),
        (out_near[1], 1 - y, x, 0),
        (out_far[0], 1 - y, 1 - x, 0),
        (out_far[1], 1 - y, 1 - x, split),
    ):
        out_weights = lax.dynamic_update_slice(
            out_weights, held[:, None, None], (at, row, column, 0, 0)
        )
    out_weights = out_weights.reshape(-1, features)
    partial = jnp.dot(both, out_weights, preferred_element_type=f32)
    partial = partial.reshape(2, tok_rows, features)
    attn_out = pick(partial, core) + swap_core(pick(partial, 1 - core).astype(bf16)).astype(f32)
    hidden = block.astype(f32) + rms_scale(attn_out, server_order(attn_post_gain))
    hidden = hidden.astype(bf16)

    hidden, piece_1, *near_1 = together(hidden, piece_1, *near_1)
    ring = [hidden]
    for step in range(1, lines):
        ring.append(over_mp(ring[-1], lines, 1))
    far_1 = second_hop(*near_1)
    piece_2 = both_cores(late_half, arrived_2, lines, z, core)
    near_2 = first_hop(piece_2)
    ring[1], piece_2, *rest = together(ring[1], piece_2, *far_1, *near_2)
    far_1, near_2 = rest[:2], rest[2:]
    for step in range(2, lines):
        ring[step] = over_mp(ring[step - 1], lines, 1)
    far_2 = second_hop(*near_2)
    mlp_weights = jnp.zeros((4, 2, lines, 2) + piece_1.shape[1:], bf16)
    mlp_weights = four_pieces(mlp_weights, piece_1, *near_1, *far_1, x, y, 0)
    mlp_weights = four_pieces(mlp_weights, piece_2, *near_2, *far_2, x, y, 1)
    mlp_weights = mlp_weights.reshape(features, -1)
    down_block = jnp.zeros((4, 2, down_own.shape[0] // 2, 1, features), bf16)
    down_block = four_pieces(down_block, down_own, *down_near, *down_far, x, y, 0)
    down_block = down_block.reshape(-1, features)
    units = down_block.shape[0]

    def feed_forward(own):
        rows = jnp.concatenate([own, swap_core(own)], axis=0)
        both_proj = jnp.dot(rows, mlp_weights, preferred_element_type=f32)
        activated = (jax.nn.silu(both_proj[:, :units]) * both_proj[:, units:]).astype(bf16)
        out = jnp.dot(activated, down_block, preferred_element_type=f32)
        return out[:tok_rows] + swap_core(out[tok_rows:].astype(bf16)).astype(f32)

    total_out = None
    for step in range(1, lines):
        part = feed_forward(ring[step])
        if total_out is not None:
            part = part + total_out.astype(f32)
        part = part.astype(bf16)
        total_out = over_mp(part, lines, 1) if step + 1 < lines else swap_home(part, lines, 1)
    own_out = feed_forward(hidden).astype(bf16)
    own_out = jnp.where(home, own_out, swap_home(own_out, lines, 0)).astype(f32)
    hidden = given_order(hidden)
    hidden = jnp.where(home, hidden, swap_home(hidden, lines, 0)).astype(f32)
    mlp_out = own_out + total_out.astype(f32)
    return (hidden + rms_scale(mlp_out, mlp_post_gain)).astype(bf16)


def per_device(*arrays):
    heads = arrays[0].shape[1] // HEAD_DIM
    shards = lax.axis_size("mp")
    if lax.axis_size("group") == 4 and shards % 4 == 0 and heads % shards == 0:
        return per_device_lines(*arrays)
    return per_device_general(*arrays)


def solution(mesh):
    return jax.shard_map(
        per_device,
        mesh=mesh,
        in_specs=(
            P(("group", "mp"), None),
            P("group", None),
            P(),
            P(),
            P(),
            P(),
            P(("mp", "group"), None),
            P(("mp", "group"), None),
            P(("mp", "group"), None),
            P(("mp", "group"), None),
            P(("mp", "group"), None),
            P(("mp", "group"), None),
            P(("mp", "group"), None),
        ),
        out_specs=P(("group", "mp"), None),
        check_vma=False,
    )
```

```python
import math

import jax
import jax.numpy as jnp
from jax import lax
from jax.sharding import PartitionSpec as P

HEAD_DIM = 128


NORM_EPSILON = 1e-06
ROPE_BASE = 500000.0


def partner_2(block, axis, apart):
    count = lax.axis_size(axis)
    route = []
    for low in range(count):
        high = low | 1 << apart
        if high != low and high < count:
            route += [(low, high), (high, low)]
    return lax.ppermute(block, axis, route)


def token_layout(prompt_lens, row_count):
    seg_ends = jnp.cumsum(prompt_lens)
    starts = seg_ends - prompt_lens
    indices = jnp.arange(row_count, dtype=jnp.int32)
    segment = jnp.sum((indices[:, None] >= seg_ends[None, :]).astype(jnp.int32), axis=1)
    member = segment[:, None] == jnp.arange(prompt_lens.shape[0], dtype=jnp.int32)[None, :]
    opening = jnp.sum(jnp.where(member, starts[None, :], 0), axis=1)
    return (segment, indices - opening)


def rotary(head_values, position, head_size):
    half_size = head_size // 2
    frequency = jnp.exp(
        jnp.arange(half_size, dtype=jnp.float32) * (-2.0 * math.log(ROPE_BASE) / head_size)
    )
    angles = position.astype(jnp.float32)[:, None] * frequency[None, :]
    cosines = jnp.cos(angles)
    sines = jnp.sin(angles)
    front_half = head_values[..., :half_size]
    back_half = head_values[..., half_size:]
    return jnp.concatenate(
        [front_half * cosines - back_half * sines, back_half * cosines + front_half * sines],
        axis=-1,
    )


def head_attention(queries, keys_rot, values_h, segment, head_size):
    scores = lax.dot_general(
        queries, keys_rot, (((1,), (1,)), ((), ())), preferred_element_type=jnp.float32
    )
    scores = scores * (1.0 / math.sqrt(head_size))
    key_rows = jnp.arange(keys_rot.shape[0], dtype=jnp.int32)
    query_segment = segment
    allowed = (query_segment[:, None] == segment[None, :]) & (
        key_rows[None, :] <= key_rows[:, None]
    )
    scores = jnp.where(allowed, scores, -1e30)
    row_max = jnp.max(scores, axis=1, keepdims=True)
    weights = jnp.exp(scores - row_max)
    weights = weights / jnp.sum(weights, axis=1, keepdims=True)
    probabilities = weights.astype(jnp.bfloat16)
    return jnp.dot(probabilities, values_h, preferred_element_type=jnp.float32).astype(jnp.bfloat16)


def rms_scale(values_in, gain):
    return (
        values_in
        * lax.rsqrt(jnp.mean(values_in * values_in, axis=-1, keepdims=True) + NORM_EPSILON)
        * gain
    )


def per_device_general(
    tokens,
    lengths,
    query_gain,
    key_gain,
    attn_post_gain,
    mlp_post_gain,
    query_weight,
    key_weight,
    value_weight,
    output_weight,
    gate_weight,
    up_weight,
    down_weight,
):
    features = tokens.shape[1]
    shards = lax.axis_size("mp")
    my_index = lax.axis_index("mp")
    col_width = features // shards
    tok_rows = tokens.shape[0]
    group_rows = tok_rows * shards
    halves = col_width < HEAD_DIM
    stack_attn = jnp.stack([query_weight, key_weight, value_weight]).astype(jnp.bfloat16)
    stack_mlp = jnp.stack([gate_weight, up_weight]).astype(jnp.bfloat16)
    down_piece = down_weight.astype(jnp.bfloat16)[None]
    output_piece = output_weight.astype(jnp.bfloat16)[None]
    attn_rows, mlp_rows, down_rows, output_rows = (
        lax.all_gather(stack_attn, "group", axis=1, tiled=True),
        lax.all_gather(stack_mlp, "group", axis=1, tiled=True),
        lax.all_gather(down_piece, "group", axis=1, tiled=True),
        lax.all_gather(output_piece, "group", axis=1, tiled=True),
    )
    attn_block, mlp_block = (
        lax.all_to_all(attn_rows, "mp", split_axis=2, concat_axis=1, tiled=True),
        lax.all_to_all(mlp_rows, "mp", split_axis=2, concat_axis=1, tiled=True),
    )
    down_block = down_rows[0]
    output_block = output_rows[0]
    parity = my_index % 2
    if halves:
        partner = partner_2(attn_block, "mp", 0)
        attn_block = jnp.where(
            parity == 0,
            jnp.concatenate([attn_block, partner], axis=2),
            jnp.concatenate([partner, attn_block], axis=2),
        )
    head_cols = attn_block.shape[2]
    col_start = my_index * col_width // HEAD_DIM * HEAD_DIM
    share_part = col_width / head_cols
    projected = jnp.einsum(
        "td,kdc->ktc",
        lax.all_gather(tokens, "mp", axis=0, tiled=True),
        attn_block,
        preferred_element_type=jnp.float32,
    )
    query_sq = jnp.sum(projected[0] * projected[0], axis=1) * share_part
    key_sq = jnp.sum(projected[1] * projected[1], axis=1) * share_part
    query_total, key_total = lax.psum((query_sq, key_sq), "mp")
    query_part = lax.dynamic_slice_in_dim(query_gain, col_start, head_cols)
    key_part = lax.dynamic_slice_in_dim(key_gain, col_start, head_cols)
    q_normed = projected[0] * lax.rsqrt(query_total / features + NORM_EPSILON)[:, None] * query_part
    k_normed = projected[1] * lax.rsqrt(key_total / features + NORM_EPSILON)[:, None] * key_part
    segment, position = token_layout(lengths[0], group_rows)
    local_heads = head_cols // HEAD_DIM

    def heads_first(flat):
        return flat.reshape(group_rows, local_heads, HEAD_DIM).transpose(1, 0, 2)

    queries = rotary(heads_first(q_normed), position, HEAD_DIM).astype(jnp.bfloat16)
    keys_rot = rotary(heads_first(k_normed), position, HEAD_DIM).astype(jnp.bfloat16)
    values_h = heads_first(projected[2].astype(jnp.bfloat16))

    def per_head(triple):
        return head_attention(triple[0], triple[1], triple[2], segment, HEAD_DIM)

    attended = lax.map(per_head, (queries, keys_rot, values_h))
    attended = attended.transpose(1, 0, 2).reshape(group_rows, head_cols)
    if halves:
        attended = lax.dynamic_slice_in_dim(attended, parity * col_width, col_width, 1)
    rows_part = attended
    attn_out = lax.psum_scatter(
        jnp.dot(rows_part, output_block, preferred_element_type=jnp.float32).astype(jnp.bfloat16),
        "mp",
        scatter_dimension=0,
        tiled=True,
    ).astype(jnp.float32)
    hidden = (tokens.astype(jnp.float32) + rms_scale(attn_out, attn_post_gain)).astype(jnp.bfloat16)
    hidden_width = mlp_block.shape[2]
    mlp_weights = jnp.concatenate([mlp_block[0], mlp_block[1]], axis=1)
    both_proj = jnp.dot(
        lax.all_gather(hidden, "mp", axis=0, tiled=True),
        mlp_weights,
        preferred_element_type=jnp.float32,
    )
    activated = (jax.nn.silu(both_proj[:, :hidden_width]) * both_proj[:, hidden_width:]).astype(
        jnp.bfloat16
    )
    rows_part = activated
    mlp_out = lax.psum_scatter(
        jnp.dot(rows_part, down_block, preferred_element_type=jnp.float32).astype(jnp.bfloat16),
        "mp",
        scatter_dimension=0,
        tiled=True,
    ).astype(jnp.float32)
    return (hidden.astype(jnp.float32) + rms_scale(mlp_out, mlp_post_gain)).astype(jnp.bfloat16)


def over_mp(block, lines, step):
    count = 2 * lines
    return lax.ppermute(block, "mp", [(i, (i + 2 * step) % count) for i in range(count)])


def swap_x(block):
    return lax.ppermute(block, "mp", [(i, i ^ 1) for i in range(lax.axis_size("mp"))])


def swap_y(block):
    return lax.ppermute(block, "group", [(i, i ^ 2) for i in range(lax.axis_size("group"))])


def swap_core(block):
    return lax.ppermute(block, "group", [(i, i ^ 1) for i in range(lax.axis_size("group"))])


def swap_home(block, lines, step):
    shards = 2 * lines
    route = []
    for group in range(lax.axis_size("group")):
        for index in range(shards):
            apart = index % 2 ^ group % 2
            to = ((index + 2 * step) % shards) ^ apart
            if step or apart:
                route.append((group * shards + index, (group ^ apart) * shards + to))
    return lax.ppermute(block, ("group", "mp"), route)


def together(*arrays):
    return lax.optimization_barrier(arrays)


def put(buffer, block, *place):
    shape = (1,) * len(place) + block.shape
    rest = (0,) * (buffer.ndim - len(place))
    return lax.dynamic_update_slice(buffer, block.reshape(shape), tuple(place) + rest)


def pick(buffer, index):
    return lax.dynamic_index_in_dim(buffer, index, 0, keepdims=False)


def first_hop(piece):
    return swap_x(piece), swap_y(piece)


def second_hop(at_x, at_y):
    split = at_x.shape[0] // 2
    return swap_y(at_x[:split]), swap_x(at_y[split:])


def four_pieces(whole, piece, at_x, at_y, far_low, far_high, x, y, part):
    def write(block, column, row, half=None):
        at = 0 if half is None else half
        block = block.reshape((1, -1) + whole.shape[2:3] + (1,) + whole.shape[4:])
        place = (2 * column + row, at, 0, part) + (0,) * (whole.ndim - 4)
        return lax.dynamic_update_slice(whole, block, place)

    whole = write(piece, x, y)
    whole = write(at_x, 1 - x, y)
    whole = write(at_y, x, 1 - y)
    whole = write(far_low, 1 - x, 1 - y, 0)
    return write(far_high, 1 - x, 1 - y, 1)


def to_lines(parts, lines, z):
    return [over_mp(pick(parts, (z + step) % lines), lines, step) for step in range(1, lines)]


def both_cores(parts, arrived, lines, z, core):
    held = jnp.zeros(parts.shape, parts.dtype)
    held = put(held, pick(parts, z), z)
    for step, block in enumerate(arrived, 1):
        held = put(held, block, (z - step) % lines)
    return to_both_cores(held, core)


def to_both_cores(held, core):
    held = held.transpose(1, 0, 2, 3)
    other = swap_core(pick(held, 1 - core))
    mine = pick(held, core)
    both = jnp.stack([jnp.where(core == 0, mine, other), jnp.where(core == 0, other, mine)], axis=1)
    return both.reshape((-1,) + both.shape[2:])


def per_device_lines(
    tokens,
    lengths,
    query_gain,
    key_gain,
    attn_post_gain,
    mlp_post_gain,
    query_weight,
    key_weight,
    value_weight,
    output_weight,
    gate_weight,
    up_weight,
    down_weight,
):
    bf16, f32 = jnp.bfloat16, jnp.float32
    features = tokens.shape[1]
    shards = lax.axis_size("mp")
    lines = shards // 2
    index = lax.axis_index("mp")
    z, x = index // 2, index % 2
    group = lax.axis_index("group")
    y, core = group // 2, group % 2
    tok_rows = tokens.shape[0]
    chip_rows = 2 * tok_rows
    group_rows = shards * tok_rows
    home = x == core

    z_cols = features // lines
    head_cols = z_cols // 2
    run = features // shards // 2

    def server_order(rows):
        parts = rows.reshape(rows.shape[:-1] + (lines, 4, run))
        return jnp.swapaxes(parts, -3, -2).reshape(rows.shape)

    def given_order(rows):
        parts = rows.reshape(rows.shape[:-1] + (4, lines, run))
        return jnp.swapaxes(parts, -3, -2).reshape(rows.shape)

    def by_owner(weights, runs):
        parts = [w.astype(bf16).reshape(w.shape[0], lines, runs, 2, -1) for w in weights]
        parts = jnp.stack(parts, axis=2).transpose(1, 4, 0, 2, 3, 5)
        return parts.reshape(lines, 2, weights[0].shape[0], -1)

    own = jnp.concatenate([server_order(tokens), server_order(output_weight.astype(bf16))], axis=0)
    attn_parts = by_owner((query_weight, key_weight, value_weight), 1)
    own, attn_parts, down_own = together(own, attn_parts, down_weight)
    sets = [[2 * a + b for a in range(lines)] for b in range(2)]
    attn_held = lax.all_to_all(
        attn_parts, "mp", split_axis=0, concat_axis=0, axis_index_groups=sets, tiled=True
    )
    ring_1 = swap_home(own, lines, 1)
    moved = swap_home(own, lines, 0)
    down_own = down_own.astype(bf16)
    down_near = first_hop(down_own)
    own, ring_1, moved, down_own, attn_held, *down_near = together(
        own, ring_1, moved, down_own, attn_held, *down_near
    )

    ring = [jnp.where(home, own, moved), ring_1]
    if lines > 2:
        ring.append(over_mp(ring[-1], lines, 1))
    attn_piece = to_both_cores(attn_held, core)
    attn_near = first_hop(attn_piece)
    down_far = second_hop(*down_near)
    gate_up = by_owner((gate_weight, up_weight), 4)
    rows = jnp.zeros((lines, 2) + tokens.shape, bf16)

    def place(rows, step, held, at_core):
        return put(rows, held[:tok_rows], (z - step) % lines, at_core)

    rows = place(place(rows, 0, ring[0], core), 1, ring[1], core)
    ring[0], ring[-1], attn_piece, rows, gate_up, *rest = together(
        ring[0], ring[-1], attn_piece, rows, gate_up, *attn_near, *down_far
    )
    attn_near, down_far = rest[:2], rest[2:]

    attn_far = second_hop(*attn_near)
    for step in range(3, lines):
        ring.append(over_mp(ring[-1], lines, 1))
    for step in range(2, lines - 1):
        rows = place(rows, step, ring[step], core)
    for step in range(lines - 1):
        rows = place(rows, step, swap_core(ring[step]), 1 - core)
    prompt_lens = jnp.where(home, lengths, swap_core(lengths))[0]
    attn_weights = jnp.zeros((4, 2, lines, 1) + attn_piece.shape[1:], bf16)
    attn_weights = four_pieces(attn_weights, attn_piece, *attn_near, *attn_far, x, y, 0)
    down_block = jnp.zeros((4, 2, down_own.shape[0] // 2, 1, features), bf16)
    down_block = four_pieces(down_block, down_own, *down_near, *down_far, x, y, 0)
    gate_up, attn_weights, down_block, rows, ring[-1], prompt_lens = together(
        gate_up, attn_weights, down_block, rows, ring[-1], prompt_lens
    )
    rows_half = gate_up.shape[2] // 2
    halves = [gate_up[:, :, :rows_half], gate_up[:, :, rows_half:]]
    arrived_1 = to_lines(halves[0], lines, z)
    last = lines - 1
    rows = place(rows, last, ring[last], core)
    rows = place(rows, last, swap_core(ring[last]), 1 - core)
    block = ring[0][:tok_rows]
    out_piece = jnp.stack([held[tok_rows:] for held in ring])
    out_near = first_hop(out_piece)

    rows = rows.reshape(group_rows, features)
    attn_weights = attn_weights.reshape(features, -1)
    projected = jnp.dot(rows, attn_weights, preferred_element_type=f32)
    q_raw = projected[:, :head_cols]
    k_raw = projected[:, head_cols : 2 * head_cols]
    squares = jnp.stack([jnp.sum(q_raw * q_raw, axis=1), jnp.sum(k_raw * k_raw, axis=1)])
    squares = squares + swap_core(squares)
    total = squares
    for step in range(1, lines):
        total = total + over_mp(squares, lines, step)
    col_start = z * z_cols + core * head_cols
    query_part = lax.dynamic_slice_in_dim(query_gain, col_start, head_cols)
    key_part = lax.dynamic_slice_in_dim(key_gain, col_start, head_cols)
    total, late_half, out_piece, *rest = together(
        total, halves[1], out_piece, *out_near, *arrived_1
    )
    out_near, arrived_1 = rest[:2], rest[2:]
    piece_1 = both_cores(halves[0], arrived_1, lines, z, core)
    arrived_2 = to_lines(late_half, lines, z)
    out_far = second_hop(*out_near)

    q_normed = q_raw * lax.rsqrt(total[0] / features + NORM_EPSILON)[:, None] * query_part
    k_normed = k_raw * lax.rsqrt(total[1] / features + NORM_EPSILON)[:, None] * key_part
    segment, position = token_layout(prompt_lens, group_rows)
    local_heads = head_cols // HEAD_DIM

    def heads_first(flat):
        return flat.reshape(group_rows, local_heads, HEAD_DIM).transpose(1, 0, 2)

    queries = rotary(heads_first(q_normed), position, HEAD_DIM).astype(bf16)
    keys_rot = rotary(heads_first(k_normed), position, HEAD_DIM).astype(bf16)
    values_h = heads_first(projected[:, 2 * head_cols :].astype(bf16))
    attended = jnp.concatenate(
        [
            head_attention(queries[h], keys_rot[h], values_h[h], segment, HEAD_DIM)
            for h in range(local_heads)
        ],
        axis=1,
    )

    attended = attended.reshape(lines, chip_rows, head_cols)
    attended, out_piece, piece_1, *rest = together(
        attended, out_piece, piece_1, *out_near, *out_far, *arrived_2
    )
    out_near, out_far, arrived_2 = rest[:2], rest[2:4], rest[4:]
    both = jnp.concatenate([pick(attended, z)] + to_lines(attended, lines, z), axis=1)
    near_1 = first_hop(piece_1)
    out_weights = jnp.zeros((lines, 2, 2) + out_piece.shape[1:], bf16)
    split = lines // 2
    for held, row, column, at in (
        (out_piece, y, x, 0),
        (out_near[0], y, 1 - x, 0),
        (out_near[1], 1 - y, x, 0),
        (out_far[0], 1 - y, 1 - x, 0),
        (out_far[1], 1 - y, 1 - x, split),
    ):
        out_weights = lax.dynamic_update_slice(
            out_weights, held[:, None, None], (at, row, column, 0, 0)
        )
    out_weights = out_weights.reshape(-1, features)
    partial = jnp.dot(both, out_weights, preferred_element_type=f32)
    partial = partial.reshape(2, tok_rows, features)
    attn_out = pick(partial, core) + swap_core(pick(partial, 1 - core).astype(bf16)).astype(f32)
    hidden = block.astype(f32) + rms_scale(attn_out, server_order(attn_post_gain))
    hidden = hidden.astype(bf16)

    ring = [hidden]
    for step in range(1, lines):
        ring.append(over_mp(ring[-1], lines, 1))
    piece_2 = both_cores(late_half, arrived_2, lines, z, core)
    near_2 = first_hop(piece_2)
    ring[1], piece_1, piece_2, *rest = together(ring[1], piece_1, piece_2, *near_1, *near_2)
    near_1, near_2 = rest[:2], rest[2:]
    for step in range(2, lines):
        ring[step] = over_mp(ring[step - 1], lines, 1)
    far_1 = second_hop(*near_1)
    far_2 = second_hop(*near_2)
    mlp_weights = jnp.zeros((4, 2, lines, 2) + piece_1.shape[1:], bf16)
    mlp_weights = four_pieces(mlp_weights, piece_1, *near_1, *far_1, x, y, 0)
    mlp_weights = four_pieces(mlp_weights, piece_2, *near_2, *far_2, x, y, 1)
    mlp_weights = mlp_weights.reshape(features, -1)
    down_block = down_block.reshape(-1, features)
    units = down_block.shape[0]

    def feed_forward(own):
        rows = jnp.concatenate([own, swap_core(own)], axis=0)
        both_proj = jnp.dot(rows, mlp_weights, preferred_element_type=f32)
        activated = (jax.nn.silu(both_proj[:, :units]) * both_proj[:, units:]).astype(bf16)
        out = jnp.dot(activated, down_block, preferred_element_type=f32)
        return out[:tok_rows] + swap_core(out[tok_rows:].astype(bf16)).astype(f32)

    total_out = None
    for step in range(1, lines):
        part = feed_forward(ring[step])
        if total_out is not None:
            part = part + total_out.astype(f32)
        part = part.astype(bf16)
        total_out = over_mp(part, lines, 1) if step + 1 < lines else swap_home(part, lines, 1)
    own_out = feed_forward(hidden).astype(bf16)
    own_out = jnp.where(home, own_out, swap_home(own_out, lines, 0)).astype(f32)
    hidden = given_order(hidden)
    hidden = jnp.where(home, hidden, swap_home(hidden, lines, 0)).astype(f32)
    mlp_out = own_out + total_out.astype(f32)
    return (hidden + rms_scale(mlp_out, mlp_post_gain)).astype(bf16)


def per_device(*arrays):
    heads = arrays[0].shape[1] // HEAD_DIM
    shards = lax.axis_size("mp")
    if lax.axis_size("group") == 4 and shards % 4 == 0 and heads % shards == 0:
        return per_device_lines(*arrays)
    return per_device_general(*arrays)


def solution(mesh):
    return jax.shard_map(
        per_device,
        mesh=mesh,
        in_specs=(
            P(("group", "mp"), None),
            P("group", None),
            P(),
            P(),
            P(),
            P(),
            P(("mp", "group"), None),
            P(("mp", "group"), None),
            P(("mp", "group"), None),
            P(("mp", "group"), None),
            P(("mp", "group"), None),
            P(("mp", "group"), None),
            P(("mp", "group"), None),
        ),
        out_specs=P(("group", "mp"), None),
        check_vma=False,
    )
```

```python
import math

import jax
import jax.numpy as jnp
from jax import lax
from jax.experimental import pallas as pl
from jax.experimental.pallas import tpu as pltpu
from jax.sharding import PartitionSpec as P

HEAD_DIM = 128
LONGEST = 512


NORM_EPSILON = 1e-06
ROPE_BASE = 500000.0


def partner_2(block, axis, apart):
    count = lax.axis_size(axis)
    route = []
    for low in range(count):
        high = low | 1 << apart
        if high != low and high < count:
            route += [(low, high), (high, low)]
    return lax.ppermute(block, axis, route)


def token_layout(prompt_lens, row_count):
    seg_ends = jnp.cumsum(prompt_lens)
    starts = seg_ends - prompt_lens
    indices = jnp.arange(row_count, dtype=jnp.int32)
    segment = jnp.sum((indices[:, None] >= seg_ends[None, :]).astype(jnp.int32), axis=1)
    member = segment[:, None] == jnp.arange(prompt_lens.shape[0], dtype=jnp.int32)[None, :]
    opening = jnp.sum(jnp.where(member, starts[None, :], 0), axis=1)
    return (segment, indices - opening)


def rotary(head_values, position, head_size):
    half_size = head_size // 2
    frequency = jnp.exp(
        jnp.arange(half_size, dtype=jnp.float32) * (-2.0 * math.log(ROPE_BASE) / head_size)
    )
    angles = position.astype(jnp.float32)[:, None] * frequency[None, :]
    cosines = jnp.cos(angles)
    sines = jnp.sin(angles)
    front_half = head_values[..., :half_size]
    back_half = head_values[..., half_size:]
    return jnp.concatenate(
        [front_half * cosines - back_half * sines, back_half * cosines + front_half * sines],
        axis=-1,
    )


def head_attention(queries, keys_rot, values_h, segment, head_size):
    scores = lax.dot_general(
        queries, keys_rot, (((1,), (1,)), ((), ())), preferred_element_type=jnp.float32
    )
    scores = scores * (1.0 / math.sqrt(head_size))
    key_rows = jnp.arange(keys_rot.shape[0], dtype=jnp.int32)
    query_segment = segment
    allowed = (query_segment[:, None] == segment[None, :]) & (
        key_rows[None, :] <= key_rows[:, None]
    )
    scores = jnp.where(allowed, scores, -1e30)
    row_max = jnp.max(scores, axis=1, keepdims=True)
    weights = jnp.exp(scores - row_max)
    weights = weights / jnp.sum(weights, axis=1, keepdims=True)
    probabilities = weights.astype(jnp.bfloat16)
    return jnp.dot(probabilities, values_h, preferred_element_type=jnp.float32).astype(jnp.bfloat16)


def rms_scale(values_in, gain):
    return (
        values_in
        * lax.rsqrt(jnp.mean(values_in * values_in, axis=-1, keepdims=True) + NORM_EPSILON)
        * gain
    )


def per_device_general(
    tokens,
    lengths,
    query_gain,
    key_gain,
    attn_post_gain,
    mlp_post_gain,
    query_weight,
    key_weight,
    value_weight,
    output_weight,
    gate_weight,
    up_weight,
    down_weight,
):
    features = tokens.shape[1]
    shards = lax.axis_size("mp")
    my_index = lax.axis_index("mp")
    col_width = features // shards
    tok_rows = tokens.shape[0]
    group_rows = tok_rows * shards
    halves = col_width < HEAD_DIM
    stack_attn = jnp.stack([query_weight, key_weight, value_weight]).astype(jnp.bfloat16)
    stack_mlp = jnp.stack([gate_weight, up_weight]).astype(jnp.bfloat16)
    down_piece = down_weight.astype(jnp.bfloat16)[None]
    output_piece = output_weight.astype(jnp.bfloat16)[None]
    attn_rows, mlp_rows, down_rows, output_rows = (
        lax.all_gather(stack_attn, "group", axis=1, tiled=True),
        lax.all_gather(stack_mlp, "group", axis=1, tiled=True),
        lax.all_gather(down_piece, "group", axis=1, tiled=True),
        lax.all_gather(output_piece, "group", axis=1, tiled=True),
    )
    attn_block, mlp_block = (
        lax.all_to_all(attn_rows, "mp", split_axis=2, concat_axis=1, tiled=True),
        lax.all_to_all(mlp_rows, "mp", split_axis=2, concat_axis=1, tiled=True),
    )
    down_block = down_rows[0]
    output_block = output_rows[0]
    parity = my_index % 2
    if halves:
        partner = partner_2(attn_block, "mp", 0)
        attn_block = jnp.where(
            parity == 0,
            jnp.concatenate([attn_block, partner], axis=2),
            jnp.concatenate([partner, attn_block], axis=2),
        )
    head_cols = attn_block.shape[2]
    col_start = my_index * col_width // HEAD_DIM * HEAD_DIM
    share_part = col_width / head_cols
    projected = jnp.einsum(
        "td,kdc->ktc",
        lax.all_gather(tokens, "mp", axis=0, tiled=True),
        attn_block,
        preferred_element_type=jnp.float32,
    )
    query_sq = jnp.sum(projected[0] * projected[0], axis=1) * share_part
    key_sq = jnp.sum(projected[1] * projected[1], axis=1) * share_part
    query_total, key_total = lax.psum((query_sq, key_sq), "mp")
    query_part = lax.dynamic_slice_in_dim(query_gain, col_start, head_cols)
    key_part = lax.dynamic_slice_in_dim(key_gain, col_start, head_cols)
    q_normed = projected[0] * lax.rsqrt(query_total / features + NORM_EPSILON)[:, None] * query_part
    k_normed = projected[1] * lax.rsqrt(key_total / features + NORM_EPSILON)[:, None] * key_part
    segment, position = token_layout(lengths[0], group_rows)
    local_heads = head_cols // HEAD_DIM

    def heads_first(flat):
        return flat.reshape(group_rows, local_heads, HEAD_DIM).transpose(1, 0, 2)

    queries = rotary(heads_first(q_normed), position, HEAD_DIM).astype(jnp.bfloat16)
    keys_rot = rotary(heads_first(k_normed), position, HEAD_DIM).astype(jnp.bfloat16)
    values_h = heads_first(projected[2].astype(jnp.bfloat16))

    def per_head(triple):
        return head_attention(triple[0], triple[1], triple[2], segment, HEAD_DIM)

    attended = lax.map(per_head, (queries, keys_rot, values_h))
    attended = attended.transpose(1, 0, 2).reshape(group_rows, head_cols)
    if halves:
        attended = lax.dynamic_slice_in_dim(attended, parity * col_width, col_width, 1)
    rows_part = attended
    attn_out = lax.psum_scatter(
        jnp.dot(rows_part, output_block, preferred_element_type=jnp.float32).astype(jnp.bfloat16),
        "mp",
        scatter_dimension=0,
        tiled=True,
    ).astype(jnp.float32)
    hidden = (tokens.astype(jnp.float32) + rms_scale(attn_out, attn_post_gain)).astype(jnp.bfloat16)
    hidden_width = mlp_block.shape[2]
    mlp_weights = jnp.concatenate([mlp_block[0], mlp_block[1]], axis=1)
    both_proj = jnp.dot(
        lax.all_gather(hidden, "mp", axis=0, tiled=True),
        mlp_weights,
        preferred_element_type=jnp.float32,
    )
    activated = (jax.nn.silu(both_proj[:, :hidden_width]) * both_proj[:, hidden_width:]).astype(
        jnp.bfloat16
    )
    rows_part = activated
    mlp_out = lax.psum_scatter(
        jnp.dot(rows_part, down_block, preferred_element_type=jnp.float32).astype(jnp.bfloat16),
        "mp",
        scatter_dimension=0,
        tiled=True,
    ).astype(jnp.float32)
    return (hidden.astype(jnp.float32) + rms_scale(mlp_out, mlp_post_gain)).astype(jnp.bfloat16)


def over_mp(block, lines, step):
    count = 2 * lines
    return lax.ppermute(block, "mp", [(i, (i + 2 * step) % count) for i in range(count)])


def swap_x(block):
    return lax.ppermute(block, "mp", [(i, i ^ 1) for i in range(lax.axis_size("mp"))])


def swap_y(block):
    return lax.ppermute(block, "group", [(i, i ^ 2) for i in range(lax.axis_size("group"))])


def swap_core(block):
    return lax.ppermute(block, "group", [(i, i ^ 1) for i in range(lax.axis_size("group"))])


def swap_home(block, lines, step):
    shards = 2 * lines
    route = []
    for group in range(lax.axis_size("group")):
        for index in range(shards):
            apart = index % 2 ^ group % 2
            to = ((index + 2 * step) % shards) ^ apart
            if step or apart:
                route.append((group * shards + index, (group ^ apart) * shards + to))
    return lax.ppermute(block, ("group", "mp"), route)


def together(*arrays):
    return lax.optimization_barrier(arrays)


def put(buffer, block, *place):
    shape = (1,) * len(place) + block.shape
    rest = (0,) * (buffer.ndim - len(place))
    return lax.dynamic_update_slice(buffer, block.reshape(shape), tuple(place) + rest)


def pick(buffer, index):
    return lax.dynamic_index_in_dim(buffer, index, 0, keepdims=False)


def first_hop(piece):
    return swap_x(piece), swap_y(piece)


def second_hop(at_x, at_y):
    split = at_x.shape[0] // 2
    return swap_y(at_x[:split]), swap_x(at_y[split:])


def four_pieces(whole, piece, at_x, at_y, far_low, far_high, x, y, part):
    def write(block, column, row, half=None):
        at = 0 if half is None else half
        block = block.reshape((1, -1) + whole.shape[2:3] + (1,) + whole.shape[4:])
        place = (2 * column + row, at, 0, part) + (0,) * (whole.ndim - 4)
        return lax.dynamic_update_slice(whole, block, place)

    whole = write(piece, x, y)
    whole = write(at_x, 1 - x, y)
    whole = write(at_y, x, 1 - y)
    whole = write(far_low, 1 - x, 1 - y, 0)
    return write(far_high, 1 - x, 1 - y, 1)


def along_lines(parts, lines):
    sets = [[2 * a + b for a in range(lines)] for b in range(2)]
    return lax.all_to_all(
        parts, "mp", split_axis=0, concat_axis=0, axis_index_groups=sets, tiled=True
    )


def to_lines(parts, lines, z):
    return [over_mp(pick(parts, (z + step) % lines), lines, step) for step in range(1, lines)]


def to_both_cores(held, core):
    held = held.transpose(1, 0, 2, 3)
    other = swap_core(pick(held, 1 - core))
    mine = pick(held, core)
    both = jnp.stack([jnp.where(core == 0, mine, other), jnp.where(core == 0, other, mine)], axis=1)
    return both.reshape((-1,) + both.shape[2:])


def product_kernel(rows_ref, weights_ref, out_ref):
    out_ref[...] = jnp.dot(rows_ref[...], weights_ref[...], preferred_element_type=jnp.float32)


def product(rows, weights):
    count, depth = rows.shape
    width = weights.shape[1]
    tile = math.gcd(count, 256)
    return pl.pallas_call(
        product_kernel,
        grid=(count // tile,),
        in_specs=[
            pl.BlockSpec((tile, depth), lambda i: (i, 0)),
            pl.BlockSpec((depth, width), lambda i: (0, 0)),
        ],
        out_specs=pl.BlockSpec((tile, width), lambda i: (i, 0)),
        out_shape=jax.ShapeDtypeStruct((count, width), jnp.float32),
        compiler_params=pltpu.CompilerParams(vmem_limit_bytes=32 * 2**20),
        cost_estimate=pl.CostEstimate(flops=1, bytes_accessed=1, transcendentals=0),
    )(rows, weights)


def attention_kernel(
    q_ref, k_ref, v_ref, q_scale, k_scale, q_gain, k_gain, cos_ref, sin_ref, seg_ref, ends_ref, out_ref
):
    count, size = q_ref.shape
    tile = math.gcd(count, 256)

    def ready(ref, scale, gain):
        normed = ref[...] * scale[...] * gain[...]
        turned = normed * cos_ref[...] + pltpu.roll(normed, size // 2, 1) * sin_ref[...]
        return turned.astype(jnp.bfloat16)

    queries = ready(q_ref, q_scale, q_gain)
    keys = ready(k_ref, k_scale, k_gain)
    values = v_ref[...].astype(jnp.bfloat16)
    for start in range(0, count, tile):
        low = max(0, start - -(-LONGEST // tile) * tile)
        stop = start + tile
        scores = lax.dot_general(
            queries[start:stop],
            keys[low:stop],
            (((1,), (1,)), ((), ())),
            preferred_element_type=jnp.float32,
        )
        scores = scores * (1.0 / math.sqrt(size))
        query_rows = start + lax.broadcasted_iota(jnp.int32, scores.shape, 0)
        key_rows = low + lax.broadcasted_iota(jnp.int32, scores.shape, 1)
        allowed = (seg_ref[start:stop, :] == ends_ref[:, low:stop]) & (key_rows <= query_rows)
        scores = jnp.where(allowed, scores, -1e30)
        weights = jnp.exp(scores - jnp.max(scores, axis=1, keepdims=True))
        weights = weights / jnp.sum(weights, axis=1, keepdims=True)
        out_ref[start:stop, :] = jnp.dot(
            weights.astype(jnp.bfloat16), values[low:stop], preferred_element_type=jnp.float32
        ).astype(jnp.bfloat16)


def attention(projected, q_scale, k_scale, q_gain, k_gain, segment, position):
    count = projected.shape[0]
    heads = projected.shape[1] // 3 // HEAD_DIM
    half = HEAD_DIM // 2
    frequency = jnp.exp(
        jnp.arange(half, dtype=jnp.float32) * (-2.0 * math.log(ROPE_BASE) / HEAD_DIM)
    )
    angles = position.astype(jnp.float32)[:, None] * frequency[None, :]
    cosines, sines = jnp.cos(angles), jnp.sin(angles)
    cosines = jnp.concatenate([cosines, cosines], axis=1)
    sines = jnp.concatenate([-sines, sines], axis=1)

    def head(first):
        return pl.BlockSpec((count, HEAD_DIM), lambda h: (0, first + h))

    def whole(shape):
        return pl.BlockSpec(shape, lambda h: (0, 0))

    return pl.pallas_call(
        attention_kernel,
        grid=(heads,),
        in_specs=[
            head(0),
            head(heads),
            head(2 * heads),
            whole((count, 1)),
            whole((count, 1)),
            pl.BlockSpec((1, HEAD_DIM), lambda h: (0, h)),
            pl.BlockSpec((1, HEAD_DIM), lambda h: (0, h)),
            whole((count, HEAD_DIM)),
            whole((count, HEAD_DIM)),
            whole((count, 1)),
            whole((1, count)),
        ],
        out_specs=head(0),
        out_shape=jax.ShapeDtypeStruct((count, heads * HEAD_DIM), jnp.bfloat16),
        compiler_params=pltpu.CompilerParams(vmem_limit_bytes=48 * 2**20),
        cost_estimate=pl.CostEstimate(flops=1, bytes_accessed=1, transcendentals=0),
    )(
        projected,
        projected,
        projected,
        q_scale[:, None],
        k_scale[:, None],
        q_gain[None],
        k_gain[None],
        cosines,
        sines,
        segment[:, None],
        segment[None],
    )


def per_device_lines(
    tokens,
    lengths,
    query_gain,
    key_gain,
    attn_post_gain,
    mlp_post_gain,
    query_weight,
    key_weight,
    value_weight,
    output_weight,
    gate_weight,
    up_weight,
    down_weight,
):
    bf16, f32 = jnp.bfloat16, jnp.float32
    features = tokens.shape[1]
    shards = lax.axis_size("mp")
    lines = shards // 2
    index = lax.axis_index("mp")
    z, x = index // 2, index % 2
    group = lax.axis_index("group")
    y, core = group // 2, group % 2
    tok_rows = tokens.shape[0]
    chip_rows = 2 * tok_rows
    group_rows = shards * tok_rows
    home = x == core

    z_cols = features // lines
    head_cols = z_cols // 2
    run = features // shards // 2

    def server_order(rows):
        parts = rows.reshape(rows.shape[:-1] + (lines, 4, run))
        return jnp.swapaxes(parts, -3, -2).reshape(rows.shape)

    def given_order(rows):
        parts = rows.reshape(rows.shape[:-1] + (4, lines, run))
        return jnp.swapaxes(parts, -3, -2).reshape(rows.shape)

    def by_owner(weights, runs):
        parts = [w.astype(bf16).reshape(w.shape[0], lines, runs, 2, -1) for w in weights]
        parts = jnp.stack(parts, axis=2).transpose(1, 4, 0, 2, 3, 5)
        return parts.reshape(lines, 2, weights[0].shape[0], -1)

    own = jnp.concatenate([server_order(tokens), server_order(output_weight.astype(bf16))], axis=0)
    attn_parts = by_owner((query_weight, key_weight, value_weight), 1)
    own, attn_parts, down_own = together(own, attn_parts, down_weight)
    attn_held = along_lines(attn_parts, lines)
    ring_1 = swap_home(own, lines, 1)
    moved = swap_home(own, lines, 0)
    down_own = down_own.astype(bf16)
    down_near = first_hop(down_own)
    gate_up = by_owner((gate_weight, up_weight), 4)
    own, ring_1, moved, down_own, attn_held, gate_up, *down_near = together(
        own, ring_1, moved, down_own, attn_held, gate_up, *down_near
    )
    gate_up_held = along_lines(gate_up, lines)

    ring = [jnp.where(home, own, moved), ring_1]
    if lines > 2:
        ring.append(over_mp(ring[-1], lines, 1))
    attn_piece = to_both_cores(attn_held, core)
    attn_near = first_hop(attn_piece)
    down_far = second_hop(*down_near)
    rows = jnp.zeros((lines, 2) + tokens.shape, bf16)

    def place(rows, step, held, at_core):
        return put(rows, held[:tok_rows], (z - step) % lines, at_core)

    rows = place(place(rows, 0, ring[0], core), 1, ring[1], core)
    ring[-1], gate_up_held = together(ring[-1], gate_up_held)

    attn_far = second_hop(*attn_near)
    for step in range(3, lines):
        ring.append(over_mp(ring[-1], lines, 1))
    for step in range(2, lines):
        rows = place(rows, step, ring[step], core)
    for step in range(lines):
        rows = place(rows, step, swap_core(ring[step]), 1 - core)
    prompt_lens = jnp.where(home, lengths, swap_core(lengths))[0]
    attn_weights = jnp.zeros((4, 2, lines, 1) + attn_piece.shape[1:], bf16)
    attn_weights = four_pieces(attn_weights, attn_piece, *attn_near, *attn_far, x, y, 0)
    down_block = jnp.zeros((4, 2, down_own.shape[0] // 2, 1, features), bf16)
    down_block = four_pieces(down_block, down_own, *down_near, *down_far, x, y, 0)
    piece = to_both_cores(gate_up_held, core)
    block = ring[0][:tok_rows]
    out_piece = jnp.stack([held[tok_rows:] for held in ring])
    out_near = first_hop(out_piece)

    rows, attn_weights, down_block, prompt_lens, piece = together(
        rows, attn_weights, down_block, prompt_lens, piece
    )
    rows = rows.reshape(group_rows, features)
    attn_weights = attn_weights.reshape(features, -1)
    projected = product(rows, attn_weights)
    q_raw = projected[:, :head_cols]
    k_raw = projected[:, head_cols : 2 * head_cols]
    squares = jnp.stack([jnp.sum(q_raw * q_raw, axis=1), jnp.sum(k_raw * k_raw, axis=1)])
    squares = squares + swap_core(squares)
    total = squares
    for step in range(1, lines):
        total = total + over_mp(squares, lines, step)
    col_start = z * z_cols + core * head_cols
    query_part = lax.dynamic_slice_in_dim(query_gain, col_start, head_cols)
    key_part = lax.dynamic_slice_in_dim(key_gain, col_start, head_cols)
    total, piece, out_piece, *out_near = together(total, piece, out_piece, *out_near)
    out_far = second_hop(*out_near)
    near = first_hop(piece)

    segment, position = token_layout(prompt_lens, group_rows)
    attended = attention(
        projected,
        lax.rsqrt(total[0] / features + NORM_EPSILON),
        lax.rsqrt(total[1] / features + NORM_EPSILON),
        query_part,
        key_part,
        segment,
        position,
    )

    attended, out_piece, *rest = together(attended, out_piece, *out_near, *out_far)
    out_near, out_far = rest[:2], rest[2:]
    attended = attended.reshape(lines, chip_rows, head_cols)
    both = jnp.concatenate([pick(attended, z)] + to_lines(attended, lines, z), axis=1)
    out_weights = jnp.zeros((lines, 2, 2) + out_piece.shape[1:], bf16)
    split = lines // 2
    for held, row, column, at in (
        (out_piece, y, x, 0),
        (out_near[0], y, 1 - x, 0),
        (out_near[1], 1 - y, x, 0),
        (out_far[0], 1 - y, 1 - x, 0),
        (out_far[1], 1 - y, 1 - x, split),
    ):
        out_weights = lax.dynamic_update_slice(
            out_weights, held[:, None, None], (at, row, column, 0, 0)
        )
    out_weights = out_weights.reshape(-1, features)
    partial = jnp.dot(both, out_weights, preferred_element_type=f32)
    partial = partial.reshape(2, tok_rows, features)
    attn_out = pick(partial, core) + swap_core(pick(partial, 1 - core).astype(bf16)).astype(f32)
    hidden = block.astype(f32) + rms_scale(attn_out, server_order(attn_post_gain))
    hidden = hidden.astype(bf16)

    ring = [hidden]
    for step in range(1, lines):
        ring.append(over_mp(ring[-1], lines, 1))
    far = second_hop(*near)
    mlp_weights = jnp.zeros((4, 2, lines, 1) + piece.shape[1:], bf16)
    mlp_weights = four_pieces(mlp_weights, piece, *near, *far, x, y, 0)
    mlp_weights = mlp_weights.reshape(features, -1)
    down_block = down_block.reshape(-1, features)
    units = down_block.shape[0]

    def feed_forward(own):
        rows = jnp.concatenate([own, swap_core(own)], axis=0)
        both_proj = jnp.dot(rows, mlp_weights, preferred_element_type=f32)
        activated = (jax.nn.silu(both_proj[:, :units]) * both_proj[:, units:]).astype(bf16)
        out = jnp.dot(activated, down_block, preferred_element_type=f32)
        return out[:tok_rows] + swap_core(out[tok_rows:].astype(bf16)).astype(f32)

    total_out = None
    for step in range(1, lines):
        part = feed_forward(ring[step])
        if total_out is not None:
            part = part + total_out.astype(f32)
        part = part.astype(bf16)
        total_out = over_mp(part, lines, 1) if step + 1 < lines else swap_home(part, lines, 1)
    own_out = feed_forward(hidden).astype(bf16)
    own_out = jnp.where(home, own_out, swap_home(own_out, lines, 0)).astype(f32)
    hidden = given_order(hidden)
    hidden = jnp.where(home, hidden, swap_home(hidden, lines, 0)).astype(f32)
    mlp_out = own_out + total_out.astype(f32)
    return (hidden + rms_scale(mlp_out, mlp_post_gain)).astype(bf16)


def per_device(*arrays):
    heads = arrays[0].shape[1] // HEAD_DIM
    shards = lax.axis_size("mp")
    if lax.axis_size("group") == 4 and shards % 4 == 0 and heads % shards == 0:
        return per_device_lines(*arrays)
    return per_device_general(*arrays)


def solution(mesh):
    return jax.shard_map(
        per_device,
        mesh=mesh,
        in_specs=(
            P(("group", "mp"), None),
            P("group", None),
            P(),
            P(),
            P(),
            P(),
            P(("mp", "group"), None),
            P(("mp", "group"), None),
            P(("mp", "group"), None),
            P(("mp", "group"), None),
            P(("mp", "group"), None),
            P(("mp", "group"), None),
            P(("mp", "group"), None),
        ),
        out_specs=P(("group", "mp"), None),
        check_vma=False,
    )
```

```python
import math

import jax
import jax.numpy as jnp
from jax import lax
from jax.experimental import pallas as pl
from jax.experimental.pallas import tpu as pltpu
from jax.sharding import PartitionSpec as P

HEAD_DIM = 128
LONGEST = 512


NORM_EPSILON = 1e-06
ROPE_BASE = 500000.0


def partner_2(block, axis, apart):
    count = lax.axis_size(axis)
    route = []
    for low in range(count):
        high = low | 1 << apart
        if high != low and high < count:
            route += [(low, high), (high, low)]
    return lax.ppermute(block, axis, route)


def token_layout(prompt_lens, row_count):
    seg_ends = jnp.cumsum(prompt_lens)
    starts = seg_ends - prompt_lens
    indices = jnp.arange(row_count, dtype=jnp.int32)
    segment = jnp.sum((indices[:, None] >= seg_ends[None, :]).astype(jnp.int32), axis=1)
    member = segment[:, None] == jnp.arange(prompt_lens.shape[0], dtype=jnp.int32)[None, :]
    opening = jnp.sum(jnp.where(member, starts[None, :], 0), axis=1)
    return (segment, indices - opening)


def rotary(head_values, position, head_size):
    half_size = head_size // 2
    frequency = jnp.exp(
        jnp.arange(half_size, dtype=jnp.float32) * (-2.0 * math.log(ROPE_BASE) / head_size)
    )
    angles = position.astype(jnp.float32)[:, None] * frequency[None, :]
    cosines = jnp.cos(angles)
    sines = jnp.sin(angles)
    front_half = head_values[..., :half_size]
    back_half = head_values[..., half_size:]
    return jnp.concatenate(
        [front_half * cosines - back_half * sines, back_half * cosines + front_half * sines],
        axis=-1,
    )


def head_attention(queries, keys_rot, values_h, segment, head_size):
    scores = lax.dot_general(
        queries, keys_rot, (((1,), (1,)), ((), ())), preferred_element_type=jnp.float32
    )
    scores = scores * (1.0 / math.sqrt(head_size))
    key_rows = jnp.arange(keys_rot.shape[0], dtype=jnp.int32)
    query_segment = segment
    allowed = (query_segment[:, None] == segment[None, :]) & (
        key_rows[None, :] <= key_rows[:, None]
    )
    scores = jnp.where(allowed, scores, -1e30)
    row_max = jnp.max(scores, axis=1, keepdims=True)
    weights = jnp.exp(scores - row_max)
    weights = weights / jnp.sum(weights, axis=1, keepdims=True)
    probabilities = weights.astype(jnp.bfloat16)
    return jnp.dot(probabilities, values_h, preferred_element_type=jnp.float32).astype(jnp.bfloat16)


def rms_scale(values_in, gain):
    return (
        values_in
        * lax.rsqrt(jnp.mean(values_in * values_in, axis=-1, keepdims=True) + NORM_EPSILON)
        * gain
    )


def per_device_general(
    tokens,
    lengths,
    query_gain,
    key_gain,
    attn_post_gain,
    mlp_post_gain,
    query_weight,
    key_weight,
    value_weight,
    output_weight,
    gate_weight,
    up_weight,
    down_weight,
):
    features = tokens.shape[1]
    shards = lax.axis_size("mp")
    my_index = lax.axis_index("mp")
    col_width = features // shards
    tok_rows = tokens.shape[0]
    group_rows = tok_rows * shards
    halves = col_width < HEAD_DIM
    stack_attn = jnp.stack([query_weight, key_weight, value_weight]).astype(jnp.bfloat16)
    stack_mlp = jnp.stack([gate_weight, up_weight]).astype(jnp.bfloat16)
    down_piece = down_weight.astype(jnp.bfloat16)[None]
    output_piece = output_weight.astype(jnp.bfloat16)[None]
    attn_rows, mlp_rows, down_rows, output_rows = (
        lax.all_gather(stack_attn, "group", axis=1, tiled=True),
        lax.all_gather(stack_mlp, "group", axis=1, tiled=True),
        lax.all_gather(down_piece, "group", axis=1, tiled=True),
        lax.all_gather(output_piece, "group", axis=1, tiled=True),
    )
    attn_block, mlp_block = (
        lax.all_to_all(attn_rows, "mp", split_axis=2, concat_axis=1, tiled=True),
        lax.all_to_all(mlp_rows, "mp", split_axis=2, concat_axis=1, tiled=True),
    )
    down_block = down_rows[0]
    output_block = output_rows[0]
    parity = my_index % 2
    if halves:
        partner = partner_2(attn_block, "mp", 0)
        attn_block = jnp.where(
            parity == 0,
            jnp.concatenate([attn_block, partner], axis=2),
            jnp.concatenate([partner, attn_block], axis=2),
        )
    head_cols = attn_block.shape[2]
    col_start = my_index * col_width // HEAD_DIM * HEAD_DIM
    share_part = col_width / head_cols
    projected = jnp.einsum(
        "td,kdc->ktc",
        lax.all_gather(tokens, "mp", axis=0, tiled=True),
        attn_block,
        preferred_element_type=jnp.float32,
    )
    query_sq = jnp.sum(projected[0] * projected[0], axis=1) * share_part
    key_sq = jnp.sum(projected[1] * projected[1], axis=1) * share_part
    query_total, key_total = lax.psum((query_sq, key_sq), "mp")
    query_part = lax.dynamic_slice_in_dim(query_gain, col_start, head_cols)
    key_part = lax.dynamic_slice_in_dim(key_gain, col_start, head_cols)
    q_normed = projected[0] * lax.rsqrt(query_total / features + NORM_EPSILON)[:, None] * query_part
    k_normed = projected[1] * lax.rsqrt(key_total / features + NORM_EPSILON)[:, None] * key_part
    segment, position = token_layout(lengths[0], group_rows)
    local_heads = head_cols // HEAD_DIM

    def heads_first(flat):
        return flat.reshape(group_rows, local_heads, HEAD_DIM).transpose(1, 0, 2)

    queries = rotary(heads_first(q_normed), position, HEAD_DIM).astype(jnp.bfloat16)
    keys_rot = rotary(heads_first(k_normed), position, HEAD_DIM).astype(jnp.bfloat16)
    values_h = heads_first(projected[2].astype(jnp.bfloat16))

    def per_head(triple):
        return head_attention(triple[0], triple[1], triple[2], segment, HEAD_DIM)

    attended = lax.map(per_head, (queries, keys_rot, values_h))
    attended = attended.transpose(1, 0, 2).reshape(group_rows, head_cols)
    if halves:
        attended = lax.dynamic_slice_in_dim(attended, parity * col_width, col_width, 1)
    rows_part = attended
    attn_out = lax.psum_scatter(
        jnp.dot(rows_part, output_block, preferred_element_type=jnp.float32).astype(jnp.bfloat16),
        "mp",
        scatter_dimension=0,
        tiled=True,
    ).astype(jnp.float32)
    hidden = (tokens.astype(jnp.float32) + rms_scale(attn_out, attn_post_gain)).astype(jnp.bfloat16)
    hidden_width = mlp_block.shape[2]
    mlp_weights = jnp.concatenate([mlp_block[0], mlp_block[1]], axis=1)
    both_proj = jnp.dot(
        lax.all_gather(hidden, "mp", axis=0, tiled=True),
        mlp_weights,
        preferred_element_type=jnp.float32,
    )
    activated = (jax.nn.silu(both_proj[:, :hidden_width]) * both_proj[:, hidden_width:]).astype(
        jnp.bfloat16
    )
    rows_part = activated
    mlp_out = lax.psum_scatter(
        jnp.dot(rows_part, down_block, preferred_element_type=jnp.float32).astype(jnp.bfloat16),
        "mp",
        scatter_dimension=0,
        tiled=True,
    ).astype(jnp.float32)
    return (hidden.astype(jnp.float32) + rms_scale(mlp_out, mlp_post_gain)).astype(jnp.bfloat16)


def over_mp(block, lines, step):
    count = 2 * lines
    return lax.ppermute(block, "mp", [(i, (i + 2 * step) % count) for i in range(count)])


def swap_x(block):
    return lax.ppermute(block, "mp", [(i, i ^ 1) for i in range(lax.axis_size("mp"))])


def swap_y(block):
    return lax.ppermute(block, "group", [(i, i ^ 2) for i in range(lax.axis_size("group"))])


def swap_core(block):
    return lax.ppermute(block, "group", [(i, i ^ 1) for i in range(lax.axis_size("group"))])


def swap_home(block, lines, step):
    shards = 2 * lines
    route = []
    for group in range(lax.axis_size("group")):
        for index in range(shards):
            apart = index % 2 ^ group % 2
            to = ((index + 2 * step) % shards) ^ apart
            if step or apart:
                route.append((group * shards + index, (group ^ apart) * shards + to))
    return lax.ppermute(block, ("group", "mp"), route)


def together(*arrays):
    return lax.optimization_barrier(arrays)


def put(buffer, block, *place):
    shape = (1,) * len(place) + block.shape
    rest = (0,) * (buffer.ndim - len(place))
    return lax.dynamic_update_slice(buffer, block.reshape(shape), tuple(place) + rest)


def pick(buffer, index):
    return lax.dynamic_index_in_dim(buffer, index, 0, keepdims=False)


def first_hop(piece):
    return swap_x(piece), swap_y(piece)


def second_hop(at_x, at_y):
    split = at_x.shape[0] // 2
    return swap_y(at_x[:split]), swap_x(at_y[split:])


def four_pieces(whole, piece, at_x, at_y, far_low, far_high, x, y, part):
    def write(block, column, row, half=None):
        at = 0 if half is None else half
        block = block.reshape((1, -1) + whole.shape[2:3] + (1,) + whole.shape[4:])
        place = (2 * column + row, at, 0, part) + (0,) * (whole.ndim - 4)
        return lax.dynamic_update_slice(whole, block, place)

    whole = write(piece, x, y)
    whole = write(at_x, 1 - x, y)
    whole = write(at_y, x, 1 - y)
    whole = write(far_low, 1 - x, 1 - y, 0)
    return write(far_high, 1 - x, 1 - y, 1)


def along_lines(parts, lines):
    sets = [[2 * a + b for a in range(lines)] for b in range(2)]
    return lax.all_to_all(
        parts, "mp", split_axis=0, concat_axis=0, axis_index_groups=sets, tiled=True
    )


def to_lines(parts, lines, z):
    return [over_mp(pick(parts, (z + step) % lines), lines, step) for step in range(1, lines)]


def to_both_cores(held, core):
    held = held.transpose(1, 0, 2, 3)
    other = swap_core(pick(held, 1 - core))
    mine = pick(held, core)
    both = jnp.stack([jnp.where(core == 0, mine, other), jnp.where(core == 0, other, mine)], axis=1)
    return both.reshape((-1,) + both.shape[2:])


def product_kernel(rows_ref, weights_ref, out_ref):
    out_ref[...] = jnp.dot(rows_ref[...], weights_ref[...], preferred_element_type=jnp.float32)


def product(rows, weights):
    count, depth = rows.shape
    width = weights.shape[1]
    tile = math.gcd(count, 256)
    return pl.pallas_call(
        product_kernel,
        grid=(count // tile,),
        in_specs=[
            pl.BlockSpec((tile, depth), lambda i: (i, 0)),
            pl.BlockSpec((depth, width), lambda i: (0, 0)),
        ],
        out_specs=pl.BlockSpec((tile, width), lambda i: (i, 0)),
        out_shape=jax.ShapeDtypeStruct((count, width), jnp.float32),
        compiler_params=pltpu.CompilerParams(vmem_limit_bytes=32 * 2**20),
        cost_estimate=pl.CostEstimate(flops=1, bytes_accessed=1, transcendentals=0),
    )(rows, weights)


def feed_forward_kernel(own_ref, other_ref, gate_ref, up_ref, down_ref, mine_ref, theirs_ref, rows, total):
    count = own_ref.shape[0]
    step = pl.program_id(0)

    @pl.when(step == 0)
    def _():
        rows[:count, :] = own_ref[...]
        rows[count:, :] = other_ref[...]
        total[...] = jnp.zeros_like(total)

    gate = jnp.dot(rows[...], gate_ref[...], preferred_element_type=jnp.float32)
    up = jnp.dot(rows[...], up_ref[...], preferred_element_type=jnp.float32)
    activated = (gate / (1.0 + jnp.exp(-gate)) * up).astype(jnp.bfloat16)
    total[...] += jnp.dot(activated, down_ref[...], preferred_element_type=jnp.float32)

    @pl.when(step == pl.num_programs(0) - 1)
    def _():
        mine_ref[...] = total[:count, :]
        theirs_ref[...] = total[count:, :].astype(jnp.bfloat16)


def feed_forward(own, other, gate_up, down):
    count, width = own.shape
    units = down.shape[0]
    run = math.gcd(units, 256)
    steps = units // run
    whole = pl.BlockSpec((count, width), lambda i: (0, 0))
    return pl.pallas_call(
        feed_forward_kernel,
        grid=(steps,),
        in_specs=[
            whole,
            whole,
            pl.BlockSpec((width, run), lambda i: (0, i)),
            pl.BlockSpec((width, run), lambda i: (0, steps + i)),
            pl.BlockSpec((run, width), lambda i: (i, 0)),
        ],
        out_specs=[whole, whole],
        out_shape=[
            jax.ShapeDtypeStruct((count, width), jnp.float32),
            jax.ShapeDtypeStruct((count, width), jnp.bfloat16),
        ],
        scratch_shapes=[
            pltpu.VMEM((2 * count, width), jnp.bfloat16),
            pltpu.VMEM((2 * count, width), jnp.float32),
        ],
        compiler_params=pltpu.CompilerParams(vmem_limit_bytes=40 * 2**20),
        cost_estimate=pl.CostEstimate(flops=1, bytes_accessed=1, transcendentals=0),
    )(own, other, gate_up, gate_up, down)


def attention_kernel(
    q_ref, k_ref, v_ref, q_scale, k_scale, q_gain, k_gain, cos_ref, sin_ref, seg_ref, ends_ref, out_ref
):
    count, size = q_ref.shape
    tile = math.gcd(count, 256)

    def ready(ref, scale, gain):
        normed = ref[...] * scale[...] * gain[...]
        turned = normed * cos_ref[...] + pltpu.roll(normed, size // 2, 1) * sin_ref[...]
        return turned.astype(jnp.bfloat16)

    queries = ready(q_ref, q_scale, q_gain)
    keys = ready(k_ref, k_scale, k_gain)
    values = v_ref[...].astype(jnp.bfloat16)
    for start in range(0, count, tile):
        low = max(0, start - -(-LONGEST // tile) * tile)
        stop = start + tile
        scores = lax.dot_general(
            queries[start:stop],
            keys[low:stop],
            (((1,), (1,)), ((), ())),
            preferred_element_type=jnp.float32,
        )
        scores = scores * (1.0 / math.sqrt(size))
        query_rows = start + lax.broadcasted_iota(jnp.int32, scores.shape, 0)
        key_rows = low + lax.broadcasted_iota(jnp.int32, scores.shape, 1)
        allowed = (seg_ref[start:stop, :] == ends_ref[:, low:stop]) & (key_rows <= query_rows)
        scores = jnp.where(allowed, scores, -1e30)
        weights = jnp.exp(scores - jnp.max(scores, axis=1, keepdims=True))
        whole = jnp.sum(weights, axis=1, keepdims=True)
        mixed = jnp.dot(
            weights.astype(jnp.bfloat16), values[low:stop], preferred_element_type=jnp.float32
        )
        out_ref[start:stop, :] = (mixed / whole).astype(jnp.bfloat16)


def attention(projected, q_scale, k_scale, q_gain, k_gain, segment, position):
    count = projected.shape[0]
    heads = projected.shape[1] // 3 // HEAD_DIM
    half = HEAD_DIM // 2
    frequency = jnp.exp(
        jnp.arange(half, dtype=jnp.float32) * (-2.0 * math.log(ROPE_BASE) / HEAD_DIM)
    )
    angles = position.astype(jnp.float32)[:, None] * frequency[None, :]
    cosines, sines = jnp.cos(angles), jnp.sin(angles)
    cosines = jnp.concatenate([cosines, cosines], axis=1)
    sines = jnp.concatenate([-sines, sines], axis=1)

    def head(first):
        return pl.BlockSpec((count, HEAD_DIM), lambda h: (0, first + h))

    def whole(shape):
        return pl.BlockSpec(shape, lambda h: (0, 0))

    return pl.pallas_call(
        attention_kernel,
        grid=(heads,),
        in_specs=[
            head(0),
            head(heads),
            head(2 * heads),
            whole((count, 1)),
            whole((count, 1)),
            pl.BlockSpec((1, HEAD_DIM), lambda h: (0, h)),
            pl.BlockSpec((1, HEAD_DIM), lambda h: (0, h)),
            whole((count, HEAD_DIM)),
            whole((count, HEAD_DIM)),
            whole((count, 1)),
            whole((1, count)),
        ],
        out_specs=head(0),
        out_shape=jax.ShapeDtypeStruct((count, heads * HEAD_DIM), jnp.bfloat16),
        compiler_params=pltpu.CompilerParams(vmem_limit_bytes=48 * 2**20),
        cost_estimate=pl.CostEstimate(flops=1, bytes_accessed=1, transcendentals=0),
    )(
        projected,
        projected,
        projected,
        q_scale[:, None],
        k_scale[:, None],
        q_gain[None],
        k_gain[None],
        cosines,
        sines,
        segment[:, None],
        segment[None],
    )


def per_device_lines(
    tokens,
    lengths,
    query_gain,
    key_gain,
    attn_post_gain,
    mlp_post_gain,
    query_weight,
    key_weight,
    value_weight,
    output_weight,
    gate_weight,
    up_weight,
    down_weight,
):
    bf16, f32 = jnp.bfloat16, jnp.float32
    features = tokens.shape[1]
    shards = lax.axis_size("mp")
    lines = shards // 2
    index = lax.axis_index("mp")
    z, x = index // 2, index % 2
    group = lax.axis_index("group")
    y, core = group // 2, group % 2
    tok_rows = tokens.shape[0]
    chip_rows = 2 * tok_rows
    group_rows = shards * tok_rows
    home = x == core

    z_cols = features // lines
    head_cols = z_cols // 2
    run = features // shards // 2

    def server_order(rows):
        parts = rows.reshape(rows.shape[:-1] + (lines, 4, run))
        return jnp.swapaxes(parts, -3, -2).reshape(rows.shape)

    def given_order(rows):
        parts = rows.reshape(rows.shape[:-1] + (4, lines, run))
        return jnp.swapaxes(parts, -3, -2).reshape(rows.shape)

    def by_owner(weights, runs):
        parts = [w.astype(bf16).reshape(w.shape[0], lines, runs, 2, -1) for w in weights]
        parts = jnp.stack(parts, axis=2).transpose(1, 4, 0, 2, 3, 5)
        return parts.reshape(lines, 2, weights[0].shape[0], -1)

    own = jnp.concatenate([server_order(tokens), server_order(output_weight.astype(bf16))], axis=0)
    own, *weights = together(own, query_weight, key_weight, value_weight)
    attn_parts = by_owner(weights, 1)
    ring_1 = swap_home(own, lines, 1)
    moved = swap_home(own, lines, 0)
    attn_parts, down_own = together(attn_parts, down_weight)
    attn_held = along_lines(attn_parts, lines)
    down_own = down_own.astype(bf16)
    down_near = first_hop(down_own)
    gate_up = by_owner((gate_weight, up_weight), 4)
    own, ring_1, moved, down_own, attn_held, gate_up, *down_near = together(
        own, ring_1, moved, down_own, attn_held, gate_up, *down_near
    )

    ring = [jnp.where(home, own, moved), ring_1]
    if lines > 2:
        ring.append(over_mp(ring[-1], lines, 1))
    attn_piece = to_both_cores(attn_held, core)
    attn_near = first_hop(attn_piece)
    rows = jnp.zeros((lines, 2) + tokens.shape, bf16)

    def place(rows, step, held, at_core):
        return put(rows, held[:tok_rows], (z - step) % lines, at_core)

    for step in range(2):
        rows = place(rows, step, ring[step], core)
        rows = place(rows, step, swap_core(ring[step]), 1 - core)
    ring[-1], gate_up = together(ring[-1], gate_up)

    attn_far = second_hop(*attn_near)
    for step in range(3, lines):
        ring.append(over_mp(ring[-1], lines, 1))
    for step in range(2, lines - 1):
        rows = place(rows, step, ring[step], core)
        rows = place(rows, step, swap_core(ring[step]), 1 - core)
    prompt_lens = jnp.where(home, lengths, swap_core(lengths))[0]
    attn_weights = jnp.zeros((4, 2, lines, 1) + attn_piece.shape[1:], bf16)
    attn_weights = four_pieces(attn_weights, attn_piece, *attn_near, *attn_far, x, y, 0)
    rows_half = gate_up.shape[2] // 2
    gate_up_1, gate_up_2 = gate_up[:, :, :rows_half], gate_up[:, :, rows_half:]
    rows, attn_weights, prompt_lens, gate_up_1, ring[-1] = together(
        rows, attn_weights, prompt_lens, gate_up_1, ring[-1]
    )
    held_1 = along_lines(gate_up_1, lines)
    last = lines - 1
    rows = place(rows, last, ring[last], core)
    rows = place(rows, last, swap_core(ring[last]), 1 - core)
    block = ring[0][:tok_rows]
    out_piece = jnp.stack([held[tok_rows:] for held in ring])
    out_near = first_hop(out_piece)

    rows = rows.reshape(group_rows, features)
    attn_weights = attn_weights.reshape(features, -1)
    projected = product(rows, attn_weights)
    q_raw = projected[:, :head_cols]
    k_raw = projected[:, head_cols : 2 * head_cols]
    squares = jnp.stack([jnp.sum(q_raw * q_raw, axis=1), jnp.sum(k_raw * k_raw, axis=1)])
    squares = squares + swap_core(squares)
    total = squares
    for step in range(1, lines):
        total = total + over_mp(squares, lines, step)
    col_start = z * z_cols + core * head_cols
    query_part = lax.dynamic_slice_in_dim(query_gain, col_start, head_cols)
    key_part = lax.dynamic_slice_in_dim(key_gain, col_start, head_cols)
    total, held_1, gate_up_2, out_piece, *rest = together(
        total, held_1, gate_up_2, out_piece, *out_near, *down_near
    )
    out_near, down_near = rest[:2], rest[2:]
    held_2 = along_lines(gate_up_2, lines)
    out_half = out_piece.shape[0] // 2
    down_half = down_own.shape[0] // 2
    far_low = jnp.concatenate([out_near[0][:out_half].reshape(-1, features), down_near[0][:down_half]])
    far_high = jnp.concatenate([out_near[1][out_half:].reshape(-1, features), down_near[1][down_half:]])
    both_far = [swap_y(far_low), swap_x(far_high)]
    piece_1 = to_both_cores(held_1, core)
    near_1 = first_hop(piece_1)

    segment, position = token_layout(prompt_lens, group_rows)
    attended = attention(
        projected,
        lax.rsqrt(total[0] / features + NORM_EPSILON),
        lax.rsqrt(total[1] / features + NORM_EPSILON),
        query_part,
        key_part,
        segment,
        position,
    )

    attended, out_piece, *rest = together(attended, out_piece, *out_near, *both_far)
    out_near, both_far = rest[:2], rest[2:]
    down_far = [far[-down_half:] for far in both_far]
    out_far = [far[:-down_half].reshape((out_half,) + out_piece.shape[1:]) for far in both_far]
    down_block = jnp.zeros((4, 2, down_half, 1, features), bf16)
    down_block = four_pieces(down_block, down_own, *down_near, *down_far, x, y, 0)
    attended = attended.reshape(lines, chip_rows, head_cols)
    both = jnp.concatenate([pick(attended, z)] + to_lines(attended, lines, z), axis=1)
    held_2, piece_1, near_x, near_y, _ = together(held_2, piece_1, *near_1, both)
    near_1 = (near_x, near_y)
    far_1 = second_hop(*near_1)
    piece_2 = to_both_cores(held_2, core)
    near_2 = first_hop(piece_2)
    out_weights = jnp.zeros((lines, 2, 2) + out_piece.shape[1:], bf16)
    split = lines // 2
    for held, row, column, at in (
        (out_piece, y, x, 0),
        (out_near[0], y, 1 - x, 0),
        (out_near[1], 1 - y, x, 0),
        (out_far[0], 1 - y, 1 - x, 0),
        (out_far[1], 1 - y, 1 - x, split),
    ):
        out_weights = lax.dynamic_update_slice(
            out_weights, held[:, None, None], (at, row, column, 0, 0)
        )
    out_weights = out_weights.reshape(-1, features)
    partial = jnp.dot(both, out_weights, preferred_element_type=f32)
    partial = partial.reshape(2, tok_rows, features)
    attn_out = pick(partial, core) + swap_core(pick(partial, 1 - core).astype(bf16)).astype(f32)
    hidden = block.astype(f32) + rms_scale(attn_out, server_order(attn_post_gain))
    hidden = hidden.astype(bf16)

    ring = [hidden]
    for step in range(1, lines):
        ring.append(over_mp(ring[-1], lines, 1))
    swap_from, *rest = together(ring[1], *far_1, *near_2)
    far_1, near_2 = rest[:2], rest[2:]
    far_2 = second_hop(*near_2)
    mlp_weights = jnp.zeros((4, 2, lines, 2) + piece_1.shape[1:], bf16)
    mlp_weights = four_pieces(mlp_weights, piece_1, *near_1, *far_1, x, y, 0)
    mlp_weights = four_pieces(mlp_weights, piece_2, *near_2, *far_2, x, y, 1)
    mlp_weights = mlp_weights.reshape(features, -1)
    down_block = down_block.reshape(-1, features)

    def both_rows(own):
        mine, theirs = feed_forward(own, swap_core(own), mlp_weights, down_block)
        return mine + swap_core(theirs).astype(f32)

    total_out = None
    for step in range(1, lines):
        part = both_rows(swap_from if step == 1 else ring[step])
        if total_out is not None:
            part = part + total_out.astype(f32)
        part = part.astype(bf16)
        total_out = over_mp(part, lines, 1) if step + 1 < lines else swap_home(part, lines, 1)
        if step == 1 and lines > 2:
            total_out, ring[0] = together(total_out, ring[0])
    own_out = both_rows(ring[0]).astype(bf16)
    own_out = jnp.where(home, own_out, swap_home(own_out, lines, 0)).astype(f32)
    hidden = given_order(hidden)
    hidden = jnp.where(home, hidden, swap_home(hidden, lines, 0)).astype(f32)
    mlp_out = own_out + total_out.astype(f32)
    return (hidden + rms_scale(mlp_out, mlp_post_gain)).astype(bf16)


def per_device(*arrays):
    heads = arrays[0].shape[1] // HEAD_DIM
    shards = lax.axis_size("mp")
    if lax.axis_size("group") == 4 and shards % 4 == 0 and heads % shards == 0:
        return per_device_lines(*arrays)
    return per_device_general(*arrays)


def solution(mesh):
    return jax.shard_map(
        per_device,
        mesh=mesh,
        in_specs=(
            P(("group", "mp"), None),
            P("group", None),
            P(),
            P(),
            P(),
            P(),
            P(("mp", "group"), None),
            P(("mp", "group"), None),
            P(("mp", "group"), None),
            P(("mp", "group"), None),
            P(("mp", "group"), None),
            P(("mp", "group"), None),
            P(("mp", "group"), None),
        ),
        out_specs=P(("group", "mp"), None),
        check_vma=False,
    )
```

```python
import math

import jax
import jax.numpy as jnp
from jax import lax
from jax.experimental import pallas as pl
from jax.experimental.pallas import tpu as pltpu
from jax.sharding import PartitionSpec as P

HEAD_DIM = 128
LONGEST = 512


NORM_EPSILON = 1e-06
ROPE_BASE = 500000.0


def partner_2(block, axis, apart):
    count = lax.axis_size(axis)
    route = []
    for low in range(count):
        high = low | 1 << apart
        if high != low and high < count:
            route += [(low, high), (high, low)]
    return lax.ppermute(block, axis, route)


def token_layout(prompt_lens, row_count):
    seg_ends = jnp.cumsum(prompt_lens)
    starts = seg_ends - prompt_lens
    indices = jnp.arange(row_count, dtype=jnp.int32)
    segment = jnp.sum((indices[:, None] >= seg_ends[None, :]).astype(jnp.int32), axis=1)
    member = segment[:, None] == jnp.arange(prompt_lens.shape[0], dtype=jnp.int32)[None, :]
    opening = jnp.sum(jnp.where(member, starts[None, :], 0), axis=1)
    return (segment, indices - opening)


def rotary(head_values, position, head_size):
    half_size = head_size // 2
    frequency = jnp.exp(
        jnp.arange(half_size, dtype=jnp.float32) * (-2.0 * math.log(ROPE_BASE) / head_size)
    )
    angles = position.astype(jnp.float32)[:, None] * frequency[None, :]
    cosines = jnp.cos(angles)
    sines = jnp.sin(angles)
    front_half = head_values[..., :half_size]
    back_half = head_values[..., half_size:]
    return jnp.concatenate(
        [front_half * cosines - back_half * sines, back_half * cosines + front_half * sines],
        axis=-1,
    )


def head_attention(queries, keys_rot, values_h, segment, head_size):
    scores = lax.dot_general(
        queries, keys_rot, (((1,), (1,)), ((), ())), preferred_element_type=jnp.float32
    )
    scores = scores * (1.0 / math.sqrt(head_size))
    key_rows = jnp.arange(keys_rot.shape[0], dtype=jnp.int32)
    query_segment = segment
    allowed = (query_segment[:, None] == segment[None, :]) & (
        key_rows[None, :] <= key_rows[:, None]
    )
    scores = jnp.where(allowed, scores, -1e30)
    row_max = jnp.max(scores, axis=1, keepdims=True)
    weights = jnp.exp(scores - row_max)
    weights = weights / jnp.sum(weights, axis=1, keepdims=True)
    probabilities = weights.astype(jnp.bfloat16)
    return jnp.dot(probabilities, values_h, preferred_element_type=jnp.float32).astype(jnp.bfloat16)


def rms_scale(values_in, gain):
    return (
        values_in
        * lax.rsqrt(jnp.mean(values_in * values_in, axis=-1, keepdims=True) + NORM_EPSILON)
        * gain
    )


def per_device_general(
    tokens,
    lengths,
    query_gain,
    key_gain,
    attn_post_gain,
    mlp_post_gain,
    query_weight,
    key_weight,
    value_weight,
    output_weight,
    gate_weight,
    up_weight,
    down_weight,
):
    features = tokens.shape[1]
    shards = lax.axis_size("mp")
    my_index = lax.axis_index("mp")
    col_width = features // shards
    tok_rows = tokens.shape[0]
    group_rows = tok_rows * shards
    halves = col_width < HEAD_DIM
    stack_attn = jnp.stack([query_weight, key_weight, value_weight]).astype(jnp.bfloat16)
    stack_mlp = jnp.stack([gate_weight, up_weight]).astype(jnp.bfloat16)
    down_piece = down_weight.astype(jnp.bfloat16)[None]
    output_piece = output_weight.astype(jnp.bfloat16)[None]
    attn_rows, mlp_rows, down_rows, output_rows = (
        lax.all_gather(stack_attn, "group", axis=1, tiled=True),
        lax.all_gather(stack_mlp, "group", axis=1, tiled=True),
        lax.all_gather(down_piece, "group", axis=1, tiled=True),
        lax.all_gather(output_piece, "group", axis=1, tiled=True),
    )
    attn_block, mlp_block = (
        lax.all_to_all(attn_rows, "mp", split_axis=2, concat_axis=1, tiled=True),
        lax.all_to_all(mlp_rows, "mp", split_axis=2, concat_axis=1, tiled=True),
    )
    down_block = down_rows[0]
    output_block = output_rows[0]
    parity = my_index % 2
    if halves:
        partner = partner_2(attn_block, "mp", 0)
        attn_block = jnp.where(
            parity == 0,
            jnp.concatenate([attn_block, partner], axis=2),
            jnp.concatenate([partner, attn_block], axis=2),
        )
    head_cols = attn_block.shape[2]
    col_start = my_index * col_width // HEAD_DIM * HEAD_DIM
    share_part = col_width / head_cols
    projected = jnp.einsum(
        "td,kdc->ktc",
        lax.all_gather(tokens, "mp", axis=0, tiled=True),
        attn_block,
        preferred_element_type=jnp.float32,
    )
    query_sq = jnp.sum(projected[0] * projected[0], axis=1) * share_part
    key_sq = jnp.sum(projected[1] * projected[1], axis=1) * share_part
    query_total, key_total = lax.psum((query_sq, key_sq), "mp")
    query_part = lax.dynamic_slice_in_dim(query_gain, col_start, head_cols)
    key_part = lax.dynamic_slice_in_dim(key_gain, col_start, head_cols)
    q_normed = projected[0] * lax.rsqrt(query_total / features + NORM_EPSILON)[:, None] * query_part
    k_normed = projected[1] * lax.rsqrt(key_total / features + NORM_EPSILON)[:, None] * key_part
    segment, position = token_layout(lengths[0], group_rows)
    local_heads = head_cols // HEAD_DIM

    def heads_first(flat):
        return flat.reshape(group_rows, local_heads, HEAD_DIM).transpose(1, 0, 2)

    queries = rotary(heads_first(q_normed), position, HEAD_DIM).astype(jnp.bfloat16)
    keys_rot = rotary(heads_first(k_normed), position, HEAD_DIM).astype(jnp.bfloat16)
    values_h = heads_first(projected[2].astype(jnp.bfloat16))

    def per_head(triple):
        return head_attention(triple[0], triple[1], triple[2], segment, HEAD_DIM)

    attended = lax.map(per_head, (queries, keys_rot, values_h))
    attended = attended.transpose(1, 0, 2).reshape(group_rows, head_cols)
    if halves:
        attended = lax.dynamic_slice_in_dim(attended, parity * col_width, col_width, 1)
    rows_part = attended
    attn_out = lax.psum_scatter(
        jnp.dot(rows_part, output_block, preferred_element_type=jnp.float32).astype(jnp.bfloat16),
        "mp",
        scatter_dimension=0,
        tiled=True,
    ).astype(jnp.float32)
    hidden = (tokens.astype(jnp.float32) + rms_scale(attn_out, attn_post_gain)).astype(jnp.bfloat16)
    hidden_width = mlp_block.shape[2]
    mlp_weights = jnp.concatenate([mlp_block[0], mlp_block[1]], axis=1)
    both_proj = jnp.dot(
        lax.all_gather(hidden, "mp", axis=0, tiled=True),
        mlp_weights,
        preferred_element_type=jnp.float32,
    )
    activated = (jax.nn.silu(both_proj[:, :hidden_width]) * both_proj[:, hidden_width:]).astype(
        jnp.bfloat16
    )
    rows_part = activated
    mlp_out = lax.psum_scatter(
        jnp.dot(rows_part, down_block, preferred_element_type=jnp.float32).astype(jnp.bfloat16),
        "mp",
        scatter_dimension=0,
        tiled=True,
    ).astype(jnp.float32)
    return (hidden.astype(jnp.float32) + rms_scale(mlp_out, mlp_post_gain)).astype(jnp.bfloat16)


def over_mp(block, lines, step):
    count = 2 * lines
    return lax.ppermute(block, "mp", [(i, (i + 2 * step) % count) for i in range(count)])


def swap_x(block):
    return lax.ppermute(block, "mp", [(i, i ^ 1) for i in range(lax.axis_size("mp"))])


def swap_y(block):
    return lax.ppermute(block, "group", [(i, i ^ 2) for i in range(lax.axis_size("group"))])


def swap_core(block):
    return lax.ppermute(block, "group", [(i, i ^ 1) for i in range(lax.axis_size("group"))])


def swap_home(block, lines, step):
    shards = 2 * lines
    route = []
    for group in range(lax.axis_size("group")):
        for index in range(shards):
            apart = index % 2 ^ group % 2
            to = ((index + 2 * step) % shards) ^ apart
            if step or apart:
                route.append((group * shards + index, (group ^ apart) * shards + to))
    return lax.ppermute(block, ("group", "mp"), route)


def together(*arrays):
    return lax.optimization_barrier(arrays)


def later(value, *earlier):
    return lax.optimization_barrier((value, *earlier))[0]


def put(buffer, block, *place):
    shape = (1,) * len(place) + block.shape
    rest = (0,) * (buffer.ndim - len(place))
    return lax.dynamic_update_slice(buffer, block.reshape(shape), tuple(place) + rest)


def pick(buffer, index):
    return lax.dynamic_index_in_dim(buffer, index, 0, keepdims=False)


def first_hop(piece):
    return swap_x(piece), swap_y(piece)


def second_hop(at_x, at_y):
    split = at_x.shape[0] // 2
    return swap_y(at_x[:split]), swap_x(at_y[split:])


def four_pieces(whole, piece, at_x, at_y, far_low, far_high, x, y, part):
    def write(block, column, row, half=None):
        at = 0 if half is None else half
        block = block.reshape((1, -1) + whole.shape[2:3] + (1,) + whole.shape[4:])
        place = (2 * column + row, at, 0, part) + (0,) * (whole.ndim - 4)
        return lax.dynamic_update_slice(whole, block, place)

    whole = write(piece, x, y)
    whole = write(at_x, 1 - x, y)
    whole = write(at_y, x, 1 - y)
    whole = write(far_low, 1 - x, 1 - y, 0)
    return write(far_high, 1 - x, 1 - y, 1)


def along_lines(parts, lines):
    sets = [[2 * a + b for a in range(lines)] for b in range(2)]
    return lax.all_to_all(
        parts, "mp", split_axis=0, concat_axis=0, axis_index_groups=sets, tiled=True
    )


def to_lines(parts, lines, z):
    return [over_mp(pick(parts, (z + step) % lines), lines, step) for step in range(1, lines)]


def to_both_cores(held, core):
    held = held.transpose(1, 0, 2, 3)
    other = swap_core(pick(held, 1 - core))
    mine = pick(held, core)
    both = jnp.stack([jnp.where(core == 0, mine, other), jnp.where(core == 0, other, mine)], axis=1)
    return both.reshape((-1,) + both.shape[2:])


def product_kernel(rows_ref, weights_ref, out_ref):
    out_ref[...] = jnp.dot(rows_ref[...], weights_ref[...], preferred_element_type=jnp.float32)


def product(rows, weights):
    count, depth = rows.shape
    width = weights.shape[1]
    tile = math.gcd(count, 256)
    return pl.pallas_call(
        product_kernel,
        grid=(count // tile,),
        in_specs=[
            pl.BlockSpec((tile, depth), lambda i: (i, 0)),
            pl.BlockSpec((depth, width), lambda i: (0, 0)),
        ],
        out_specs=pl.BlockSpec((tile, width), lambda i: (i, 0)),
        out_shape=jax.ShapeDtypeStruct((count, width), jnp.float32),
        compiler_params=pltpu.CompilerParams(vmem_limit_bytes=32 * 2**20),
        cost_estimate=pl.CostEstimate(flops=1, bytes_accessed=1, transcendentals=0),
    )(rows, weights)


def feed_forward_kernel(own_ref, other_ref, gate_ref, up_ref, down_ref, mine_ref, theirs_ref, rows, total):
    count = own_ref.shape[0]
    step = pl.program_id(0)

    @pl.when(step == 0)
    def _():
        rows[:count, :] = own_ref[...]
        rows[count:, :] = other_ref[...]
        total[...] = jnp.zeros_like(total)

    gate = jnp.dot(rows[...], gate_ref[...], preferred_element_type=jnp.float32)
    up = jnp.dot(rows[...], up_ref[...], preferred_element_type=jnp.float32)
    activated = (gate / (1.0 + jnp.exp(-gate)) * up).astype(jnp.bfloat16)
    total[...] += jnp.dot(activated, down_ref[...], preferred_element_type=jnp.float32)

    @pl.when(step == pl.num_programs(0) - 1)
    def _():
        mine_ref[...] = total[:count, :]
        theirs_ref[...] = total[count:, :].astype(jnp.bfloat16)


def feed_forward(own, other, gate_up, down):
    count, width = own.shape
    units = down.shape[0]
    run = math.gcd(units, 256)
    steps = units // run
    whole = pl.BlockSpec((count, width), lambda i: (0, 0))
    return pl.pallas_call(
        feed_forward_kernel,
        grid=(steps,),
        in_specs=[
            whole,
            whole,
            pl.BlockSpec((width, run), lambda i: (0, i)),
            pl.BlockSpec((width, run), lambda i: (0, steps + i)),
            pl.BlockSpec((run, width), lambda i: (i, 0)),
        ],
        out_specs=[whole, whole],
        out_shape=[
            jax.ShapeDtypeStruct((count, width), jnp.float32),
            jax.ShapeDtypeStruct((count, width), jnp.bfloat16),
        ],
        scratch_shapes=[
            pltpu.VMEM((2 * count, width), jnp.bfloat16),
            pltpu.VMEM((2 * count, width), jnp.float32),
        ],
        compiler_params=pltpu.CompilerParams(vmem_limit_bytes=40 * 2**20),
        cost_estimate=pl.CostEstimate(flops=1, bytes_accessed=1, transcendentals=0),
    )(own, other, gate_up, gate_up, down)


def attention_kernel(
    q_ref, k_ref, v_ref, q_scale, k_scale, q_gain, k_gain, cos_ref, sin_ref, seg_ref, ends_ref, out_ref
):
    count, size = q_ref.shape
    tile = math.gcd(count, 256)

    def ready(ref, scale, gain):
        normed = ref[...] * scale[...] * gain[...]
        turned = normed * cos_ref[...] + pltpu.roll(normed, size // 2, 1) * sin_ref[...]
        return turned.astype(jnp.bfloat16)

    queries = ready(q_ref, q_scale, q_gain)
    keys = ready(k_ref, k_scale, k_gain)
    values = v_ref[...].astype(jnp.bfloat16)
    for start in range(0, count, tile):
        low = max(0, start - -(-LONGEST // tile) * tile)
        stop = start + tile
        scores = lax.dot_general(
            queries[start:stop],
            keys[low:stop],
            (((1,), (1,)), ((), ())),
            preferred_element_type=jnp.float32,
        )
        scores = scores * (1.0 / math.sqrt(size))
        query_rows = start + lax.broadcasted_iota(jnp.int32, scores.shape, 0)
        key_rows = low + lax.broadcasted_iota(jnp.int32, scores.shape, 1)
        allowed = (seg_ref[start:stop, :] == ends_ref[:, low:stop]) & (key_rows <= query_rows)
        scores = jnp.where(allowed, scores, -1e30)
        weights = jnp.exp(scores - jnp.max(scores, axis=1, keepdims=True))
        whole = jnp.sum(weights, axis=1, keepdims=True)
        mixed = jnp.dot(
            weights.astype(jnp.bfloat16), values[low:stop], preferred_element_type=jnp.float32
        )
        out_ref[start:stop, :] = (mixed / whole).astype(jnp.bfloat16)


def rotary_tables(position):
    half = HEAD_DIM // 2
    frequency = jnp.exp(
        jnp.arange(half, dtype=jnp.float32) * (-2.0 * math.log(ROPE_BASE) / HEAD_DIM)
    )
    angles = position.astype(jnp.float32)[:, None] * frequency[None, :]
    cosines, sines = jnp.cos(angles), jnp.sin(angles)
    return jnp.concatenate([cosines, cosines], axis=1), jnp.concatenate([-sines, sines], axis=1)


def attention(projected, q_scale, k_scale, q_gain, k_gain, segment, cosines, sines):
    count = projected.shape[0]
    heads = projected.shape[1] // 3 // HEAD_DIM

    def head(first):
        return pl.BlockSpec((count, HEAD_DIM), lambda h: (0, first + h))

    def whole(shape):
        return pl.BlockSpec(shape, lambda h: (0, 0))

    return pl.pallas_call(
        attention_kernel,
        grid=(heads,),
        in_specs=[
            head(0),
            head(heads),
            head(2 * heads),
            whole((count, 1)),
            whole((count, 1)),
            pl.BlockSpec((1, HEAD_DIM), lambda h: (0, h)),
            pl.BlockSpec((1, HEAD_DIM), lambda h: (0, h)),
            whole((count, HEAD_DIM)),
            whole((count, HEAD_DIM)),
            whole((count, 1)),
            whole((1, count)),
        ],
        out_specs=head(0),
        out_shape=jax.ShapeDtypeStruct((count, heads * HEAD_DIM), jnp.bfloat16),
        compiler_params=pltpu.CompilerParams(vmem_limit_bytes=48 * 2**20),
        cost_estimate=pl.CostEstimate(flops=1, bytes_accessed=1, transcendentals=0),
    )(
        projected,
        projected,
        projected,
        q_scale[:, None],
        k_scale[:, None],
        q_gain[None],
        k_gain[None],
        cosines,
        sines,
        segment[:, None],
        segment[None],
    )


def per_device_lines(
    tokens,
    lengths,
    query_gain,
    key_gain,
    attn_post_gain,
    mlp_post_gain,
    query_weight,
    key_weight,
    value_weight,
    output_weight,
    gate_weight,
    up_weight,
    down_weight,
):
    bf16, f32 = jnp.bfloat16, jnp.float32
    features = tokens.shape[1]
    shards = lax.axis_size("mp")
    lines = shards // 2
    index = lax.axis_index("mp")
    z, x = index // 2, index % 2
    group = lax.axis_index("group")
    y, core = group // 2, group % 2
    tok_rows = tokens.shape[0]
    chip_rows = 2 * tok_rows
    group_rows = shards * tok_rows
    home = x == core

    z_cols = features // lines
    head_cols = z_cols // 2
    run = features // shards // 2

    def server_order(rows):
        parts = rows.reshape(rows.shape[:-1] + (lines, 4, run))
        return jnp.swapaxes(parts, -3, -2).reshape(rows.shape)

    def given_order(rows):
        parts = rows.reshape(rows.shape[:-1] + (4, lines, run))
        return jnp.swapaxes(parts, -3, -2).reshape(rows.shape)

    def by_owner(weights, runs):
        parts = [w.astype(bf16).reshape(w.shape[0], lines, runs, 2, -1) for w in weights]
        parts = jnp.stack(parts, axis=2).transpose(1, 4, 0, 2, 3, 5)
        return parts.reshape(lines, 2, weights[0].shape[0], -1)

    own = jnp.concatenate([server_order(tokens), server_order(output_weight.astype(bf16))], axis=0)
    own, *weights = together(own, query_weight, key_weight, value_weight)
    attn_parts = by_owner(weights, 1)
    ring_1 = swap_home(own, lines, 1)
    moved = swap_home(own, lines, 0)
    attn_parts, down_own = together(attn_parts, down_weight)
    attn_held = along_lines(attn_parts, lines)
    down_own = down_own.astype(bf16)
    down_near = first_hop(down_own)
    rows = jnp.zeros((lines, 2) + tokens.shape, bf16)
    gate_up = by_owner((gate_weight, up_weight), 4)
    own, ring_1, moved, down_own, attn_held, gate_up, rows, *down_near = together(
        own, ring_1, moved, down_own, attn_held, gate_up, rows, *down_near
    )

    ring = [jnp.where(home, own, moved), ring_1]
    if lines > 2:
        ring.append(over_mp(ring[-1], lines, 1))
    attn_piece = to_both_cores(attn_held, core)
    attn_near = first_hop(attn_piece)

    def place(rows, step, held, at_core):
        return put(rows, held[:tok_rows], (z - step) % lines, at_core)

    for step in range(2):
        rows = place(rows, step, ring[step], core)
        rows = place(rows, step, swap_core(ring[step]), 1 - core)
    ring[-1], gate_up = together(ring[-1], gate_up)

    attn_far = second_hop(*attn_near)
    for step in range(3, lines):
        ring.append(over_mp(ring[-1], lines, 1))
    for step in range(2, lines - 1):
        rows = place(rows, step, ring[step], core)
        rows = place(rows, step, swap_core(ring[step]), 1 - core)
    prompt_lens = jnp.where(home, lengths, swap_core(lengths))[0]
    attn_weights = jnp.zeros((4, 2, lines, 1) + attn_piece.shape[1:], bf16)
    attn_weights = four_pieces(attn_weights, attn_piece, *attn_near, *attn_far, x, y, 0)
    rows_half = gate_up.shape[2] // 2
    gate_up_1, gate_up_2 = gate_up[:, :, :rows_half], gate_up[:, :, rows_half:]
    segment, position = token_layout(prompt_lens, group_rows)
    cosines, sines = rotary_tables(position)
    rows, attn_weights, segment, cosines, sines, gate_up_1, ring[-1] = together(
        rows, attn_weights, segment, cosines, sines, gate_up_1, ring[-1]
    )
    held_1 = along_lines(gate_up_1, lines)
    last = lines - 1
    rows = place(rows, last, ring[last], core)
    rows = place(rows, last, swap_core(ring[last]), 1 - core)
    block = ring[0][:tok_rows]
    out_piece = jnp.stack([held[tok_rows:] for held in ring])
    out_near = first_hop(out_piece)

    rows = rows.reshape(group_rows, features)
    attn_weights = attn_weights.reshape(features, -1)
    projected = product(rows, attn_weights)
    q_raw = projected[:, :head_cols]
    k_raw = projected[:, head_cols : 2 * head_cols]
    squares = jnp.stack([jnp.sum(q_raw * q_raw, axis=1), jnp.sum(k_raw * k_raw, axis=1)])
    squares = squares + swap_core(squares)
    squares, out_piece, held_1, *out_near = together(squares, out_piece, held_1, *out_near)
    total = squares
    for step in range(1, lines):
        total = total + over_mp(squares, lines, step)
    col_start = z * z_cols + core * head_cols
    query_part = lax.dynamic_slice_in_dim(query_gain, col_start, head_cols)
    key_part = lax.dynamic_slice_in_dim(key_gain, col_start, head_cols)
    out_half = out_piece.shape[0] // 2
    down_half = down_own.shape[0] // 2
    far_low = jnp.concatenate([out_near[0][:out_half].reshape(-1, features), down_near[0][:down_half]])
    far_high = jnp.concatenate([out_near[1][out_half:].reshape(-1, features), down_near[1][down_half:]])
    both_far = [swap_y(far_low), swap_x(far_high)]
    piece_1 = to_both_cores(held_1, core)
    held_2 = along_lines(later(gate_up_2, total), lines)
    total, piece_1 = together(total, piece_1)
    near_1 = first_hop(piece_1)

    attended = attention(
        projected,
        lax.rsqrt(total[0] / features + NORM_EPSILON),
        lax.rsqrt(total[1] / features + NORM_EPSILON),
        query_part,
        key_part,
        segment,
        cosines,
        sines,
    )

    attended, *both_far = together(attended, *both_far)
    out_far = [far[:-down_half].reshape((out_half,) + out_piece.shape[1:]) for far in both_far]
    attended = attended.reshape(lines, chip_rows, head_cols)
    both = jnp.concatenate([pick(attended, z)] + to_lines(attended, lines, z), axis=1)
    both, *near_1 = together(both, *near_1)
    out_weights = later(jnp.zeros((lines, 2, 2) + out_piece.shape[1:], bf16), attended)
    split = lines // 2
    for held, row, column, at in (
        (out_piece, y, x, 0),
        (out_near[0], y, 1 - x, 0),
        (out_near[1], 1 - y, x, 0),
        (out_far[0], 1 - y, 1 - x, 0),
        (out_far[1], 1 - y, 1 - x, split),
    ):
        out_weights = lax.dynamic_update_slice(
            out_weights, later(held, attended)[:, None, None], (at, row, column, 0, 0)
        )
    out_weights = out_weights.reshape(-1, features)
    partial = jnp.dot(both, out_weights, preferred_element_type=f32)
    partial = partial.reshape(2, tok_rows, features)
    attn_out = pick(partial, core) + swap_core(pick(partial, 1 - core).astype(bf16)).astype(f32)
    far_1 = second_hop(*near_1)
    piece_2 = to_both_cores(later(held_2, partial), core)
    near_2 = first_hop(piece_2)
    hidden = block.astype(f32) + rms_scale(attn_out, server_order(attn_post_gain))
    hidden = hidden.astype(bf16)

    ring = [hidden]
    for step in range(1, lines):
        ring.append(over_mp(ring[-1], lines, 1))
    swap_from, *rest = together(ring[1], *far_1, *near_2)
    far_1, near_2 = rest[:2], rest[2:]
    far_2 = second_hop(*near_2)
    mlp_weights = jnp.zeros((4, 2, lines, 2) + piece_1.shape[1:], bf16)
    mlp_weights = four_pieces(mlp_weights, piece_1, *near_1, *far_1, x, y, 0)
    mlp_weights = four_pieces(mlp_weights, piece_2, *near_2, *far_2, x, y, 1)
    mlp_weights = mlp_weights.reshape(features, -1)
    down_pieces = [later(piece, hidden) for piece in (down_own, *down_near, *both_far)]
    down_pieces[3:] = [far[-down_half:] for far in down_pieces[3:]]
    down_block = jnp.zeros((4, 2, down_half, 1, features), bf16)
    down_block = four_pieces(down_block, *down_pieces, x, y, 0)
    down_block = down_block.reshape(-1, features)

    def both_rows(own):
        mine, theirs = feed_forward(own, swap_core(own), mlp_weights, down_block)
        return mine + swap_core(theirs).astype(f32)

    total_out = None
    for step in range(1, lines):
        part = both_rows(swap_from if step == 1 else ring[step])
        if total_out is not None:
            part = part + total_out.astype(f32)
        part = part.astype(bf16)
        total_out = over_mp(part, lines, 1) if step + 1 < lines else swap_home(part, lines, 1)
        if step == 1 and lines > 2:
            total_out, ring[0] = together(total_out, ring[0])
    own_out = both_rows(ring[0]).astype(bf16)
    own_out = jnp.where(home, own_out, swap_home(own_out, lines, 0)).astype(f32)
    hidden = given_order(hidden)
    hidden = jnp.where(home, hidden, swap_home(hidden, lines, 0)).astype(f32)
    mlp_out = own_out + total_out.astype(f32)
    return (hidden + rms_scale(mlp_out, mlp_post_gain)).astype(bf16)


def per_device(*arrays):
    heads = arrays[0].shape[1] // HEAD_DIM
    shards = lax.axis_size("mp")
    if lax.axis_size("group") == 4 and shards % 4 == 0 and heads % shards == 0:
        return per_device_lines(*arrays)
    return per_device_general(*arrays)


def solution(mesh):
    return jax.shard_map(
        per_device,
        mesh=mesh,
        in_specs=(
            P(("group", "mp"), None),
            P("group", None),
            P(),
            P(),
            P(),
            P(),
            P(("mp", "group"), None),
            P(("mp", "group"), None),
            P(("mp", "group"), None),
            P(("mp", "group"), None),
            P(("mp", "group"), None),
            P(("mp", "group"), None),
            P(("mp", "group"), None),
        ),
        out_specs=P(("group", "mp"), None),
        check_vma=False,
    )
```

```python
import math

import jax
import jax.numpy as jnp
from jax import lax
from jax.experimental import pallas as pl
from jax.experimental.pallas import tpu as pltpu
from jax.sharding import PartitionSpec as P

HEAD_DIM = 128
LONGEST = 512


NORM_EPSILON = 1e-06
ROPE_BASE = 500000.0


def partner_2(block, axis, apart):
    count = lax.axis_size(axis)
    route = []
    for low in range(count):
        high = low | 1 << apart
        if high != low and high < count:
            route += [(low, high), (high, low)]
    return lax.ppermute(block, axis, route)


def token_layout(prompt_lens, row_count):
    seg_ends = jnp.cumsum(prompt_lens)
    starts = seg_ends - prompt_lens
    indices = jnp.arange(row_count, dtype=jnp.int32)
    segment = jnp.sum((indices[:, None] >= seg_ends[None, :]).astype(jnp.int32), axis=1)
    member = segment[:, None] == jnp.arange(prompt_lens.shape[0], dtype=jnp.int32)[None, :]
    opening = jnp.sum(jnp.where(member, starts[None, :], 0), axis=1)
    return (segment, indices - opening)


def rotary(head_values, position, head_size):
    half_size = head_size // 2
    frequency = jnp.exp(
        jnp.arange(half_size, dtype=jnp.float32) * (-2.0 * math.log(ROPE_BASE) / head_size)
    )
    angles = position.astype(jnp.float32)[:, None] * frequency[None, :]
    cosines = jnp.cos(angles)
    sines = jnp.sin(angles)
    front_half = head_values[..., :half_size]
    back_half = head_values[..., half_size:]
    return jnp.concatenate(
        [front_half * cosines - back_half * sines, back_half * cosines + front_half * sines],
        axis=-1,
    )


def head_attention(queries, keys_rot, values_h, segment, head_size):
    scores = lax.dot_general(
        queries, keys_rot, (((1,), (1,)), ((), ())), preferred_element_type=jnp.float32
    )
    scores = scores * (1.0 / math.sqrt(head_size))
    key_rows = jnp.arange(keys_rot.shape[0], dtype=jnp.int32)
    query_segment = segment
    allowed = (query_segment[:, None] == segment[None, :]) & (
        key_rows[None, :] <= key_rows[:, None]
    )
    scores = jnp.where(allowed, scores, -1e30)
    row_max = jnp.max(scores, axis=1, keepdims=True)
    weights = jnp.exp(scores - row_max)
    weights = weights / jnp.sum(weights, axis=1, keepdims=True)
    probabilities = weights.astype(jnp.bfloat16)
    return jnp.dot(probabilities, values_h, preferred_element_type=jnp.float32).astype(jnp.bfloat16)


def rms_scale(values_in, gain):
    return (
        values_in
        * lax.rsqrt(jnp.mean(values_in * values_in, axis=-1, keepdims=True) + NORM_EPSILON)
        * gain
    )


def per_device_general(
    tokens,
    lengths,
    query_gain,
    key_gain,
    attn_post_gain,
    mlp_post_gain,
    query_weight,
    key_weight,
    value_weight,
    output_weight,
    gate_weight,
    up_weight,
    down_weight,
):
    features = tokens.shape[1]
    shards = lax.axis_size("mp")
    my_index = lax.axis_index("mp")
    col_width = features // shards
    tok_rows = tokens.shape[0]
    group_rows = tok_rows * shards
    halves = col_width < HEAD_DIM
    stack_attn = jnp.stack([query_weight, key_weight, value_weight]).astype(jnp.bfloat16)
    stack_mlp = jnp.stack([gate_weight, up_weight]).astype(jnp.bfloat16)
    down_piece = down_weight.astype(jnp.bfloat16)[None]
    output_piece = output_weight.astype(jnp.bfloat16)[None]
    attn_rows, mlp_rows, down_rows, output_rows = (
        lax.all_gather(stack_attn, "group", axis=1, tiled=True),
        lax.all_gather(stack_mlp, "group", axis=1, tiled=True),
        lax.all_gather(down_piece, "group", axis=1, tiled=True),
        lax.all_gather(output_piece, "group", axis=1, tiled=True),
    )
    attn_block, mlp_block = (
        lax.all_to_all(attn_rows, "mp", split_axis=2, concat_axis=1, tiled=True),
        lax.all_to_all(mlp_rows, "mp", split_axis=2, concat_axis=1, tiled=True),
    )
    down_block = down_rows[0]
    output_block = output_rows[0]
    parity = my_index % 2
    if halves:
        partner = partner_2(attn_block, "mp", 0)
        attn_block = jnp.where(
            parity == 0,
            jnp.concatenate([attn_block, partner], axis=2),
            jnp.concatenate([partner, attn_block], axis=2),
        )
    head_cols = attn_block.shape[2]
    col_start = my_index * col_width // HEAD_DIM * HEAD_DIM
    share_part = col_width / head_cols
    projected = jnp.einsum(
        "td,kdc->ktc",
        lax.all_gather(tokens, "mp", axis=0, tiled=True),
        attn_block,
        preferred_element_type=jnp.float32,
    )
    query_sq = jnp.sum(projected[0] * projected[0], axis=1) * share_part
    key_sq = jnp.sum(projected[1] * projected[1], axis=1) * share_part
    query_total, key_total = lax.psum((query_sq, key_sq), "mp")
    query_part = lax.dynamic_slice_in_dim(query_gain, col_start, head_cols)
    key_part = lax.dynamic_slice_in_dim(key_gain, col_start, head_cols)
    q_normed = projected[0] * lax.rsqrt(query_total / features + NORM_EPSILON)[:, None] * query_part
    k_normed = projected[1] * lax.rsqrt(key_total / features + NORM_EPSILON)[:, None] * key_part
    segment, position = token_layout(lengths[0], group_rows)
    local_heads = head_cols // HEAD_DIM

    def heads_first(flat):
        return flat.reshape(group_rows, local_heads, HEAD_DIM).transpose(1, 0, 2)

    queries = rotary(heads_first(q_normed), position, HEAD_DIM).astype(jnp.bfloat16)
    keys_rot = rotary(heads_first(k_normed), position, HEAD_DIM).astype(jnp.bfloat16)
    values_h = heads_first(projected[2].astype(jnp.bfloat16))

    def per_head(triple):
        return head_attention(triple[0], triple[1], triple[2], segment, HEAD_DIM)

    attended = lax.map(per_head, (queries, keys_rot, values_h))
    attended = attended.transpose(1, 0, 2).reshape(group_rows, head_cols)
    if halves:
        attended = lax.dynamic_slice_in_dim(attended, parity * col_width, col_width, 1)
    rows_part = attended
    attn_out = lax.psum_scatter(
        jnp.dot(rows_part, output_block, preferred_element_type=jnp.float32).astype(jnp.bfloat16),
        "mp",
        scatter_dimension=0,
        tiled=True,
    ).astype(jnp.float32)
    hidden = (tokens.astype(jnp.float32) + rms_scale(attn_out, attn_post_gain)).astype(jnp.bfloat16)
    hidden_width = mlp_block.shape[2]
    mlp_weights = jnp.concatenate([mlp_block[0], mlp_block[1]], axis=1)
    both_proj = jnp.dot(
        lax.all_gather(hidden, "mp", axis=0, tiled=True),
        mlp_weights,
        preferred_element_type=jnp.float32,
    )
    activated = (jax.nn.silu(both_proj[:, :hidden_width]) * both_proj[:, hidden_width:]).astype(
        jnp.bfloat16
    )
    rows_part = activated
    mlp_out = lax.psum_scatter(
        jnp.dot(rows_part, down_block, preferred_element_type=jnp.float32).astype(jnp.bfloat16),
        "mp",
        scatter_dimension=0,
        tiled=True,
    ).astype(jnp.float32)
    return (hidden.astype(jnp.float32) + rms_scale(mlp_out, mlp_post_gain)).astype(jnp.bfloat16)


def over_mp(block, lines, step):
    count = 2 * lines
    return lax.ppermute(block, "mp", [(i, (i + 2 * step) % count) for i in range(count)])


def swap_x(block):
    return lax.ppermute(block, "mp", [(i, i ^ 1) for i in range(lax.axis_size("mp"))])


def swap_y(block):
    return lax.ppermute(block, "group", [(i, i ^ 2) for i in range(lax.axis_size("group"))])


def swap_core(block):
    return lax.ppermute(block, "group", [(i, i ^ 1) for i in range(lax.axis_size("group"))])


def swap_home(block, lines, step):
    shards = 2 * lines
    route = []
    for group in range(lax.axis_size("group")):
        for index in range(shards):
            apart = index % 2 ^ group % 2
            to = ((index + 2 * step) % shards) ^ apart
            if step or apart:
                route.append((group * shards + index, (group ^ apart) * shards + to))
    return lax.ppermute(block, ("group", "mp"), route)


def together(*arrays):
    return lax.optimization_barrier(arrays)


def later(value, *earlier):
    return lax.optimization_barrier((value, *earlier))[0]


def put(buffer, block, *place):
    shape = (1,) * len(place) + block.shape
    rest = (0,) * (buffer.ndim - len(place))
    return lax.dynamic_update_slice(buffer, block.reshape(shape), tuple(place) + rest)


def pick(buffer, index):
    return lax.dynamic_index_in_dim(buffer, index, 0, keepdims=False)


def first_hop(piece):
    return swap_x(piece), swap_y(piece)


def second_hop(at_x, at_y):
    split = at_x.shape[0] // 2
    return swap_y(at_x[:split]), swap_x(at_y[split:])


def four_pieces(whole, piece, at_x, at_y, far_low, far_high, x, y, part):
    def write(block, column, row, half=None):
        at = 0 if half is None else half
        block = block.reshape((1, -1) + whole.shape[2:3] + (1,) + whole.shape[4:])
        place = (2 * column + row, at, 0, part) + (0,) * (whole.ndim - 4)
        return lax.dynamic_update_slice(whole, block, place)

    whole = write(piece, x, y)
    whole = write(at_x, 1 - x, y)
    whole = write(at_y, x, 1 - y)
    whole = write(far_low, 1 - x, 1 - y, 0)
    return write(far_high, 1 - x, 1 - y, 1)


def along_lines(parts, lines):
    sets = [[2 * a + b for a in range(lines)] for b in range(2)]
    return lax.all_to_all(
        parts, "mp", split_axis=0, concat_axis=0, axis_index_groups=sets, tiled=True
    )


def to_lines(parts, lines, z):
    return [over_mp(pick(parts, (z + step) % lines), lines, step) for step in range(1, lines)]


def along_lines_in_steps(parts, lines, z):
    held = put(jnp.zeros(parts.shape, parts.dtype), pick(parts, z), z)
    for step, block in enumerate(to_lines(parts, lines, z), 1):
        held = put(held, block, (z - step) % lines)
    return held


def to_both_cores(held, core):
    held = held.transpose(1, 0, 2, 3)
    other = swap_core(pick(held, 1 - core))
    mine = pick(held, core)
    both = jnp.stack([jnp.where(core == 0, mine, other), jnp.where(core == 0, other, mine)], axis=1)
    return both.reshape((-1,) + both.shape[2:])


def product_kernel(rows_ref, weights_ref, out_ref):
    out_ref[...] = jnp.dot(rows_ref[...], weights_ref[...], preferred_element_type=jnp.float32)


def product(rows, weights):
    count, depth = rows.shape
    width = weights.shape[1]
    tile = math.gcd(count, 256)
    return pl.pallas_call(
        product_kernel,
        grid=(count // tile,),
        in_specs=[
            pl.BlockSpec((tile, depth), lambda i: (i, 0)),
            pl.BlockSpec((depth, width), lambda i: (0, 0)),
        ],
        out_specs=pl.BlockSpec((tile, width), lambda i: (i, 0)),
        out_shape=jax.ShapeDtypeStruct((count, width), jnp.float32),
        compiler_params=pltpu.CompilerParams(vmem_limit_bytes=32 * 2**20),
        cost_estimate=pl.CostEstimate(flops=1, bytes_accessed=1, transcendentals=0),
    )(rows, weights)


def feed_forward_kernel(own_ref, other_ref, gate_ref, up_ref, down_ref, mine_ref, theirs_ref, rows, total):
    count = own_ref.shape[0]
    step = pl.program_id(0)

    @pl.when(step == 0)
    def _():
        rows[:count, :] = own_ref[...]
        rows[count:, :] = other_ref[...]

    gate = jnp.dot(rows[...], gate_ref[...], preferred_element_type=jnp.float32)
    up = jnp.dot(rows[...], up_ref[...], preferred_element_type=jnp.float32)
    activated = (gate / (1.0 + jnp.exp(-gate)) * up).astype(jnp.bfloat16)
    part = jnp.dot(activated, down_ref[...], preferred_element_type=jnp.float32)
    last = pl.num_programs(0) - 1

    @pl.when(step == 0)
    def _():
        total[...] = part

    @pl.when((step > 0) & (step < last))
    def _():
        total[...] += part

    @pl.when(step == last)
    def _():
        mine_ref[...] = total[:count, :] + part[:count, :]
        theirs_ref[...] = (total[count:, :] + part[count:, :]).astype(jnp.bfloat16)


def feed_forward(own, other, gate_up, down):
    count, width = own.shape
    units = down.shape[0]
    run = math.gcd(units, 256)
    steps = units // run
    whole = pl.BlockSpec((count, width), lambda i: (0, 0))
    return pl.pallas_call(
        feed_forward_kernel,
        grid=(steps,),
        in_specs=[
            whole,
            whole,
            pl.BlockSpec((width, run), lambda i: (0, i)),
            pl.BlockSpec((width, run), lambda i: (0, steps + i)),
            pl.BlockSpec((run, width), lambda i: (i, 0)),
        ],
        out_specs=[whole, whole],
        out_shape=[
            jax.ShapeDtypeStruct((count, width), jnp.float32),
            jax.ShapeDtypeStruct((count, width), jnp.bfloat16),
        ],
        scratch_shapes=[
            pltpu.VMEM((2 * count, width), jnp.bfloat16),
            pltpu.VMEM((2 * count, width), jnp.float32),
        ],
        compiler_params=pltpu.CompilerParams(vmem_limit_bytes=32 * 2**20),
        cost_estimate=pl.CostEstimate(flops=1, bytes_accessed=1, transcendentals=0),
    )(own, other, gate_up, gate_up, down)


def attention_kernel(
    q_ref, k_ref, v_ref, q_scale, k_scale, q_gain, k_gain, cos_ref, sin_ref, seg_ref, ends_ref, out_ref
):
    count, size = q_ref.shape
    tile = math.gcd(count, 256)

    def ready(ref, scale, gain):
        normed = ref[...] * scale[...] * gain[...]
        turned = normed * cos_ref[...] + pltpu.roll(normed, size // 2, 1) * sin_ref[...]
        return turned.astype(jnp.bfloat16)

    queries = ready(q_ref, q_scale, q_gain)
    keys = ready(k_ref, k_scale, k_gain)
    values = v_ref[...].astype(jnp.bfloat16)
    for start in range(0, count, tile):
        low = max(0, start - -(-LONGEST // tile) * tile)
        stop = start + tile
        scores = lax.dot_general(
            queries[start:stop],
            keys[low:stop],
            (((1,), (1,)), ((), ())),
            preferred_element_type=jnp.float32,
        )
        scores = scores * (1.0 / math.sqrt(size))
        query_rows = start + lax.broadcasted_iota(jnp.int32, scores.shape, 0)
        key_rows = low + lax.broadcasted_iota(jnp.int32, scores.shape, 1)
        allowed = (seg_ref[start:stop, :] == ends_ref[:, low:stop]) & (key_rows <= query_rows)
        scores = jnp.where(allowed, scores, -1e30)
        weights = jnp.exp(scores - jnp.max(scores, axis=1, keepdims=True))
        whole = jnp.sum(weights, axis=1, keepdims=True)
        mixed = jnp.dot(
            weights.astype(jnp.bfloat16), values[low:stop], preferred_element_type=jnp.float32
        )
        out_ref[start:stop, :] = (mixed / whole).astype(jnp.bfloat16)


def rotary_tables(position):
    half = HEAD_DIM // 2
    frequency = jnp.exp(
        jnp.arange(half, dtype=jnp.float32) * (-2.0 * math.log(ROPE_BASE) / HEAD_DIM)
    )
    angles = position.astype(jnp.float32)[:, None] * frequency[None, :]
    cosines, sines = jnp.cos(angles), jnp.sin(angles)
    return jnp.concatenate([cosines, cosines], axis=1), jnp.concatenate([-sines, sines], axis=1)


def attention(projected, q_scale, k_scale, q_gain, k_gain, segment, cosines, sines):
    count = projected.shape[0]
    heads = projected.shape[1] // 3 // HEAD_DIM

    def head(first):
        return pl.BlockSpec((count, HEAD_DIM), lambda h: (0, first + h))

    def whole(shape):
        return pl.BlockSpec(shape, lambda h: (0, 0))

    return pl.pallas_call(
        attention_kernel,
        grid=(heads,),
        in_specs=[
            head(0),
            head(heads),
            head(2 * heads),
            whole((count, 1)),
            whole((count, 1)),
            pl.BlockSpec((1, HEAD_DIM), lambda h: (0, h)),
            pl.BlockSpec((1, HEAD_DIM), lambda h: (0, h)),
            whole((count, HEAD_DIM)),
            whole((count, HEAD_DIM)),
            whole((count, 1)),
            whole((1, count)),
        ],
        out_specs=head(0),
        out_shape=jax.ShapeDtypeStruct((count, heads * HEAD_DIM), jnp.bfloat16),
        compiler_params=pltpu.CompilerParams(vmem_limit_bytes=48 * 2**20),
        cost_estimate=pl.CostEstimate(flops=1, bytes_accessed=1, transcendentals=0),
    )(
        projected,
        projected,
        projected,
        q_scale[:, None],
        k_scale[:, None],
        q_gain[None],
        k_gain[None],
        cosines,
        sines,
        segment[:, None],
        segment[None],
    )


def per_device_lines(
    tokens,
    lengths,
    query_gain,
    key_gain,
    attn_post_gain,
    mlp_post_gain,
    query_weight,
    key_weight,
    value_weight,
    output_weight,
    gate_weight,
    up_weight,
    down_weight,
):
    bf16, f32 = jnp.bfloat16, jnp.float32
    features = tokens.shape[1]
    shards = lax.axis_size("mp")
    lines = shards // 2
    index = lax.axis_index("mp")
    z, x = index // 2, index % 2
    group = lax.axis_index("group")
    y, core = group // 2, group % 2
    tok_rows = tokens.shape[0]
    chip_rows = 2 * tok_rows
    group_rows = shards * tok_rows
    home = x == core

    z_cols = features // lines
    head_cols = z_cols // 2
    run = features // shards // 2

    def server_order(rows):
        parts = rows.reshape(rows.shape[:-1] + (lines, 4, run))
        return jnp.swapaxes(parts, -3, -2).reshape(rows.shape)

    def given_order(rows):
        parts = rows.reshape(rows.shape[:-1] + (4, lines, run))
        return jnp.swapaxes(parts, -3, -2).reshape(rows.shape)

    def by_owner(weights, runs):
        parts = [w.astype(bf16).reshape(w.shape[0], lines, runs, 2, -1) for w in weights]
        parts = jnp.stack(parts, axis=2).transpose(1, 4, 0, 2, 3, 5)
        return parts.reshape(lines, 2, weights[0].shape[0], -1)

    own = jnp.concatenate([server_order(tokens), server_order(output_weight.astype(bf16))], axis=0)
    own, *weights = together(own, query_weight, key_weight, value_weight)
    attn_parts = by_owner(weights, 1)
    ring_1 = swap_home(own, lines, 1)
    moved = swap_home(own, lines, 0)
    attn_parts, down_own = together(attn_parts, down_weight)
    attn_held = along_lines(attn_parts, lines)
    down_own = down_own.astype(bf16)
    down_near = first_hop(down_own)
    rows = jnp.zeros((lines, 2) + tokens.shape, bf16)
    gate_up = by_owner((gate_weight, up_weight), 4)
    own, ring_1, moved, down_own, attn_held, gate_up, rows, *down_near = together(
        own, ring_1, moved, down_own, attn_held, gate_up, rows, *down_near
    )

    ring = [jnp.where(home, own, moved), ring_1]
    if lines > 2:
        ring.append(over_mp(ring[-1], lines, 1))
    attn_piece = to_both_cores(attn_held, core)
    attn_near = first_hop(attn_piece)

    def place(rows, step, held, at_core):
        return put(rows, held[:tok_rows], (z - step) % lines, at_core)

    for step in range(2):
        rows = place(rows, step, ring[step], core)
        rows = place(rows, step, swap_core(ring[step]), 1 - core)
    ring[-1], gate_up = together(ring[-1], gate_up)

    attn_far = second_hop(*attn_near)
    for step in range(3, lines):
        ring.append(over_mp(ring[-1], lines, 1))
    for step in range(2, lines - 1):
        rows = place(rows, step, ring[step], core)
        rows = place(rows, step, swap_core(ring[step]), 1 - core)
    prompt_lens = jnp.where(home, lengths, swap_core(lengths))[0]
    attn_weights = jnp.zeros((4, 2, lines, 1) + attn_piece.shape[1:], bf16)
    attn_weights = four_pieces(attn_weights, attn_piece, *attn_near, *attn_far, x, y, 0)
    rows_half = gate_up.shape[2] // 2
    gate_up_1, gate_up_2 = gate_up[:, :, :rows_half], gate_up[:, :, rows_half:]
    segment, position = token_layout(prompt_lens, group_rows)
    cosines, sines = rotary_tables(position)
    rows, attn_weights, segment, cosines, sines, gate_up_1, ring[-1] = together(
        rows, attn_weights, segment, cosines, sines, gate_up_1, ring[-1]
    )
    last = lines - 1
    rows = place(rows, last, ring[last], core)
    swapped = swap_core(ring[last])
    rows = place(rows, last, swapped, 1 - core)
    held_1 = along_lines_in_steps(later(gate_up_1, swapped), lines, z)
    block = ring[0][:tok_rows]
    out_piece = later(jnp.stack([held[tok_rows:] for held in ring]), swapped)
    out_near = first_hop(out_piece)

    rows = rows.reshape(group_rows, features)
    attn_weights = attn_weights.reshape(features, -1)
    projected = product(rows, attn_weights)
    q_raw = projected[:, :head_cols]
    k_raw = projected[:, head_cols : 2 * head_cols]
    squares = jnp.stack([jnp.sum(q_raw * q_raw, axis=1), jnp.sum(k_raw * k_raw, axis=1)])
    squares, out_piece, *out_near = together(squares, out_piece, *out_near)
    squares = squares + swap_core(squares)
    squares, held_1 = together(squares, held_1)
    total = squares
    for step in range(1, lines):
        total = total + over_mp(squares, lines, step)
    col_start = z * z_cols + core * head_cols
    query_part = lax.dynamic_slice_in_dim(query_gain, col_start, head_cols)
    key_part = lax.dynamic_slice_in_dim(key_gain, col_start, head_cols)
    out_half = out_piece.shape[0] // 2
    down_half = down_own.shape[0] // 2
    far_low = jnp.concatenate([out_near[0][:out_half].reshape(-1, features), down_near[0][:down_half]])
    far_high = jnp.concatenate([out_near[1][out_half:].reshape(-1, features), down_near[1][down_half:]])
    both_far = [swap_y(far_low), swap_x(far_high)]
    piece_1 = to_both_cores(held_1, core)
    held_2 = along_lines(later(gate_up_2, total), lines)
    total, piece_1 = together(total, piece_1)
    near_1 = first_hop(piece_1)

    attended = attention(
        projected,
        lax.rsqrt(total[0] / features + NORM_EPSILON),
        lax.rsqrt(total[1] / features + NORM_EPSILON),
        query_part,
        key_part,
        segment,
        cosines,
        sines,
    )

    attended, *both_far = together(attended, *both_far)
    out_far = [far[:-down_half].reshape((out_half,) + out_piece.shape[1:]) for far in both_far]
    attended = attended.reshape(lines, chip_rows, head_cols)
    both = jnp.concatenate([pick(attended, z)] + to_lines(attended, lines, z), axis=1)
    both, *near_1 = together(both, *near_1)
    out_weights = later(jnp.zeros((lines, 2, 2) + out_piece.shape[1:], bf16), attended)
    split = lines // 2
    for held, row, column, at in (
        (out_piece, y, x, 0),
        (out_near[0], y, 1 - x, 0),
        (out_near[1], 1 - y, x, 0),
        (out_far[0], 1 - y, 1 - x, 0),
        (out_far[1], 1 - y, 1 - x, split),
    ):
        out_weights = lax.dynamic_update_slice(
            out_weights, later(held, attended)[:, None, None], (at, row, column, 0, 0)
        )
    out_weights = out_weights.reshape(-1, features)
    partial = jnp.dot(both, out_weights, preferred_element_type=f32)
    partial = partial.reshape(2, tok_rows, features)
    attn_out = pick(partial, core) + swap_core(pick(partial, 1 - core).astype(bf16)).astype(f32)
    far_1 = second_hop(*near_1)
    piece_2 = to_both_cores(later(held_2, partial), core)
    near_2 = first_hop(piece_2)
    hidden = block.astype(f32) + rms_scale(attn_out, server_order(attn_post_gain))
    hidden = hidden.astype(bf16)

    ring = [hidden]
    for step in range(1, lines):
        ring.append(over_mp(ring[-1], lines, 1))
    swap_from, *rest = together(ring[1], *far_1, *near_2)
    far_1, near_2 = rest[:2], rest[2:]
    far_2 = second_hop(*near_2)
    mlp_weights = later(jnp.zeros((4, 2, lines, 2) + piece_1.shape[1:], bf16), hidden)
    early_pieces = [later(piece, hidden) for piece in (piece_1, *near_1)]
    mlp_weights = four_pieces(mlp_weights, *early_pieces, *far_1, x, y, 0)
    mlp_weights = four_pieces(mlp_weights, piece_2, *near_2, *far_2, x, y, 1)
    mlp_weights = mlp_weights.reshape(features, -1)
    down_pieces = [later(piece, hidden) for piece in (down_own, *down_near, *both_far)]
    down_pieces[3:] = [far[-down_half:] for far in down_pieces[3:]]
    down_block = jnp.zeros((4, 2, down_half, 1, features), bf16)
    down_block = four_pieces(down_block, *down_pieces, x, y, 0)
    down_block = down_block.reshape(-1, features)

    def both_rows(own):
        mine, theirs = feed_forward(own, swap_core(own), mlp_weights, down_block)
        return mine + swap_core(theirs).astype(f32)

    total_out = None
    for step in range(1, lines):
        part = both_rows(swap_from if step == 1 else ring[step])
        if total_out is not None:
            part = part + total_out.astype(f32)
        part = part.astype(bf16)
        total_out = over_mp(part, lines, 1) if step + 1 < lines else swap_home(part, lines, 1)
        if step == 1 and lines > 2:
            total_out, ring[0] = together(total_out, ring[0])
    own_out = both_rows(ring[0]).astype(bf16)
    own_out = jnp.where(home, own_out, swap_home(own_out, lines, 0)).astype(f32)
    hidden = given_order(hidden)
    hidden = jnp.where(home, hidden, swap_home(hidden, lines, 0)).astype(f32)
    mlp_out = own_out + total_out.astype(f32)
    return (hidden + rms_scale(mlp_out, mlp_post_gain)).astype(bf16)


def per_device(*arrays):
    heads = arrays[0].shape[1] // HEAD_DIM
    shards = lax.axis_size("mp")
    if lax.axis_size("group") == 4 and shards % 4 == 0 and heads % shards == 0:
        return per_device_lines(*arrays)
    return per_device_general(*arrays)


def solution(mesh):
    return jax.shard_map(
        per_device,
        mesh=mesh,
        in_specs=(
            P(("group", "mp"), None),
            P("group", None),
            P(),
            P(),
            P(),
            P(),
            P(("mp", "group"), None),
            P(("mp", "group"), None),
            P(("mp", "group"), None),
            P(("mp", "group"), None),
            P(("mp", "group"), None),
            P(("mp", "group"), None),
            P(("mp", "group"), None),
        ),
        out_specs=P(("group", "mp"), None),
        check_vma=False,
    )
```

```python
import math

import jax
import jax.numpy as jnp
from jax import lax
from jax.experimental import pallas as pl
from jax.experimental.pallas import tpu as pltpu
from jax.sharding import PartitionSpec as P

HEAD_DIM = 128
LONGEST = 512


NORM_EPSILON = 1e-06
ROPE_BASE = 500000.0


def partner_2(block, axis, apart):
    count = lax.axis_size(axis)
    route = []
    for low in range(count):
        high = low | 1 << apart
        if high != low and high < count:
            route += [(low, high), (high, low)]
    return lax.ppermute(block, axis, route)


def token_layout(prompt_lens, row_count):
    seg_ends = jnp.cumsum(prompt_lens)
    starts = seg_ends - prompt_lens
    indices = jnp.arange(row_count, dtype=jnp.int32)
    segment = jnp.sum((indices[:, None] >= seg_ends[None, :]).astype(jnp.int32), axis=1)
    member = segment[:, None] == jnp.arange(prompt_lens.shape[0], dtype=jnp.int32)[None, :]
    opening = jnp.sum(jnp.where(member, starts[None, :], 0), axis=1)
    return (segment, indices - opening)


def rotary(head_values, position, head_size):
    half_size = head_size // 2
    frequency = jnp.exp(
        jnp.arange(half_size, dtype=jnp.float32) * (-2.0 * math.log(ROPE_BASE) / head_size)
    )
    angles = position.astype(jnp.float32)[:, None] * frequency[None, :]
    cosines = jnp.cos(angles)
    sines = jnp.sin(angles)
    front_half = head_values[..., :half_size]
    back_half = head_values[..., half_size:]
    return jnp.concatenate(
        [front_half * cosines - back_half * sines, back_half * cosines + front_half * sines],
        axis=-1,
    )


def head_attention(queries, keys_rot, values_h, segment, head_size):
    scores = lax.dot_general(
        queries, keys_rot, (((1,), (1,)), ((), ())), preferred_element_type=jnp.float32
    )
    scores = scores * (1.0 / math.sqrt(head_size))
    key_rows = jnp.arange(keys_rot.shape[0], dtype=jnp.int32)
    query_segment = segment
    allowed = (query_segment[:, None] == segment[None, :]) & (
        key_rows[None, :] <= key_rows[:, None]
    )
    scores = jnp.where(allowed, scores, -1e30)
    row_max = jnp.max(scores, axis=1, keepdims=True)
    weights = jnp.exp(scores - row_max)
    weights = weights / jnp.sum(weights, axis=1, keepdims=True)
    probabilities = weights.astype(jnp.bfloat16)
    return jnp.dot(probabilities, values_h, preferred_element_type=jnp.float32).astype(jnp.bfloat16)


def rms_scale(values_in, gain):
    return (
        values_in
        * lax.rsqrt(jnp.mean(values_in * values_in, axis=-1, keepdims=True) + NORM_EPSILON)
        * gain
    )


def per_device_general(
    tokens,
    lengths,
    query_gain,
    key_gain,
    attn_post_gain,
    mlp_post_gain,
    query_weight,
    key_weight,
    value_weight,
    output_weight,
    gate_weight,
    up_weight,
    down_weight,
):
    features = tokens.shape[1]
    shards = lax.axis_size("mp")
    my_index = lax.axis_index("mp")
    col_width = features // shards
    tok_rows = tokens.shape[0]
    group_rows = tok_rows * shards
    halves = col_width < HEAD_DIM
    stack_attn = jnp.stack([query_weight, key_weight, value_weight]).astype(jnp.bfloat16)
    stack_mlp = jnp.stack([gate_weight, up_weight]).astype(jnp.bfloat16)
    down_piece = down_weight.astype(jnp.bfloat16)[None]
    output_piece = output_weight.astype(jnp.bfloat16)[None]
    attn_rows, mlp_rows, down_rows, output_rows = (
        lax.all_gather(stack_attn, "group", axis=1, tiled=True),
        lax.all_gather(stack_mlp, "group", axis=1, tiled=True),
        lax.all_gather(down_piece, "group", axis=1, tiled=True),
        lax.all_gather(output_piece, "group", axis=1, tiled=True),
    )
    attn_block, mlp_block = (
        lax.all_to_all(attn_rows, "mp", split_axis=2, concat_axis=1, tiled=True),
        lax.all_to_all(mlp_rows, "mp", split_axis=2, concat_axis=1, tiled=True),
    )
    down_block = down_rows[0]
    output_block = output_rows[0]
    parity = my_index % 2
    if halves:
        partner = partner_2(attn_block, "mp", 0)
        attn_block = jnp.where(
            parity == 0,
            jnp.concatenate([attn_block, partner], axis=2),
            jnp.concatenate([partner, attn_block], axis=2),
        )
    head_cols = attn_block.shape[2]
    col_start = my_index * col_width // HEAD_DIM * HEAD_DIM
    share_part = col_width / head_cols
    projected = jnp.einsum(
        "td,kdc->ktc",
        lax.all_gather(tokens, "mp", axis=0, tiled=True),
        attn_block,
        preferred_element_type=jnp.float32,
    )
    query_sq = jnp.sum(projected[0] * projected[0], axis=1) * share_part
    key_sq = jnp.sum(projected[1] * projected[1], axis=1) * share_part
    query_total, key_total = lax.psum((query_sq, key_sq), "mp")
    query_part = lax.dynamic_slice_in_dim(query_gain, col_start, head_cols)
    key_part = lax.dynamic_slice_in_dim(key_gain, col_start, head_cols)
    q_normed = projected[0] * lax.rsqrt(query_total / features + NORM_EPSILON)[:, None] * query_part
    k_normed = projected[1] * lax.rsqrt(key_total / features + NORM_EPSILON)[:, None] * key_part
    segment, position = token_layout(lengths[0], group_rows)
    local_heads = head_cols // HEAD_DIM

    def heads_first(flat):
        return flat.reshape(group_rows, local_heads, HEAD_DIM).transpose(1, 0, 2)

    queries = rotary(heads_first(q_normed), position, HEAD_DIM).astype(jnp.bfloat16)
    keys_rot = rotary(heads_first(k_normed), position, HEAD_DIM).astype(jnp.bfloat16)
    values_h = heads_first(projected[2].astype(jnp.bfloat16))

    def per_head(triple):
        return head_attention(triple[0], triple[1], triple[2], segment, HEAD_DIM)

    attended = lax.map(per_head, (queries, keys_rot, values_h))
    attended = attended.transpose(1, 0, 2).reshape(group_rows, head_cols)
    if halves:
        attended = lax.dynamic_slice_in_dim(attended, parity * col_width, col_width, 1)
    rows_part = attended
    attn_out = lax.psum_scatter(
        jnp.dot(rows_part, output_block, preferred_element_type=jnp.float32).astype(jnp.bfloat16),
        "mp",
        scatter_dimension=0,
        tiled=True,
    ).astype(jnp.float32)
    hidden = (tokens.astype(jnp.float32) + rms_scale(attn_out, attn_post_gain)).astype(jnp.bfloat16)
    hidden_width = mlp_block.shape[2]
    mlp_weights = jnp.concatenate([mlp_block[0], mlp_block[1]], axis=1)
    both_proj = jnp.dot(
        lax.all_gather(hidden, "mp", axis=0, tiled=True),
        mlp_weights,
        preferred_element_type=jnp.float32,
    )
    activated = (jax.nn.silu(both_proj[:, :hidden_width]) * both_proj[:, hidden_width:]).astype(
        jnp.bfloat16
    )
    rows_part = activated
    mlp_out = lax.psum_scatter(
        jnp.dot(rows_part, down_block, preferred_element_type=jnp.float32).astype(jnp.bfloat16),
        "mp",
        scatter_dimension=0,
        tiled=True,
    ).astype(jnp.float32)
    return (hidden.astype(jnp.float32) + rms_scale(mlp_out, mlp_post_gain)).astype(jnp.bfloat16)


def over_mp(block, lines, step):
    count = 2 * lines
    return lax.ppermute(block, "mp", [(i, (i + 2 * step) % count) for i in range(count)])


def swap_x(block):
    return lax.ppermute(block, "mp", [(i, i ^ 1) for i in range(lax.axis_size("mp"))])


def swap_y(block):
    return lax.ppermute(block, "group", [(i, i ^ 2) for i in range(lax.axis_size("group"))])


def swap_core(block):
    return lax.ppermute(block, "group", [(i, i ^ 1) for i in range(lax.axis_size("group"))])


def swap_home(block, lines, step):
    shards = 2 * lines
    route = []
    for group in range(lax.axis_size("group")):
        for index in range(shards):
            apart = index % 2 ^ group % 2
            to = ((index + 2 * step) % shards) ^ apart
            if step or apart:
                route.append((group * shards + index, (group ^ apart) * shards + to))
    return lax.ppermute(block, ("group", "mp"), route)


def together(*arrays):
    return lax.optimization_barrier(arrays)


def later(value, *earlier):
    return lax.optimization_barrier((value, *earlier))[0]


def put(buffer, block, *place):
    shape = (1,) * len(place) + block.shape
    rest = (0,) * (buffer.ndim - len(place))
    return lax.dynamic_update_slice(buffer, block.reshape(shape), tuple(place) + rest)


def pick(buffer, index):
    return lax.dynamic_index_in_dim(buffer, index, 0, keepdims=False)


def first_hop(piece):
    return swap_x(piece), swap_y(piece)


def second_hop(at_x, at_y):
    split = at_x.shape[0] // 2
    return swap_y(at_x[:split]), swap_x(at_y[split:])


def four_pieces(whole, piece, at_x, at_y, far_low, far_high, x, y, part):
    def write(block, column, row, half=None):
        at = 0 if half is None else half
        block = block.reshape((1, -1) + whole.shape[2:3] + (1,) + whole.shape[4:])
        place = (2 * column + row, at, 0, part) + (0,) * (whole.ndim - 4)
        return lax.dynamic_update_slice(whole, block, place)

    whole = write(piece, x, y)
    whole = write(at_x, 1 - x, y)
    whole = write(at_y, x, 1 - y)
    whole = write(far_low, 1 - x, 1 - y, 0)
    return write(far_high, 1 - x, 1 - y, 1)


def along_lines(parts, lines):
    sets = [[2 * a + b for a in range(lines)] for b in range(2)]
    return lax.all_to_all(
        parts, "mp", split_axis=0, concat_axis=0, axis_index_groups=sets, tiled=True
    )


def to_lines(parts, lines, z):
    return [over_mp(pick(parts, (z + step) % lines), lines, step) for step in range(1, lines)]


def along_lines_in_steps(parts, lines, z):
    held = put(jnp.zeros(parts.shape, parts.dtype), pick(parts, z), z)
    for step, block in enumerate(to_lines(parts, lines, z), 1):
        held = put(held, block, (z - step) % lines)
    return held


def to_both_cores(held, core):
    held = held.transpose(1, 0, 2, 3)
    other = swap_core(pick(held, 1 - core))
    mine = pick(held, core)
    both = jnp.stack([jnp.where(core == 0, mine, other), jnp.where(core == 0, other, mine)], axis=1)
    return both.reshape((-1,) + both.shape[2:])


def product_kernel(rows_ref, weights_ref, out_ref):
    out_ref[...] = jnp.dot(rows_ref[...], weights_ref[...], preferred_element_type=jnp.float32)


def product(rows, weights):
    count, depth = rows.shape
    width = weights.shape[1]
    tile = math.gcd(count, 320)
    return pl.pallas_call(
        product_kernel,
        grid=(count // tile,),
        in_specs=[
            pl.BlockSpec((tile, depth), lambda i: (i, 0)),
            pl.BlockSpec((depth, width), lambda i: (0, 0)),
        ],
        out_specs=pl.BlockSpec((tile, width), lambda i: (i, 0)),
        out_shape=jax.ShapeDtypeStruct((count, width), jnp.float32),
        compiler_params=pltpu.CompilerParams(vmem_limit_bytes=32 * 2**20),
        cost_estimate=pl.CostEstimate(flops=1, bytes_accessed=1, transcendentals=0),
    )(rows, weights)


def feed_forward_kernel(own_ref, other_ref, gate_ref, up_ref, down_ref, mine_ref, theirs_ref, rows, total):
    count = own_ref.shape[0]
    step = pl.program_id(0)

    @pl.when(step == 0)
    def _():
        rows[:count, :] = own_ref[...]
        rows[count:, :] = other_ref[...]

    gate = jnp.dot(rows[...], gate_ref[...], preferred_element_type=jnp.float32)
    up = jnp.dot(rows[...], up_ref[...], preferred_element_type=jnp.float32)
    activated = (gate / (1.0 + jnp.exp(-gate)) * up).astype(jnp.bfloat16)
    part = jnp.dot(activated, down_ref[...], preferred_element_type=jnp.float32)
    last = pl.num_programs(0) - 1

    @pl.when(step == 0)
    def _():
        total[...] = part

    @pl.when((step > 0) & (step < last))
    def _():
        total[...] += part

    @pl.when(step == last)
    def _():
        mine_ref[...] = total[:count, :] + part[:count, :]
        theirs_ref[...] = (total[count:, :] + part[count:, :]).astype(jnp.bfloat16)


def feed_forward(own, other, gate_up, down):
    count, width = own.shape
    units = down.shape[0]
    run = math.gcd(units, 256)
    steps = units // run
    whole = pl.BlockSpec((count, width), lambda i: (0, 0))
    return pl.pallas_call(
        feed_forward_kernel,
        grid=(steps,),
        in_specs=[
            whole,
            whole,
            pl.BlockSpec((width, run), lambda i: (0, i)),
            pl.BlockSpec((width, run), lambda i: (0, steps + i)),
            pl.BlockSpec((run, width), lambda i: (i, 0)),
        ],
        out_specs=[whole, whole],
        out_shape=[
            jax.ShapeDtypeStruct((count, width), jnp.float32),
            jax.ShapeDtypeStruct((count, width), jnp.bfloat16),
        ],
        scratch_shapes=[
            pltpu.VMEM((2 * count, width), jnp.bfloat16),
            pltpu.VMEM((2 * count, width), jnp.float32),
        ],
        compiler_params=pltpu.CompilerParams(vmem_limit_bytes=32 * 2**20),
        cost_estimate=pl.CostEstimate(flops=1, bytes_accessed=1, transcendentals=0),
    )(own, other, gate_up, gate_up, down)


def attention_kernel(
    q_ref, k_ref, v_ref, q_scale, k_scale, q_gain, k_gain, cos_ref, sin_ref, seg_ref, ends_ref, out_ref
):
    count, size = q_ref.shape
    tile = math.gcd(count, 256)

    def ready(ref, scale, gain):
        normed = ref[...] * scale[...] * gain[...]
        turned = normed * cos_ref[...] + pltpu.roll(normed, size // 2, 1) * sin_ref[...]
        return turned.astype(jnp.bfloat16)

    queries = ready(q_ref, q_scale, q_gain)
    keys = ready(k_ref, k_scale, k_gain)
    values = v_ref[...].astype(jnp.bfloat16)
    for start in range(0, count, tile):
        low = max(0, start - -(-LONGEST // tile) * tile)
        stop = start + tile
        scores = lax.dot_general(
            queries[start:stop],
            keys[low:stop],
            (((1,), (1,)), ((), ())),
            preferred_element_type=jnp.float32,
        )
        scores = scores * (1.0 / math.sqrt(size))
        query_rows = start + lax.broadcasted_iota(jnp.int32, scores.shape, 0)
        key_rows = low + lax.broadcasted_iota(jnp.int32, scores.shape, 1)
        allowed = (seg_ref[start:stop, :] == ends_ref[:, low:stop]) & (key_rows <= query_rows)
        scores = jnp.where(allowed, scores, -1e30)
        weights = jnp.exp(scores - jnp.max(scores, axis=1, keepdims=True))
        whole = jnp.sum(weights, axis=1, keepdims=True)
        mixed = jnp.dot(
            weights.astype(jnp.bfloat16), values[low:stop], preferred_element_type=jnp.float32
        )
        out_ref[start:stop, :] = (mixed / whole).astype(jnp.bfloat16)


def rotary_tables(position):
    half = HEAD_DIM // 2
    frequency = jnp.exp(
        jnp.arange(half, dtype=jnp.float32) * (-2.0 * math.log(ROPE_BASE) / HEAD_DIM)
    )
    angles = position.astype(jnp.float32)[:, None] * frequency[None, :]
    cosines, sines = jnp.cos(angles), jnp.sin(angles)
    return jnp.concatenate([cosines, cosines], axis=1), jnp.concatenate([-sines, sines], axis=1)


def attention(projected, q_scale, k_scale, q_gain, k_gain, segment, cosines, sines):
    count = projected.shape[0]
    heads = projected.shape[1] // 3 // HEAD_DIM

    def head(first):
        return pl.BlockSpec((count, HEAD_DIM), lambda h: (0, first + h))

    def whole(shape):
        return pl.BlockSpec(shape, lambda h: (0, 0))

    return pl.pallas_call(
        attention_kernel,
        grid=(heads,),
        in_specs=[
            head(0),
            head(heads),
            head(2 * heads),
            whole((count, 1)),
            whole((count, 1)),
            pl.BlockSpec((1, HEAD_DIM), lambda h: (0, h)),
            pl.BlockSpec((1, HEAD_DIM), lambda h: (0, h)),
            whole((count, HEAD_DIM)),
            whole((count, HEAD_DIM)),
            whole((count, 1)),
            whole((1, count)),
        ],
        out_specs=head(0),
        out_shape=jax.ShapeDtypeStruct((count, heads * HEAD_DIM), jnp.bfloat16),
        compiler_params=pltpu.CompilerParams(vmem_limit_bytes=48 * 2**20),
        cost_estimate=pl.CostEstimate(flops=1, bytes_accessed=1, transcendentals=0),
    )(
        projected,
        projected,
        projected,
        q_scale[:, None],
        k_scale[:, None],
        q_gain[None],
        k_gain[None],
        cosines,
        sines,
        segment[:, None],
        segment[None],
    )


def per_device_lines(
    tokens,
    lengths,
    query_gain,
    key_gain,
    attn_post_gain,
    mlp_post_gain,
    query_weight,
    key_weight,
    value_weight,
    output_weight,
    gate_weight,
    up_weight,
    down_weight,
):
    bf16, f32 = jnp.bfloat16, jnp.float32
    features = tokens.shape[1]
    shards = lax.axis_size("mp")
    lines = shards // 2
    index = lax.axis_index("mp")
    z, x = index // 2, index % 2
    group = lax.axis_index("group")
    y, core = group // 2, group % 2
    tok_rows = tokens.shape[0]
    chip_rows = 2 * tok_rows
    group_rows = shards * tok_rows
    home = x == core

    z_cols = features // lines
    head_cols = z_cols // 2
    run = features // shards // 2

    def server_order(rows):
        parts = rows.reshape(rows.shape[:-1] + (lines, 4, run))
        return jnp.swapaxes(parts, -3, -2).reshape(rows.shape)

    def given_order(rows):
        parts = rows.reshape(rows.shape[:-1] + (4, lines, run))
        return jnp.swapaxes(parts, -3, -2).reshape(rows.shape)

    def by_owner(weights, runs):
        parts = [w.astype(bf16).reshape(w.shape[0], lines, runs, 2, -1) for w in weights]
        parts = jnp.stack(parts, axis=2).transpose(1, 4, 0, 2, 3, 5)
        return parts.reshape(lines, 2, weights[0].shape[0], -1)

    own = jnp.concatenate([server_order(tokens), server_order(output_weight.astype(bf16))], axis=0)
    own, *weights = together(own, query_weight, key_weight, value_weight)
    attn_parts = by_owner(weights, 1)
    ring_1 = swap_home(own, lines, 1)
    moved = swap_home(own, lines, 0)
    attn_parts, down_own = together(attn_parts, down_weight)
    attn_held = along_lines(attn_parts, lines)
    down_own = down_own.astype(bf16)
    down_near = first_hop(down_own)
    rows = jnp.zeros((lines, 2) + tokens.shape, bf16)
    gate_up = by_owner((gate_weight, up_weight), 4)
    own, ring_1, moved, attn_held, gate_up, rows = together(
        own, ring_1, moved, attn_held, gate_up, rows
    )

    ring = [jnp.where(home, own, moved), ring_1]
    if lines > 2:
        ring.append(over_mp(ring[-1], lines, 1))
    attn_piece = to_both_cores(attn_held, core)
    attn_near = first_hop(attn_piece)

    def place(rows, step, held, at_core):
        return put(rows, held[:tok_rows], (z - step) % lines, at_core)

    for step in range(2):
        rows = place(rows, step, ring[step], core)
        rows = place(rows, step, swap_core(ring[step]), 1 - core)
    ring[-1], gate_up = together(ring[-1], gate_up)

    attn_far = second_hop(*attn_near)
    for step in range(3, lines):
        ring.append(over_mp(ring[-1], lines, 1))
    for step in range(2, lines - 1):
        rows = place(rows, step, ring[step], core)
        rows = place(rows, step, swap_core(ring[step]), 1 - core)
    prompt_lens = jnp.where(home, lengths, swap_core(lengths))[0]
    attn_weights = jnp.zeros((4, 2, lines, 1) + attn_piece.shape[1:], bf16)
    attn_weights = four_pieces(attn_weights, attn_piece, *attn_near, *attn_far, x, y, 0)
    rows_half = gate_up.shape[2] // 2
    gate_up_1, gate_up_2 = gate_up[:, :, :rows_half], gate_up[:, :, rows_half:]
    segment, position = token_layout(prompt_lens, group_rows)
    cosines, sines = rotary_tables(position)
    rows, attn_weights, segment, cosines, sines, gate_up_1, ring[-1] = together(
        rows, attn_weights, segment, cosines, sines, gate_up_1, ring[-1]
    )
    last = lines - 1
    rows = place(rows, last, ring[last], core)
    swapped = swap_core(ring[last])
    rows = place(rows, last, swapped, 1 - core)
    held_1 = along_lines_in_steps(later(gate_up_1, swapped), lines, z)
    block = ring[0][:tok_rows]
    out_piece = later(jnp.stack([held[tok_rows:] for held in ring]), swapped)
    out_near = first_hop(out_piece)

    rows = rows.reshape(group_rows, features)
    attn_weights = attn_weights.reshape(features, -1)
    projected = product(rows, attn_weights)
    q_raw = projected[:, :head_cols]
    k_raw = projected[:, head_cols : 2 * head_cols]
    squares = jnp.stack([jnp.sum(q_raw * q_raw, axis=1), jnp.sum(k_raw * k_raw, axis=1)])
    squares, out_piece, *out_near = together(squares, out_piece, *out_near)
    squares = squares + swap_core(squares)
    squares, held_1 = together(squares, held_1)
    total = squares
    for step in range(1, lines):
        total = total + over_mp(squares, lines, step)
    col_start = z * z_cols + core * head_cols
    query_part = lax.dynamic_slice_in_dim(query_gain, col_start, head_cols)
    key_part = lax.dynamic_slice_in_dim(key_gain, col_start, head_cols)
    out_half = out_piece.shape[0] // 2
    down_half = down_own.shape[0] // 2
    far_low = jnp.concatenate([out_near[0][:out_half].reshape(-1, features), down_near[0][:down_half]])
    far_high = jnp.concatenate([out_near[1][out_half:].reshape(-1, features), down_near[1][down_half:]])
    both_far = [swap_y(far_low), swap_x(far_high)]
    piece_1 = to_both_cores(held_1, core)
    held_2 = along_lines(later(gate_up_2, total), lines)
    total, piece_1 = together(total, piece_1)
    near_1 = first_hop(piece_1)

    attended = attention(
        projected,
        lax.rsqrt(total[0] / features + NORM_EPSILON),
        lax.rsqrt(total[1] / features + NORM_EPSILON),
        query_part,
        key_part,
        segment,
        cosines,
        sines,
    )

    attended, *both_far = together(attended, *both_far)
    out_far = [far[:-down_half].reshape((out_half,) + out_piece.shape[1:]) for far in both_far]
    attended = attended.reshape(lines, chip_rows, head_cols)
    both = jnp.concatenate([pick(attended, z)] + to_lines(attended, lines, z), axis=1)
    both, *near_1 = together(both, *near_1)
    out_weights = later(jnp.zeros((lines, 2, 2) + out_piece.shape[1:], bf16), attended)
    split = lines // 2
    for held, row, column, at in (
        (out_piece, y, x, 0),
        (out_near[0], y, 1 - x, 0),
        (out_near[1], 1 - y, x, 0),
        (out_far[0], 1 - y, 1 - x, 0),
        (out_far[1], 1 - y, 1 - x, split),
    ):
        out_weights = lax.dynamic_update_slice(
            out_weights, later(held, attended)[:, None, None], (at, row, column, 0, 0)
        )
    out_weights = out_weights.reshape(-1, features)
    partial = jnp.dot(both, out_weights, preferred_element_type=f32)
    partial = partial.reshape(2, tok_rows, features)
    attn_out = pick(partial, core) + swap_core(pick(partial, 1 - core).astype(bf16)).astype(f32)
    far_1 = second_hop(*near_1)
    piece_2 = to_both_cores(later(held_2, partial), core)
    near_2 = first_hop(piece_2)
    hidden = block.astype(f32) + rms_scale(attn_out, server_order(attn_post_gain))
    hidden = hidden.astype(bf16)

    ring = [hidden]
    for step in range(1, lines):
        ring.append(over_mp(ring[-1], lines, 1))
    swap_from, *rest = together(ring[1], *far_1, *near_2)
    far_1, near_2 = rest[:2], rest[2:]
    far_2 = second_hop(*near_2)
    mlp_weights = later(jnp.zeros((4, 2, lines, 2) + piece_1.shape[1:], bf16), hidden)
    early_pieces = [later(piece, hidden) for piece in (piece_1, *near_1)]
    mlp_weights = four_pieces(mlp_weights, *early_pieces, *far_1, x, y, 0)
    mlp_weights = four_pieces(mlp_weights, piece_2, *near_2, *far_2, x, y, 1)
    mlp_weights = mlp_weights.reshape(features, -1)
    down_pieces = [later(piece, hidden) for piece in (down_own, *down_near, *both_far)]
    down_pieces[3:] = [far[-down_half:] for far in down_pieces[3:]]
    down_block = jnp.zeros((4, 2, down_half, 1, features), bf16)
    down_block = four_pieces(down_block, *down_pieces, x, y, 0)
    down_block = down_block.reshape(-1, features)

    def both_rows(own):
        mine, theirs = feed_forward(own, swap_core(own), mlp_weights, down_block)
        return mine + swap_core(theirs).astype(f32)

    total_out = None
    for step in range(1, lines):
        part = both_rows(swap_from if step == 1 else ring[step])
        if total_out is not None:
            part = part + total_out.astype(f32)
        part = part.astype(bf16)
        total_out = over_mp(part, lines, 1) if step + 1 < lines else swap_home(part, lines, 1)
        if step == 1 and lines > 2:
            total_out, ring[0] = together(total_out, ring[0])
    own_out = both_rows(ring[0]).astype(bf16)
    own_out = jnp.where(home, own_out, swap_home(own_out, lines, 0)).astype(f32)
    hidden = given_order(hidden)
    hidden = jnp.where(home, hidden, swap_home(hidden, lines, 0)).astype(f32)
    mlp_out = own_out + total_out.astype(f32)
    return (hidden + rms_scale(mlp_out, mlp_post_gain)).astype(bf16)


def per_device(*arrays):
    heads = arrays[0].shape[1] // HEAD_DIM
    shards = lax.axis_size("mp")
    if lax.axis_size("group") == 4 and shards % 4 == 0 and heads % shards == 0:
        return per_device_lines(*arrays)
    return per_device_general(*arrays)


def solution(mesh):
    return jax.shard_map(
        per_device,
        mesh=mesh,
        in_specs=(
            P(("group", "mp"), None),
            P("group", None),
            P(),
            P(),
            P(),
            P(),
            P(("mp", "group"), None),
            P(("mp", "group"), None),
            P(("mp", "group"), None),
            P(("mp", "group"), None),
            P(("mp", "group"), None),
            P(("mp", "group"), None),
            P(("mp", "group"), None),
        ),
        out_specs=P(("group", "mp"), None),
        check_vma=False,
    )
```
